32 devices in a mesh: nodes: 8 (over y, x, core), tp: 4 (over z).
Axes of the slice: x: 2, y: 2, z: 4, core: 2. Of those that a mesh axis runs over, the one named last changes fastest.
Arguments:
- tokens: bfloat16 [32768, 512], P(('nodes', 'tp')), may hold values from -6 to 6
- hop_mask: int32 [32768], P(('nodes', 'tp')), may hold values from 0 to 1, as said below
- graph_ids: int32 [4096], P(('nodes', 'tp')), may hold values from 0 to 63
- norm1_gain: bfloat16 [512], replicated, may hold values from 0.5 to 1.5
- norm1_shift: bfloat16 [512], replicated, may hold values from -2 to 2
- w_query: bfloat16 [512, 512], P(None, 'tp'), may hold values from -0.25 to 0.25
- w_key: bfloat16 [512, 512], P(None, 'tp'), may hold values from -0.25 to 0.25
- w_value: bfloat16 [512, 512], P(None, 'tp'), may hold values from -0.25 to 0.25
- w_out: bfloat16 [512, 512], P('tp'), may hold values from -0.5 to 0.5
- norm2_gain: bfloat16 [512], replicated, may hold values from 0.5 to 1.5
- norm2_shift: bfloat16 [512], replicated, may hold values from -2 to 2
- w_up: bfloat16 [512, 1024], P(None, 'tp'), may hold values from -0.25 to 0.25
- w_down: bfloat16 [1024, 512], P('tp'), may hold values from -0.375 to 0.375
- hop_weight: bfloat16 [512], replicated, may hold values from -0.25 to 0.25
- cotangent: bfloat16 [4096, 512], P(('nodes', 'tp')), may hold values from -6 to 6
Outputs:
- readout: bfloat16 [4096, 512], P(('nodes', 'tp'))
- grad_tokens: bfloat16 [32768, 512], P(('nodes', 'tp'))
- grad_norm1_gain: float32 [512], replicated
- grad_norm1_shift: float32 [512], replicated
- grad_query: float32 [512, 512], P(None, 'tp')
- grad_key: float32 [512, 512], P(None, 'tp')
- grad_value: float32 [512, 512], P(None, 'tp')
- grad_out: float32 [512, 512], P('tp')
- grad_norm2_gain: float32 [512], replicated
- grad_norm2_shift: float32 [512], replicated
- grad_up: float32 [512, 1024], P(None, 'tp')
- grad_down: float32 [1024, 512], P('tp')
- grad_hop_weight: float32 [512], replicated
The draws below stay inside these ranges and needn't reach their ends.
Inputs may be any that keep to these rules, and one draw needn't show every extreme that they name: `hop_mask`: hops 0 and 1 of every node are real tokens.
All inputs are finite; a program needn't handle non-finite values.
Results may differ from the reference program's by a relative error of at most 0.038.
Values may be sent and summed in bfloat16 or wider, within the bound.
A program may use at most 128 MiB of HBM per device.

```python
import math
import jax
import jax.numpy as jnp
from jax import lax

D = 512
HEADS = 8
FF = 1024
HOPS = 8
HEAD = 64
GRAPHS = 64
NODES = 4096
TOKENS = 32768


def draw_hop_mask(key, part):
    key = jax.random.fold_in(key, 11)
    levels = jax.random.randint(key, (NODES, HOPS), 0, 10)
    present = (levels < 7).astype(jnp.int32)
    position = jnp.arange(HOPS, dtype=jnp.int32)[None, :]
    present = jnp.where(position < 2, 1, present)
    return present.reshape(NODES * HOPS).astype(jnp.int32)


def touch_ends(values, stream_key, least, high):
    extent = values.shape
    spot = [jax.random.randint(jax.random.fold_in(stream_key, axis), (), 0, extent[axis]) for axis in range(len(extent))]
    values = values.at[tuple(spot)].set(least)
    longest = extent.index(max(extent))
    spot[longest] = (spot[longest] + 1) % extent[longest]
    return values.at[tuple(spot)].set(high)


def level_of(own_key, dims, cuts, smallest, largest):
    level, own = 1.0, jax.random.fold_in(own_key, 6)
    for dim, shards_of in cuts:
        steps = jnp.exp(jax.random.uniform(jax.random.fold_in(own, dim), (shards_of,), jnp.float32, smallest / len(cuts), largest / len(cuts)))
        level = level * jnp.repeat(steps, dims[dim] // shards_of).reshape([-1 if axis == dim else 1 for axis in range(len(dims))])
    return level


def scatter_about(stream_key, shape, scale, most, cuts=(), kind=jnp.bfloat16):
    drawn = scale * jax.random.normal(stream_key, shape, jnp.float32)
    if cuts:
        drawn = drawn * level_of(stream_key, shape, cuts, -0.22, 0.18)
    return jnp.clip(drawn, -most, most).astype(kind)


def setup_inputs(seed: int = 0) -> dict:
    key_list = jax.random.split(jax.random.key(seed), 16)
    tokens = scatter_about(key_list[0], (TOKENS, D), 1.0, 6.0, ((0, 32),))
    hop_mask = draw_hop_mask(jax.random.fold_in(key_list[15], 71), 0)
    graph_ids = touch_ends(jax.random.randint(key_list[2], (NODES,), 0, GRAPHS), jax.random.fold_in(key_list[2], 1), 0, GRAPHS - 1).astype(jnp.int32)
    norm1_gain = jnp.clip(1.0 + 0.1 * jax.random.normal(key_list[3], (D,), jnp.float32), 0.5, 1.5).astype(jnp.bfloat16)
    norm1_shift = scatter_about(key_list[4], (D,), 0.3, 2.0)
    w_query = scatter_about(key_list[5], (D, D), D ** -0.5, 0.25, ((1, 4),))
    w_key = scatter_about(key_list[6], (D, D), D ** -0.5, 0.25, ((1, 4),))
    w_value = scatter_about(key_list[7], (D, D), D ** -0.5, 0.25, ((1, 4),))
    w_out = scatter_about(key_list[8], (D, D), (D // 4) ** -0.5, 0.5, ((0, 4),))
    norm2_gain = jnp.clip(1.0 + 0.1 * jax.random.normal(key_list[9], (D,), jnp.float32), 0.5, 1.5).astype(jnp.bfloat16)
    norm2_shift = scatter_about(key_list[10], (D,), 0.3, 2.0)
    w_up = scatter_about(key_list[11], (D, FF), D ** -0.5, 0.25, ((1, 4),))
    w_down = scatter_about(key_list[12], (FF, D), (FF // 4) ** -0.5, 0.375, ((0, 4),))
    hop_weight = scatter_about(key_list[13], (D,), D ** -0.5, 0.25)
    cotangent = scatter_about(key_list[14], (NODES, D), 1.0, 6.0, ((0, 32),))
    return dict(tokens=tokens, hop_mask=hop_mask, graph_ids=graph_ids, norm1_gain=norm1_gain, norm1_shift=norm1_shift, w_query=w_query, w_key=w_key, w_value=w_value, w_out=w_out, norm2_gain=norm2_gain, norm2_shift=norm2_shift, w_up=w_up, w_down=w_down, hop_weight=hop_weight, cotangent=cotangent)


@jax.custom_vjp
def low(v):
    return lax.optimization_barrier(v.astype(jnp.bfloat16)).astype(jnp.float32)

@jax.custom_vjp
def low_back(v):
    return v

def low_keep(v):
    return (low(v), None)

def low_pass(kept, grad):
    return (grad,)

def back_keep(v):
    return (v, None)

def back_low(kept, grad):
    return (low(grad),)
low.defvjp(low_keep, low_pass)
low_back.defvjp(back_keep, back_low)
EPSILON = 1e-05
NEGATIVE = -1000000000.0
HIGHEST = lax.Precision.HIGHEST

def rounded_both(values):
    return low(low_back(values))

def norm_rows(values, gains, shifts):
    centre = values - lax.optimization_barrier(jnp.mean(values, axis=-1, keepdims=True))
    spread = lax.optimization_barrier(jnp.mean(centre * centre, axis=-1, keepdims=True))
    return centre * lax.rsqrt(spread + EPSILON) * gains + shifts

def layer_block(block_rows, block_mask, params):
    gain_one, shift_one, query_w, key_w, value_w, out_w, gain_two, shift_two, up_w, down_w = params
    total_rows = block_rows.shape[0]
    node_count = total_rows // HOPS
    scale = HEAD ** (-0.5)
    shape_four = (node_count, HOPS, HEADS, HEAD)
    normed = low(norm_rows(block_rows, gain_one, shift_one))
    queries = rounded_both(jnp.dot(normed, query_w, precision=HIGHEST)).reshape(shape_four)
    keys_all = rounded_both(jnp.dot(normed, key_w, precision=HIGHEST)).reshape(shape_four)
    values_all = rounded_both(jnp.dot(normed, value_w, precision=HIGHEST)).reshape(shape_four)
    scores = low_back(jnp.einsum('nqhe,nkhe->hqkn', queries, keys_all, precision=HIGHEST) * scale)
    allowed = (block_mask.reshape(node_count, HOPS).T > 0.5)[None, None]
    scores = jnp.where(allowed, scores, NEGATIVE)
    probs = low(jax.nn.softmax(scores, axis=2))
    context = rounded_both(jnp.einsum('hqkn,nkhe->nqhe', probs, values_all, precision=HIGHEST))
    context = context.reshape(total_rows, D)
    attended = low_back(jnp.dot(context, out_w, precision=HIGHEST))
    residual_one = block_rows + attended
    normed_two = low(norm_rows(residual_one, gain_two, shift_two))
    before = low_back(jnp.dot(normed_two, up_w, precision=HIGHEST))
    activated = low(jax.nn.gelu(before, approximate=False))
    branch = low_back(jnp.dot(activated, down_w, precision=HIGHEST))
    return residual_one + branch

def hop_readout(layer_out, mask_float, graph_ids, hop_w):
    per_node = layer_out.reshape(NODES, HOPS, D)
    first = per_node[:, 0]
    rest = per_node[:, 1:]
    valid = mask_float.reshape(NODES, HOPS)[:, 1:]
    logits = jnp.einsum('nkd,d->nk', rest, hop_w, precision=HIGHEST)
    logits = jnp.where(valid > 0.5, logits, NEGATIVE)
    weights = jax.nn.softmax(logits, axis=1)
    member = (graph_ids[:, None] == jnp.arange(GRAPHS, dtype=jnp.int32)[None, :]).astype(jnp.float32)
    sums = jnp.dot(member.T, weights, precision=HIGHEST)
    counts = lax.optimization_barrier(jnp.sum(member, axis=0))
    means = sums / (counts + 1.0)[:, None]
    coef = valid * (weights - jnp.dot(member, means, precision=HIGHEST))
    return first + jnp.einsum('nk,nkd->nd', coef, rest, precision=HIGHEST)

def reference(tokens, hop_mask, graph_ids, norm1_gain, norm1_shift, w_query, w_key, w_value, w_out, norm2_gain, norm2_shift, w_up, w_down, hop_weight, cotangent):
    mask_float = hop_mask.astype(jnp.float32)
    block = HOPS * math.gcd(NODES, 512)
    layer_step = jax.checkpoint(layer_block)
    floats = [item.astype(jnp.float32) for item in (tokens, norm1_gain, norm1_shift, w_query, w_key, w_value, w_out, norm2_gain, norm2_shift, w_up, w_down, hop_weight)]

    def forward(tokens_f, gain_one, shift_one, query_w, key_w, value_w, out_w, gain_two, shift_two, up_w, down_w, hop_w):
        params = (gain_one, shift_one, query_w, key_w, value_w, out_w, gain_two, shift_two, up_w, down_w)
        stacked = tokens_f.reshape(TOKENS // block, block, D)
        masks = mask_float.reshape(TOKENS // block, block)
        outputs = lax.map(lambda pieces: layer_step(pieces[0], pieces[1], params), (stacked, masks))
        return hop_readout(outputs.reshape(TOKENS, D), mask_float, graph_ids, hop_w)
    result, pull = jax.vjp(forward, *floats)
    grads = pull(cotangent.astype(jnp.float32))
    return (result.astype(jnp.bfloat16), grads[0].astype(jnp.bfloat16), grads[1], grads[2], grads[3], grads[4], grads[5], grads[6], grads[7], grads[8], grads[9], grads[10], grads[11])
```

```python
import jax
import jax.numpy as jnp
from jax import lax
from jax.sharding import PartitionSpec as P

HOPS = 8
HEAD = 64
GRAPHS = 64


EPSILON = 1e-05
NEGATIVE = -1000000000.0
HIGHEST = lax.Precision.HIGHEST


def norm_rows(values, gains, shifts):
    centre = values - jnp.mean(values, axis=-1, keepdims=True)
    spread = jnp.mean(centre * centre, axis=-1, keepdims=True)
    return centre * lax.rsqrt(spread + EPSILON) * gains + shifts


def masked_scores(query_four, key_four, allowed, scale):
    scores = (
        jnp.einsum("nqhe,nkhe->hqkn", query_four, key_four, preferred_element_type=jnp.float32)
        * scale
    )
    return jnp.where(allowed, scores, NEGATIVE)


def exact_gelu(values):
    return jax.nn.gelu(values, approximate=False)


def shards(
    tokens,
    hop_mask,
    graph_ids,
    norm1_gain,
    norm1_shift,
    w_query,
    w_key,
    w_value,
    w_out,
    norm2_gain,
    norm2_shift,
    w_up,
    w_down,
    hop_weight,
    cotangent,
):
    rows_here = tokens.shape[0]
    width = tokens.shape[1]
    nodes_here = rows_here // HOPS
    scale = HEAD ** (-0.5)
    query_w, key_w, value_w, up_w = (w_query, w_key, w_value, w_up)
    out_w, down_w = (w_out, w_down)
    tp = lax.axis_size("tp")
    cols = w_query.shape[1]
    ff_cols = w_up.shape[1]
    qkv = lax.all_gather(jnp.concatenate([w_query, w_key, w_value, w_up], axis=1), "tp", axis=0)
    outd = lax.all_gather(jnp.concatenate([w_out, w_down], axis=0), "tp", axis=0)

    def wide(lo, n):
        return jnp.transpose(qkv[:, :, lo : lo + n], (1, 0, 2)).reshape(width, tp * n)

    query_w, key_w, value_w = (wide(0, cols), wide(cols, cols), wide(2 * cols, cols))
    up_w = wide(3 * cols, ff_cols)
    out_w = outd[:, :cols].reshape(tp * cols, width)
    down_w = outd[:, cols:].reshape(tp * ff_cols, width)
    group_rows = rows_here
    node_group = group_rows // HOPS
    heads_here = query_w.shape[1] // HEAD
    shape_four = (node_group, HOPS, heads_here, HEAD)
    tokens_f = tokens.astype(jnp.float32)
    gain_one = norm1_gain.astype(jnp.float32)
    shift_one = norm1_shift.astype(jnp.float32)
    gain_two = norm2_gain.astype(jnp.float32)
    shift_two = norm2_shift.astype(jnp.float32)
    hop_vector = hop_weight.astype(jnp.float32)
    normed_one = norm_rows(tokens_f, gain_one, shift_one).astype(jnp.bfloat16)
    gathered_one, group_mask = normed_one, hop_mask.astype(jnp.bfloat16)
    allowed = (group_mask.reshape(node_group, HOPS).T > 0.5)[None, None]
    queries = jnp.dot(gathered_one, query_w, preferred_element_type=jnp.float32).astype(
        jnp.bfloat16
    )
    keys_all = jnp.dot(gathered_one, key_w, preferred_element_type=jnp.float32).astype(jnp.bfloat16)
    values_all = jnp.dot(gathered_one, value_w, preferred_element_type=jnp.float32).astype(
        jnp.bfloat16
    )
    query_four = queries.reshape(shape_four)
    key_four = keys_all.reshape(shape_four)
    value_four = values_all.reshape(shape_four)
    scores = masked_scores(query_four, key_four, allowed, scale)
    peak = jnp.max(scores, axis=2, keepdims=True)
    log_total = peak + jnp.log(jnp.sum(jnp.exp(scores - peak), axis=2, keepdims=True))
    probs = jnp.exp(scores - log_total)
    context = jnp.einsum(
        "hqkn,nkhe->nqhe",
        probs.astype(jnp.bfloat16),
        value_four,
        preferred_element_type=jnp.float32,
    )
    context = context.astype(jnp.bfloat16).reshape(group_rows, heads_here * HEAD)
    piece = context
    attended = jnp.dot(piece, out_w, preferred_element_type=jnp.float32)
    residual_one = tokens_f + attended
    normed_two = norm_rows(residual_one, gain_two, shift_two).astype(jnp.bfloat16)
    gathered_two = normed_two
    before = jnp.dot(gathered_two, up_w, preferred_element_type=jnp.float32)
    activated = exact_gelu(before).astype(jnp.bfloat16)
    piece = activated
    branch = jnp.dot(piece, down_w, preferred_element_type=jnp.float32)
    layer_out = residual_one + branch
    per_node = layer_out.reshape(nodes_here, HOPS, width)
    first = per_node[:, 0]
    rest = per_node[:, 1:]
    valid = hop_mask.reshape(nodes_here, HOPS)[:, 1:].astype(jnp.float32)
    logits = jnp.einsum("nkd,d->nk", rest, hop_vector, precision=HIGHEST)
    logits = jnp.where(valid > 0.5, logits, NEGATIVE)
    weights = jax.nn.softmax(logits, axis=1)
    member = (graph_ids[:, None] == jnp.arange(GRAPHS, dtype=jnp.int32)[None, :]).astype(
        jnp.float32
    )
    grad_read = cotangent.astype(jnp.float32)
    grad_coef = jnp.einsum("nd,nkd->nk", grad_read, rest, precision=HIGHEST)
    direct = valid * grad_coef
    sums, counts, grad_means = lax.psum(
        (
            jnp.dot(member.T, weights, precision=HIGHEST),
            jnp.sum(member, axis=0),
            -jnp.dot(member.T, direct, precision=HIGHEST),
        ),
        ("nodes", "tp"),
    )
    denom = (counts + 1.0)[:, None]
    means = sums / denom
    coef = valid * (weights - jnp.dot(member, means, precision=HIGHEST))
    readout = (first + jnp.einsum("nk,nkd->nd", coef, rest, precision=HIGHEST)).astype(jnp.bfloat16)
    grad_rest = coef[:, :, None] * grad_read[:, None, :]
    grad_weights = direct + jnp.dot(member, grad_means / denom, precision=HIGHEST)
    grad_logits = weights * (grad_weights - jnp.sum(weights * grad_weights, axis=1, keepdims=True))
    grad_rest = grad_rest + grad_logits[:, :, None] * hop_vector[None, None, :]
    grad_hop = jnp.einsum("nk,nkd->d", grad_logits, rest, precision=HIGHEST)
    grad_layer = jnp.concatenate([grad_read[:, None, :], grad_rest], axis=1).reshape(
        rows_here, width
    )
    grad_branch = grad_layer.astype(jnp.bfloat16)
    grad_activated = jnp.einsum(
        "rd,fd->rf", grad_branch, down_w, preferred_element_type=jnp.float32
    )
    grad_down = jnp.einsum("rf,rd->fd", activated, grad_branch, preferred_element_type=jnp.float32)
    gelu_pull = jax.vjp(exact_gelu, before)[1]
    grad_before = gelu_pull(grad_activated)[0].astype(jnp.bfloat16)
    grad_up = jnp.einsum("rd,rf->df", gathered_two, grad_before, preferred_element_type=jnp.float32)
    piece = grad_before
    grad_normed_two = jnp.einsum("rf,df->rd", piece, up_w, preferred_element_type=jnp.float32)
    norm_two_pull = jax.vjp(norm_rows, residual_one, gain_two, shift_two)[1]
    back_two, grad_gain_two, grad_shift_two = norm_two_pull(grad_normed_two)
    grad_residual = grad_layer + back_two
    grad_attended = grad_residual.astype(jnp.bfloat16)
    grad_context = jnp.einsum(
        "rd,cd->rc", grad_attended, out_w, preferred_element_type=jnp.float32
    ).astype(jnp.bfloat16)
    grad_outw = jnp.einsum("rc,rd->cd", context, grad_attended, preferred_element_type=jnp.float32)
    context_four = grad_context.reshape(shape_four)
    again_scores = masked_scores(query_four, key_four, allowed, scale)
    probs_again = jnp.exp(again_scores - log_total)
    grad_values = jnp.einsum(
        "hqkn,nqhe->nkhe",
        probs_again.astype(jnp.bfloat16),
        context_four,
        preferred_element_type=jnp.float32,
    ).astype(jnp.bfloat16)
    grad_probs = jnp.einsum(
        "nqhe,nkhe->hqkn", context_four, value_four, preferred_element_type=jnp.float32
    )
    grad_scores = probs_again * (
        grad_probs - jnp.sum(probs_again * grad_probs, axis=2, keepdims=True)
    )
    grad_scores = grad_scores.astype(jnp.bfloat16)
    grad_queries = (
        jnp.einsum("hqkn,nkhe->nqhe", grad_scores, key_four, preferred_element_type=jnp.float32)
        * scale
    ).astype(jnp.bfloat16)
    grad_keys = (
        jnp.einsum("hqkn,nqhe->nkhe", grad_scores, query_four, preferred_element_type=jnp.float32)
        * scale
    ).astype(jnp.bfloat16)
    flat_queries = grad_queries.reshape(group_rows, heads_here * HEAD)
    flat_keys = grad_keys.reshape(group_rows, heads_here * HEAD)
    flat_values = grad_values.reshape(group_rows, heads_here * HEAD)
    grad_qw = jnp.einsum(
        "rd,rc->dc", gathered_one, flat_queries, preferred_element_type=jnp.float32
    )
    grad_kw = jnp.einsum("rd,rc->dc", gathered_one, flat_keys, preferred_element_type=jnp.float32)
    grad_vw = jnp.einsum("rd,rc->dc", gathered_one, flat_values, preferred_element_type=jnp.float32)
    total = jnp.einsum("rc,dc->rd", flat_queries, query_w, preferred_element_type=jnp.float32)
    total = total + jnp.einsum("rc,dc->rd", flat_keys, key_w, preferred_element_type=jnp.float32)
    grad_normed_one = total + jnp.einsum(
        "rc,dc->rd", flat_values, value_w, preferred_element_type=jnp.float32
    )
    norm_one_pull = jax.vjp(norm_rows, tokens_f, gain_one, shift_one)[1]
    back_one, grad_gain_one, grad_shift_one = norm_one_pull(grad_normed_one)
    grad_tokens = (grad_residual + back_one).astype(jnp.bfloat16)
    def lead(grad, n):
        return jnp.transpose(grad.reshape(width, tp, n), (1, 0, 2)).astype(jnp.bfloat16)

    left = jnp.concatenate(
        [lead(grad_qw, cols), lead(grad_kw, cols), lead(grad_vw, cols), lead(grad_up, ff_cols)], axis=2
    )
    right = jnp.concatenate(
        [
            grad_outw.reshape(tp, cols, width).astype(jnp.bfloat16),
            grad_down.reshape(tp, ff_cols, width).astype(jnp.bfloat16),
        ],
        axis=1,
    )
    left, right = lax.psum(
        (
            lax.psum_scatter(left, "tp", scatter_dimension=0, tiled=True)[0],
            lax.psum_scatter(right, "tp", scatter_dimension=0, tiled=True)[0],
        ),
        "nodes",
    )
    left, right = left.astype(jnp.float32), right.astype(jnp.float32)
    sum_q, sum_k, sum_v = (left[:, :cols], left[:, cols : 2 * cols], left[:, 2 * cols : 3 * cols])
    sum_up = left[:, 3 * cols :]
    sum_o, sum_down = right[:cols], right[cols:]
    sum_g1, sum_s1, sum_g2, sum_s2, sum_hop = lax.psum(
        (grad_gain_one, grad_shift_one, grad_gain_two, grad_shift_two, grad_hop), ("nodes", "tp")
    )
    return (
        readout,
        grad_tokens,
        sum_g1,
        sum_s1,
        sum_q,
        sum_k,
        sum_v,
        sum_o,
        sum_g2,
        sum_s2,
        sum_up,
        sum_down,
        sum_hop,
    )


def solution(mesh):
    return jax.shard_map(
        shards,
        mesh=mesh,
        in_specs=(
            P(("nodes", "tp"), None),
            P(("nodes", "tp")),
            P(("nodes", "tp")),
            P(),
            P(),
            P(None, "tp"),
            P(None, "tp"),
            P(None, "tp"),
            P("tp", None),
            P(),
            P(),
            P(None, "tp"),
            P("tp", None),
            P(),
            P(("nodes", "tp"), None),
        ),
        out_specs=(
            P(("nodes", "tp"), None),
            P(("nodes", "tp"), None),
            P(),
            P(),
            P(None, "tp"),
            P(None, "tp"),
            P(None, "tp"),
            P("tp", None),
            P(),
            P(),
            P(None, "tp"),
            P("tp", None),
            P(),
        ),
        check_vma=False,
    )
```

```python
import functools

import jax
import jax.numpy as jnp
from jax import lax
from jax.experimental import pallas as pl
from jax.experimental.pallas import tpu as pltpu
from jax.sharding import PartitionSpec as P

HOPS = 8
HEAD = 64
GRAPHS = 64
EPSILON = 1e-05
NEGATIVE = -1000000000.0
MESH = pl.DeviceIdType.MESH
F32 = jnp.float32
BF16 = jnp.bfloat16
CHUNK = 256
TILE = 128


def mm(a, b):
    return lax.dot_general(a, b, (((1,), (0,)), ((), ())), preferred_element_type=F32)


def mm_rt(a, b):
    return lax.dot_general(a, b, (((1,), (1,)), ((), ())), preferred_element_type=F32)


def mm_lt(a, b):
    return lax.dot_general(a, b, (((0,), (0,)), ((), ())), preferred_element_type=F32)


def iota(shape, axis):
    return lax.broadcasted_iota(jnp.int32, shape, axis)


def centred(values):
    centre = values - jnp.mean(values, axis=-1, keepdims=True)
    spread = jnp.mean(centre * centre, axis=-1, keepdims=True)
    return centre * lax.rsqrt(spread + EPSILON), lax.rsqrt(spread + EPSILON)


def gelu_both(x):
    size = jnp.abs(x)
    t = 1.0 / (1.0 + (0.3275911 * 0.7071067811865476) * size)
    bell = jnp.exp(-0.5 * (x * x))
    poly = 1.061405429 * t - 1.453152027
    poly = poly * t + 1.421413741
    poly = poly * t - 0.284496736
    poly = poly * t + 0.254829592
    tail = (0.5 * t) * poly * bell
    phi = jnp.where(x >= 0, 1.0 - tail, tail)
    return x * phi, phi + x * (bell * 0.3989422804014327)


def seg8(x, op, lane):
    for bit in (1, 2, 4):
        up = pltpu.roll(x, bit, x.ndim - 1)
        down = pltpu.roll(x, 128 - bit, x.ndim - 1)
        x = op(x, jnp.where((lane & bit) != 0, up, down))
    return x


class Group:
    def __init__(self, array, wide, recv_core, recv_z, part, recv_plane, final, send, recv):
        self.array, self.wide = array, wide
        self.recv_core, self.recv_z, self.part = recv_core, recv_z, part
        self.recv_plane, self.final = recv_plane, final
        self.send, self.recv = send, recv
        self.half_rows = part.shape[0]
        self.piece_rows = part.shape[0] // 4
        self.width = part.shape[1]

    def half(self, c):
        rows = pl.ds(pl.multiple_of(c * self.half_rows, self.half_rows), self.half_rows)
        return self.array.at[rows] if self.wide else self.array.at[:, rows]

    def slot(self, c, d):
        rows = pl.ds(pl.multiple_of(c * self.half_rows, self.half_rows), self.half_rows)
        if self.wide:
            return self.array.at[rows, d * self.width : (d + 1) * self.width]
        return self.array.at[d, rows]

    def piece(self, ref, p, base=0):
        start = pl.multiple_of(base + p * self.piece_rows, 16)
        return ref.at[pl.ds(start, self.piece_rows)]


def kernel(
    nn,
    tok_hbm,
    mask_ref,
    gid_ref,
    g1_ref,
    s1_ref,
    wq_hbm,
    wk_hbm,
    wv_hbm,
    wo_hbm,
    g2_ref,
    s2_ref,
    wu_hbm,
    wd_hbm,
    hw_ref,
    cot_hbm,
    readout_ref,
    gtok_ref,
    small_ref,
    fin_in_ref,
    fin_out_ref,
    fin_up_ref,
    fin_dn_ref,
    w_in,
    w_up,
    w_od,
    tok,
    cot,
    n1,
    qkv,
    pn,
    ctx,
    res,
    n2,
    act,
    gp,
    lay,
    vcol,
    mt,
    gexp,
    wcol,
    dcol,
    ab,
    zed,
    gbef,
    gl,
    datt,
    dctx,
    dqkv,
    g_up,
    g_dn,
    g_out,
    g_in,
    rc_up,
    rc_dn,
    rc_out,
    rc_in,
    rz_up,
    rz_dn,
    rz_out,
    rz_in,
    sm_up,
    sm_dn,
    sm_out,
    sm_in,
    rp_up,
    rp_dn,
    rp_out,
    rp_in,
    ar_one,
    ar_nodes,
    ar_tp,
    sv_one,
    sv_nodes,
    sv_tp,
    lsem,
    wsend,
    wrecv,
    gsend,
    grecv,
    asend,
    arecv,
    bsend,
    brecv,
):
    n, t = lax.axis_index("nodes"), lax.axis_index("tp")
    rows_here, width = tok.shape
    chunks = rows_here // CHUNK
    tiles = rows_here // TILE
    c = n % 2
    plane = (n // 2) % 4
    half = (plane % 2 + plane // 2) % 2
    quarter = 2 * half + c
    other = 2 * (1 - half) + c
    extra = [b for b in range(3, 12) if (1 << b) < nn]

    def node_peer(k):
        out = n
        for b in range(12):
            if (k >> b) & 1:
                bit = (n // (1 << b)) % 2
                out = out + (1 << b) * (1 - 2 * bit)
        return (out, t)

    def tp_peer(k):
        out = t
        for b in range(2):
            if (k >> b) & 1:
                bit = (t // (1 << b)) % 2
                out = out + (1 << b) * (1 - 2 * bit)
        return (n, out)

    def remote(src, dst, ssem, rsem, peer):
        return pltpu.make_async_remote_copy(
            src_ref=src, dst_ref=dst, send_sem=ssem, recv_sem=rsem, device_id=peer, device_id_type=MESH
        )

    qw = wq_hbm.shape[1]
    local = [
        pltpu.make_async_copy(wq_hbm, w_in.at[:, 0:qw], lsem.at[0]),
        pltpu.make_async_copy(wk_hbm, w_in.at[:, qw : 2 * qw], lsem.at[1]),
        pltpu.make_async_copy(wv_hbm, w_in.at[:, 2 * qw : 3 * qw], lsem.at[2]),
        pltpu.make_async_copy(tok_hbm, tok, lsem.at[3]),
        pltpu.make_async_copy(wo_hbm, w_od.at[0, 0:qw], lsem.at[4]),
        pltpu.make_async_copy(wd_hbm, w_od.at[0, qw:], lsem.at[5]),
        pltpu.make_async_copy(wu_hbm, w_up.at[:, 0 : wu_hbm.shape[1]], lsem.at[6]),
        pltpu.make_async_copy(cot_hbm, cot, lsem.at[7]),
    ]
    for copy in local:
        copy.start()

    barrier = pltpu.get_barrier_semaphore()
    greet = [node_peer(k) for k in range(1, 8)] + [node_peer(1 << b) for b in extra]
    greet += [tp_peer(k) for k in range(1, 4)]
    for peer in greet:
        pl.semaphore_signal(barrier, inc=1, device_id=peer, device_id_type=MESH)
    pl.semaphore_wait(barrier, len(greet))

    def block_of(ref, group, rows, d0, d1):
        if group == 1:
            return ref.at[d0:d1, rows]
        w = ref.shape[1] // 4
        return ref.at[rows, d0 * w : d1 * w]

    weights = [(w_in, 0), (w_od, 1), (w_up, 2)]

    def weight_copies(which):
        ref, group = weights[which]
        total = ref.shape[1] if group == 1 else ref.shape[0]
        quart = total // 4

        def rows(q, off, size):
            return pl.ds(pl.multiple_of(q * quart + off, 16), size)

        base = which * 7
        out = []
        for d in range(1, 4):
            out.append(
                remote(
                    block_of(ref, group, rows(quarter, 0, quart), 0, 1),
                    block_of(ref, group, rows(quarter, 0, quart), d, d + 1),
                    wsend.at[base + d - 1],
                    wrecv.at[base + d - 1],
                    tp_peer(d),
                )
            )
        for e, peer in enumerate((2, 4)):
            piece = block_of(ref, group, rows(quarter, e * (quart // 2), quart // 2), 1, 4)
            out.append(remote(piece, piece, wsend.at[base + 3 + e], wrecv.at[base + 3 + e], node_peer(peer)))
        for e, q in enumerate((quarter, other)):
            piece = block_of(ref, group, rows(q, 0, quart), 1, 4)
            out.append(remote(piece, piece, wsend.at[base + 5 + e], wrecv.at[base + 5 + e], node_peer(1)))
        return out

    copies_in, copies_od, copies_up = weight_copies(0), weight_copies(1), weight_copies(2)

    def step_z(copies):
        for cp in copies[0:3]:
            cp.start()

    def step_plane(copies):
        for cp in copies[0:3]:
            cp.wait()
        for cp in copies[3:6]:
            cp.start()

    def step_core(copies):
        for cp in copies[3:5]:
            cp.wait()
        copies[6].start()

    def step_end(copies):
        for cp in copies[5:7]:
            cp.wait()

    for i in (0, 1, 2):
        local[i].wait()
    step_z(copies_in)

    gain1 = g1_ref[...].astype(F32)
    shift1 = s1_ref[...].astype(F32)
    gain2 = g2_ref[...].astype(F32)
    shift2 = s2_ref[...].astype(F32)
    hopw = hw_ref[...].astype(F32)

    eye = iota((TILE, TILE), 0) == iota((TILE, TILE), 1)
    ones = jnp.ones((TILE, TILE), BF16)
    lane8 = iota((HOPS, TILE), 1)
    block8 = lane8 // HOPS
    left = iota((TILE, TILE), 1) < HEAD
    nodes_chunk = CHUNK // HOPS
    spread_c = (iota((CHUNK, nodes_chunk), 0) // HOPS == iota((CHUNK, nodes_chunk), 1)).astype(F32).astype(BF16)

    def rows_of(i, size):
        return pl.ds(pl.multiple_of(i * size, size), size)

    mask_f = mask_ref[...].astype(F32)
    for i in range(tiles):
        col = mm(jnp.where(eye, mask_f[i : i + 1, :], 0.0).astype(BF16), ones)
        vcol[i * TILE : (i + 1) * TILE, :] = col
        acc = jnp.zeros((HOPS, TILE), F32)
        col3 = col.reshape(TILE // HOPS, HOPS, TILE)
        for r in range(TILE // HOPS):
            acc = jnp.where(block8 == r, col3[r], acc)
        mt[i] = acc
    gcol = mm(jnp.where(eye, gid_ref[...].astype(F32), 0.0).astype(BF16), ones).astype(BF16)
    for i in range(chunks):
        gexp[i * CHUNK : (i + 1) * CHUNK, :] = mm(spread_c, gcol[i * nodes_chunk : (i + 1) * nodes_chunk])

    local[3].wait()

    def norm_one(i, carry):
        x = tok[rows_of(i, CHUNK), :].astype(F32)
        hat, _ = centred(x)
        n1[rows_of(i, CHUNK), :] = (hat * gain1 + shift1).astype(BF16)
        return carry

    lax.fori_loop(0, chunks, norm_one, 0)

    for i in (4, 5, 6, 7):
        local[i].wait()
    step_plane(copies_in)
    step_z(copies_od)
    step_z(copies_up)
    step_core(copies_in)
    step_end(copies_in)

    def project(i, carry):
        r = rows_of(i, CHUNK)
        out = mm(n1[r, :], w_in[...])
        for d in range(4):
            base = d * 3 * qw
            qkv[r, base : base + qw] = (out[:, base : base + qw] * (HEAD**-0.5)).astype(BF16)
            qkv[r, base + qw : base + 3 * qw] = out[:, base + qw : base + 3 * qw].astype(BF16)
        return carry

    lax.fori_loop(0, chunks, project, 0)
    step_plane(copies_od)
    step_plane(copies_up)

    def pair(x):
        zero = jnp.zeros_like(x)
        return jnp.concatenate([jnp.where(left, x, zero), jnp.where(left, zero, x)], axis=0)

    def compact(x):
        out = []
        for h in range(2):
            x3 = x[:, h * TILE : (h + 1) * TILE].reshape(TILE // HOPS, HOPS, TILE)
            acc = x3[0]
            for r in range(1, TILE // HOPS):
                acc = jnp.where(block8 == r, x3[r], acc)
            out.append(acc)
        return out

    def expand(pairs):
        cols = []
        for x in pairs:
            zero = jnp.zeros_like(x)
            cols.append(
                jnp.concatenate([jnp.where(block8 == r, x, zero) for r in range(TILE // HOPS)], axis=0).astype(BF16)
            )
        return jnp.concatenate(cols, axis=1)

    def attend(i, carry):
        r = rows_of(i, TILE)
        keep = mask_ref[pl.ds(i, 1), :].astype(F32) > 0.5
        for d in range(4):
            base = d * 3 * qw
            q = qkv[r, base : base + qw]
            k = qkv[r, base + qw : base + 2 * qw]
            v = qkv[r, base + 2 * qw : base + 3 * qw]
            scores = compact(mm_rt(q, pair(k)))
            probs = []
            for h in range(2):
                s = jnp.where(keep, scores[h], NEGATIVE)
                e = jnp.exp(s - seg8(s, jnp.maximum, lane8))
                p = e / seg8(e, jnp.add, lane8)
                pn[i * 8 + 2 * d + h] = p
                probs.append(p)
            ctx[r, d * qw : (d + 1) * qw] = mm(expand(probs), pair(v)).astype(BF16)
        return carry

    lax.fori_loop(0, tiles, attend, 0)
    step_core(copies_od)
    step_core(copies_up)
    step_end(copies_od)
    step_end(copies_up)

    ow = w_od.shape[1]
    down_rows = ow - qw

    def w_out():
        return w_od[:, 0:qw, :].reshape(4 * qw, width)

    def w_down():
        return w_od[:, qw:ow, :].reshape(4 * down_rows, width)

    hop3 = iota((nodes_chunk, HOPS, TILE), 1)
    lane3 = iota((nodes_chunk, HOPS, TILE), 2)
    node3 = iota((nodes_chunk, HOPS, TILE), 0)
    lane_graph = (lane3 % GRAPHS).astype(F32)

    def feed(i, acc):
        r = rows_of(i, CHUNK)
        attended = mm(ctx[r, :], w_out())
        x = tok[r, :].astype(F32) + attended
        res[r, :] = x
        hat, _ = centred(x)
        normed = (hat * gain2 + shift2).astype(BF16)
        n2[r, :] = normed
        value, slope = gelu_both(mm(normed, w_up[...]))
        value = value.astype(BF16)
        act[r, :] = value
        gp[r, :] = slope.astype(BF16)
        out = x + mm(value, w_down())
        lay[r, :] = out
        dr = mm(spread_c, cot[rows_of(i, nodes_chunk), :])
        logit = jnp.sum(out * hopw, axis=-1, keepdims=True)
        gcoef = jnp.sum(out * dr, axis=-1, keepdims=True)
        shape = (nodes_chunk, HOPS, TILE)
        valid = vcol[r, :].reshape(shape)
        valid = jnp.where(hop3 > 0, valid, 0.0)
        logit = jnp.where(valid > 0.5, jnp.broadcast_to(logit, (CHUNK, TILE)).reshape(shape), NEGATIVE)
        e = jnp.exp(logit - jnp.max(logit, axis=1, keepdims=True))
        e = jnp.where(hop3 > 0, e, 0.0)
        weight = e / jnp.sum(e, axis=1, keepdims=True)
        direct = valid * jnp.broadcast_to(gcoef, (CHUNK, TILE)).reshape(shape)
        wcol[r, :] = weight.reshape(CHUNK, TILE)
        dcol[r, :] = direct.reshape(CHUNK, TILE)
        mine = gexp[r, :].reshape(shape) == lane_graph
        both = jnp.where(lane3 < GRAPHS, jnp.where(hop3 == 0, 1.0, weight), -direct)
        return acc + jnp.sum(jnp.where(mine, both, 0.0), axis=0)

    sums = lax.fori_loop(0, chunks, feed, jnp.zeros((HOPS, TILE), F32))

    def reduce_all(value, one, by_nodes, by_tp, ssem, rsem, overlap=None):
        one[0] = value
        copies = [
            remote(one.at[0], by_nodes.at[k - 1], ssem.at[k - 1], rsem.at[k - 1], node_peer(k)) for k in range(1, 8)
        ]
        for cp in copies:
            cp.start()
        if overlap is not None:
            overlap()
        for cp in copies:
            cp.wait()
        value = one[0]
        for k in range(7):
            value = value + by_nodes[k]
        at = 7
        for b in extra:
            one[at - 6] = value
            cp = remote(one.at[at - 6], by_nodes.at[at], ssem.at[at], rsem.at[at], node_peer(1 << b))
            cp.start()
            cp.wait()
            value = value + by_nodes[at]
            at += 1
        last = one.shape[0] - 1
        one[last] = value
        copies = [
            remote(one.at[last], by_tp.at[k - 1], ssem.at[at + k - 1], rsem.at[at + k - 1], tp_peer(k))
            for k in range(1, 4)
        ]
        for cp in copies:
            cp.start()
        return copies, lambda: one[last] + by_tp[0] + by_tp[1] + by_tp[2]

    def small_products():
        drdown = mm_rt(cot[...], w_down()).astype(BF16)
        hopdown = mm_rt(jnp.broadcast_to(hw_ref[...], (16, width)), w_down()).astype(BF16)
        for i in range(chunks):
            piece = drdown[i * nodes_chunk : (i + 1) * nodes_chunk]
            ab[i, 0:nodes_chunk] = piece
            ab[i, nodes_chunk : 2 * nodes_chunk] = piece
            ab[i, 2 * nodes_chunk : 2 * nodes_chunk + 16] = hopdown
            ab[i, 2 * nodes_chunk + 16 :] = jnp.zeros((TILE - 2 * nodes_chunk - 16, ab.shape[2]), BF16)

    copies, total = reduce_all(sums, ar_one, ar_nodes, ar_tp, asend, arecv, small_products)
    for cp in copies:
        cp.wait()
    sums = total()
    row = jnp.broadcast_to(sums[0:1, :], (HOPS, TILE))
    counts = jnp.where(lane8 < GRAPHS, row, pltpu.roll(row, GRAPHS, 1))
    means = (sums / (counts + 1.0))[None]

    def back_one(i, carry):
        gain_acc, shift_acc, hop_acc, zed_acc = carry
        r = rows_of(i, CHUNK)
        shape = (nodes_chunk, HOPS, TILE)
        picked = jnp.where(gexp[r, :].reshape(shape) == lane_graph, means, 0.0)
        mean_r = jnp.sum(jnp.where(lane3 < GRAPHS, picked, 0.0), axis=-1, keepdims=True)
        grad_mean = jnp.sum(jnp.where(lane3 < GRAPHS, 0.0, picked), axis=-1, keepdims=True)
        weight = wcol[r, :].reshape(shape)
        valid = vcol[r, :].reshape(shape)
        coef = jnp.where(hop3 > 0, valid * (weight - mean_r), 1.0)
        grad_w = dcol[r, :].reshape(shape) + grad_mean
        glog = weight * (grad_w - jnp.sum(weight * grad_w, axis=1, keepdims=True))
        coef_hi = coef.astype(BF16).astype(F32)
        glog_hi = glog.astype(BF16).astype(F32)
        zero = jnp.zeros_like(coef)
        mix = jnp.where(lane3 == node3, coef_hi, zero)
        mix = jnp.where(lane3 == node3 + nodes_chunk, coef - coef_hi, mix)
        mix = jnp.where(lane3 == 2 * nodes_chunk, glog_hi, mix)
        mix = jnp.where(lane3 == 2 * nodes_chunk + 1, glog - glog_hi, mix)
        mix = mix.reshape(CHUNK, TILE).astype(BF16)

        dr = cot[rows_of(i, nodes_chunk), :]
        hop16 = jnp.broadcast_to(hw_ref[...], (16, width))
        rest = jnp.zeros((TILE - 2 * nodes_chunk - 16, width), BF16)
        dh = jnp.concatenate([dr, dr, hop16, rest], axis=0)
        grad_layer = mm(mix, dh)
        gl[r, :] = grad_layer
        before_back = (mm(mix, ab[i]) * gp[r, :].astype(F32)).astype(BF16)
        gbef[r, :] = before_back

        seen = mm_lt(mix, lay[r, :].astype(BF16))
        readout_ref[rows_of(i, nodes_chunk), :] = (seen[0:nodes_chunk] + seen[nodes_chunk : 2 * nodes_chunk]).astype(
            BF16
        )
        hop_acc = hop_acc + seen[2 * nodes_chunk : 2 * nodes_chunk + 8]
        fold = mm_lt(mix, act[r, :])
        zed[rows_of(i, nodes_chunk), :] = (fold[0:nodes_chunk] + fold[nodes_chunk : 2 * nodes_chunk]).astype(BF16)
        zed_acc = zed_acc + fold[2 * nodes_chunk : 2 * nodes_chunk + 8]

        dy = mm_rt(before_back, w_up[...])
        hat, inv = centred(res[r, :])
        gain_acc = gain_acc + jnp.sum((dy * hat).reshape(nodes_chunk, HOPS, width), axis=0)
        shift_acc = shift_acc + jnp.sum(dy.reshape(nodes_chunk, HOPS, width), axis=0)
        g = dy * gain2
        back = inv * (
            g - jnp.mean(g, axis=-1, keepdims=True) - hat * jnp.mean(g * hat, axis=-1, keepdims=True)
        )
        grad_res = grad_layer + back
        gl[r, :] = grad_res
        att = grad_res.astype(BF16)
        datt[r, :] = att
        dctx[r, :] = mm_rt(att, w_out()).astype(BF16)
        return gain_acc, shift_acc, hop_acc, zed_acc

    zero8 = jnp.zeros((HOPS, width), F32)
    gain_two, shift_two, hop_sum, zed_sum = lax.fori_loop(
        0, chunks, back_one, (zero8, zero8, zero8, jnp.zeros((HOPS, zed.shape[1]), F32))
    )

    groups = []
    sets = [
        (g_dn, False, rc_dn, rz_dn, sm_dn, rp_dn, fin_dn_ref),
        (g_up, True, rc_up, rz_up, sm_up, rp_up, fin_up_ref),
        (g_out, False, rc_out, rz_out, sm_out, rp_out, fin_out_ref),
        (g_in, True, rc_in, rz_in, sm_in, rp_in, fin_in_ref),
    ]
    for i, item in enumerate(sets):
        groups.append(Group(*item, gsend.at[i], grecv.at[i]))
    dn, up, ot, qk = groups

    def core_copy(g):
        return remote(g.half(1 - c), g.recv_core, g.send.at[0], g.recv.at[0], node_peer(1))

    def z_copies(g):
        return [
            remote(g.slot(c, d), g.recv_z.at[d - 1], g.send.at[d], g.recv.at[d], tp_peer(d)) for d in range(1, 4)
        ]

    def plane_peer_piece(e):
        out = plane
        for b in range(2):
            if (e >> b) & 1:
                out = out + (1 << b) * (1 - 2 * ((plane // (1 << b)) % 2))
        return out

    def plane_copies(g):
        return [
            remote(
                g.piece(g.part, plane_peer_piece(e)),
                g.recv_plane.at[e - 1],
                g.send.at[3 + e],
                g.recv.at[3 + e],
                node_peer(2 * e),
            )
            for e in range(1, 4)
        ]

    def final_copies(g):
        mine = g.piece(g.final, plane, c * g.half_rows)
        return [remote(mine, mine, g.send.at[6 + e], g.recv.at[6 + e], node_peer(2 * e)) for e in range(1, 4)]

    def last_copy(g):
        rows = g.final.at[pl.ds(pl.multiple_of(c * g.half_rows, g.half_rows), g.half_rows)]
        return remote(rows, rows, g.send.at[10], g.recv.at[10], node_peer(1))

    def go_core(g):
        core_copy(g).start()

    def go_z(g):
        core_copy(g).wait()
        mine = g.half(c)
        mine[...] = (mine[...].astype(F32) + g.recv_core[...].astype(F32)).astype(BF16)
        for cp in z_copies(g):
            cp.start()

    def go_plane(g):
        for cp in z_copies(g):
            cp.wait()
        total = g.slot(c, 0)[...].astype(F32)
        for d in range(3):
            total = total + g.recv_z[d].astype(F32)
        g.part[...] = total.astype(BF16)
        for cp in plane_copies(g):
            cp.start()

    def go_final(g):
        for cp in plane_copies(g):
            cp.wait()
        total = g.piece(g.part, plane)[...].astype(F32)
        for e in range(3):
            total = total + g.recv_plane[e].astype(F32)
        for j, b in enumerate(extra):
            g.recv_plane[3 + 2 * j] = total.astype(BF16)
            cp = remote(
                g.recv_plane.at[3 + 2 * j],
                g.recv_plane.at[4 + 2 * j],
                g.send.at[11 + j],
                g.recv.at[11 + j],
                node_peer(1 << b),
            )
            cp.start()
            cp.wait()
            total = total + g.recv_plane[4 + 2 * j].astype(F32)
        g.piece(g.final, plane, c * g.half_rows)[...] = total.astype(BF16)
        for cp in final_copies(g):
            cp.start()

    def go_last(g):
        for cp in final_copies(g):
            cp.wait()
        last_copy(g).start()

    def finish(g):
        last_copy(g).wait()

    zed[rows_here // HOPS :, :] = jnp.concatenate([zed_sum, jnp.zeros_like(zed_sum)], axis=0).astype(BF16)
    drh = jnp.concatenate([cot[...], jnp.broadcast_to(hw_ref[...], (16, width))], axis=0)
    g_dn[...] = mm_lt(zed[...], drh).astype(BF16).reshape(g_dn.shape)
    go_core(dn)
    g_up[...] = mm_lt(n2[...], gbef[...]).astype(BF16)
    go_core(up)
    go_z(dn)
    g_out[...] = mm_lt(ctx[...], datt[...]).astype(BF16).reshape(g_out.shape)
    go_core(ot)
    go_z(up)

    def attend_back(i, carry):
        r = rows_of(i, TILE)
        keep = mt[i] > 0.5
        for d in range(4):
            base = d * 3 * qw
            q = qkv[r, base : base + qw]
            k = qkv[r, base + qw : base + 2 * qw]
            v = qkv[r, base + 2 * qw : base + 3 * qw]
            do = dctx[r, d * qw : (d + 1) * qw]
            k2, q2, v2, do2 = pair(k), pair(q), pair(v), pair(do)
            grad_p = compact(mm_rt(do, v2))
            ds = []
            for h in range(2):
                p = pn[i * 8 + 2 * d + h]
                ds.append(p * (grad_p[h] - seg8(p * grad_p[h], jnp.add, lane8)))
            dqkv[r, base : base + qw] = (mm(expand(ds), k2) * (HEAD**-0.5)).astype(BF16)
            scores = compact(mm_rt(k, q2))
            grad_pt = compact(mm_rt(v, do2))
            probs, dst = [], []
            for h in range(2):
                s = jnp.where(keep, scores[h], NEGATIVE)
                e = jnp.exp(s - jnp.max(s, axis=0, keepdims=True))
                p = e / jnp.sum(e, axis=0, keepdims=True)
                probs.append(p)
                dst.append(p * (grad_pt[h] - jnp.sum(p * grad_pt[h], axis=0, keepdims=True)))
            dqkv[r, base + qw : base + 2 * qw] = mm(expand(dst), q2).astype(BF16)
            dqkv[r, base + 2 * qw : base + 3 * qw] = mm(expand(probs), do2).astype(BF16)
        return carry

    lax.fori_loop(0, tiles, attend_back, 0)
    go_z(ot)
    go_plane(dn)
    go_plane(up)
    g_in[...] = mm_lt(n1[...], dqkv[...]).astype(BF16)
    go_core(qk)
    go_plane(ot)
    go_final(dn)
    go_final(up)

    def back_two(i, carry):
        gain_acc, shift_acc = carry
        r = rows_of(i, CHUNK)
        dy = mm_rt(dqkv[r, :], w_in[...])
        hat, inv = centred(tok[r, :].astype(F32))
        gain_acc = gain_acc + jnp.sum((dy * hat).reshape(nodes_chunk, HOPS, width), axis=0)
        shift_acc = shift_acc + jnp.sum(dy.reshape(nodes_chunk, HOPS, width), axis=0)
        g = dy * gain1
        back = inv * (
            g - jnp.mean(g, axis=-1, keepdims=True) - hat * jnp.mean(g * hat, axis=-1, keepdims=True)
        )
        gtok_ref[r, :] = (gl[r, :] + back).astype(BF16)
        return gain_acc, shift_acc

    go_z(qk)
    gain_one, shift_one = lax.fori_loop(0, chunks, back_two, (zero8, zero8))

    def fold8(x):
        return jnp.sum(x, axis=0, keepdims=True)

    small = jnp.concatenate(
        [fold8(gain_one), fold8(shift_one), fold8(gain_two), fold8(shift_two), fold8(hop_sum[0:2]), zero8[0:3]], axis=0
    )

    def rest_of():
        go_final(ot)
        go_last(dn)
        go_last(up)
        go_plane(qk)

    copies, total_small = reduce_all(small, sv_one, sv_nodes, sv_tp, bsend, brecv, rest_of)
    go_last(ot)
    go_final(qk)
    finish(dn)
    finish(up)
    finish(ot)
    for cp in copies:
        cp.wait()
    small_ref[...] = total_small()
    go_last(qk)
    finish(qk)


def shards(
    nn,
    tokens,
    hop_mask,
    graph_ids,
    norm1_gain,
    norm1_shift,
    w_query,
    w_key,
    w_value,
    w_out,
    norm2_gain,
    norm2_shift,
    w_up,
    w_down,
    hop_weight,
    cotangent,
):
    rows, width = tokens.shape
    nodes = rows // HOPS
    qw, uw = w_query.shape[1], w_up.shape[1]
    vm = pl.BlockSpec(memory_space=pltpu.VMEM)
    hbm = pl.BlockSpec(memory_space=pl.ANY)
    extra = len([b for b in range(3, 12) if (1 << b) < nn])

    def v(*shape, dtype=BF16):
        return pltpu.VMEM(shape, dtype)

    tiles, chunks = rows // TILE, rows // CHUNK
    half = width // 2
    scratch = [
        v(width, 12 * qw),
        v(width, 4 * uw),
        v(4, qw + uw, width),
        v(rows, width),
        v(nodes, width),
        v(rows, width),
        v(rows, 12 * qw),
        v(tiles * 8, HOPS, TILE, dtype=F32),
        v(rows, width),
        v(rows, width, dtype=F32),
        v(rows, width),
        v(rows, 4 * uw),
        v(rows, 4 * uw),
        v(rows, width, dtype=F32),
        v(rows, TILE, dtype=F32),
        v(tiles, HOPS, TILE, dtype=F32),
        v(rows, TILE, dtype=F32),
        v(rows, TILE, dtype=F32),
        v(rows, TILE, dtype=F32),
        v(chunks, TILE, 4 * uw),
        v(nodes + 16, 4 * uw),
        v(rows, 4 * uw),
        v(rows, width, dtype=F32),
        v(rows, width),
        v(rows, width),
        v(rows, 12 * qw),
        v(width, 4 * uw),
        v(4, uw, width),
        v(4, qw, width),
        v(width, 12 * qw),
        v(half, 4 * uw),
        v(4, uw // 2, width),
        v(4, qw // 2, width),
        v(half, 12 * qw),
        v(3, half, uw),
        v(3, uw // 2, width),
        v(3, qw // 2, width),
        v(3, half, 3 * qw),
        v(half, uw),
        v(uw // 2, width),
        v(qw // 2, width),
        v(half, 3 * qw),
        v(3 + 2 * extra, half // 4, uw),
        v(3 + 2 * extra, uw // 8, width),
        v(3 + 2 * extra, qw // 8, width),
        v(3 + 2 * extra, half // 4, 3 * qw),
        v(2 + extra, HOPS, TILE, dtype=F32),
        v(7 + extra, HOPS, TILE, dtype=F32),
        v(3, HOPS, TILE, dtype=F32),
        v(2 + extra, 8, width, dtype=F32),
        v(7 + extra, 8, width, dtype=F32),
        v(3, 8, width, dtype=F32),
        pltpu.SemaphoreType.DMA((8,)),
        pltpu.SemaphoreType.DMA((21,)),
        pltpu.SemaphoreType.DMA((21,)),
        pltpu.SemaphoreType.DMA((4, 11 + extra)),
        pltpu.SemaphoreType.DMA((4, 11 + extra)),
        pltpu.SemaphoreType.DMA((10 + extra,)),
        pltpu.SemaphoreType.DMA((10 + extra,)),
        pltpu.SemaphoreType.DMA((10 + extra,)),
        pltpu.SemaphoreType.DMA((10 + extra,)),
    ]
    outs = [
        jax.ShapeDtypeStruct((nodes, width), BF16),
        jax.ShapeDtypeStruct((rows, width), BF16),
        jax.ShapeDtypeStruct((8, width), F32),
        jax.ShapeDtypeStruct((width, 3 * qw), BF16),
        jax.ShapeDtypeStruct((qw, width), BF16),
        jax.ShapeDtypeStruct((width, uw), BF16),
        jax.ShapeDtypeStruct((uw, width), BF16),
    ]
    line = (1, width)
    readout, gtok, small, fin_in, fin_out, fin_up, fin_dn = pl.pallas_call(
        functools.partial(kernel, nn),
        out_shape=outs,
        in_specs=[hbm, vm, vm, vm, vm, hbm, hbm, hbm, hbm, vm, vm, hbm, hbm, vm, hbm],
        out_specs=[vm] * 7,
        scratch_shapes=scratch,
        compiler_params=pltpu.CompilerParams(
            collective_id=0, has_side_effects=True, vmem_limit_bytes=60 * 1024 * 1024
        ),
        name="layer",
    )(
        tokens,
        hop_mask.reshape(tiles, TILE),
        graph_ids.reshape(1, nodes),
        norm1_gain.reshape(line),
        norm1_shift.reshape(line),
        w_query,
        w_key,
        w_value,
        w_out,
        norm2_gain.reshape(line),
        norm2_shift.reshape(line),
        w_up,
        w_down,
        hop_weight.reshape(line),
        cotangent,
    )
    fin_in = fin_in.astype(F32)
    return (
        readout,
        gtok,
        small[0],
        small[1],
        fin_in[:, 0:qw],
        fin_in[:, qw : 2 * qw],
        fin_in[:, 2 * qw :],
        fin_out.astype(F32),
        small[2],
        small[3],
        fin_up.astype(F32),
        fin_dn.astype(F32),
        small[4],
    )


def solution(mesh):
    spread = P(("nodes", "tp"), None)
    flat = P(("nodes", "tp"))
    cols, rows = P(None, "tp"), P("tp", None)
    return jax.shard_map(
        functools.partial(shards, mesh.shape["nodes"]),
        mesh=mesh,
        in_specs=(spread, flat, flat, P(), P(), cols, cols, cols, rows, P(), P(), cols, rows, P(), spread),
        out_specs=(spread, spread, P(), P(), cols, cols, cols, rows, P(), P(), cols, rows, P()),
        check_vma=False,
    )
```

```python
import functools

import jax
import jax.numpy as jnp
from jax import lax
from jax.experimental import pallas as pl
from jax.experimental.pallas import tpu as pltpu
from jax.sharding import PartitionSpec as P

HOPS = 8
HEAD = 64
GRAPHS = 64
EPSILON = 1e-05
NEGATIVE = -1000000000.0
MESH = pl.DeviceIdType.MESH
F32 = jnp.float32
BF16 = jnp.bfloat16
CHUNK = 256
TILE = 128


def mm(a, b):
    return lax.dot_general(a, b, (((1,), (0,)), ((), ())), preferred_element_type=F32)


def mm_rt(a, b):
    return lax.dot_general(a, b, (((1,), (1,)), ((), ())), preferred_element_type=F32)


def mm_lt(a, b):
    return lax.dot_general(a, b, (((0,), (0,)), ((), ())), preferred_element_type=F32)


def iota(shape, axis):
    return lax.broadcasted_iota(jnp.int32, shape, axis)


def centred(values):
    centre = values - jnp.mean(values, axis=-1, keepdims=True)
    spread = jnp.mean(centre * centre, axis=-1, keepdims=True)
    return centre * lax.rsqrt(spread + EPSILON), lax.rsqrt(spread + EPSILON)


def gelu_both(x):
    size = jnp.abs(x)
    t = 1.0 / (1.0 + (0.3275911 * 0.7071067811865476) * size)
    bell = jnp.exp(-0.5 * (x * x))
    poly = 1.061405429 * t - 1.453152027
    poly = poly * t + 1.421413741
    poly = poly * t - 0.284496736
    poly = poly * t + 0.254829592
    tail = (0.5 * t) * poly * bell
    phi = jnp.where(x >= 0, 1.0 - tail, tail)
    return x * phi, phi + x * (bell * 0.3989422804014327)


def tokens_of(ref):
    return ref[...].astype(F32).reshape(1, ref.shape[0])


class Group:
    def __init__(self, array, wide, cols, recv_core, recv_plane, recv_z, final, send, recv, base):
        self.array, self.wide = array, wide
        self.cols = cols
        self.recv_core, self.recv_plane, self.recv_z = recv_core, recv_plane, recv_z
        self.final = final
        self.send, self.recv, self.base = send, recv, base
        rows = final.shape[0]
        self.half_rows = rows // 2
        self.piece_rows = rows // 8
        self.width = final.shape[1]

    def sems(self, k):
        return self.send.at[self.base + k], self.recv.at[self.base + k]

    def rows(self, c, p=None):
        if p is None:
            return pl.ds(pl.multiple_of(c * self.half_rows, 16), self.half_rows)
        return pl.ds(pl.multiple_of(c * self.half_rows + p * self.piece_rows, 16), self.piece_rows)

    def block(self, rows):
        if self.wide:
            return self.array.at[rows, self.cols[0] * self.width : self.cols[1] * self.width]
        return self.array.at[:, rows]

    def slot(self, rows, d):
        if self.wide:
            return self.array.at[rows, d * self.width : (d + 1) * self.width]
        return self.array.at[d, rows]


def kernel(
    nn,
    tok_hbm,
    mask_ref,
    gid_ref,
    g1_ref,
    s1_ref,
    wq_hbm,
    wk_hbm,
    wv_hbm,
    wo_hbm,
    g2_ref,
    s2_ref,
    wu_hbm,
    wd_hbm,
    hw_ref,
    cot_hbm,
    readout_ref,
    gtok_ref,
    small_ref,
    fin_in_ref,
    fin_out_ref,
    fin_up_ref,
    fin_dn_ref,
    w_in,
    w_up,
    w_od,
    tok,
    cot,
    n1,
    qkv,
    pn,
    ctx,
    res,
    n2,
    act,
    gp,
    lay,
    emask,
    pmask,
    vcol,
    mt,
    gexp,
    wcol,
    dcol,
    ab,
    zed,
    gbef,
    gl,
    datt,
    dctx,
    dqkv,
    g_up,
    g_dn,
    g_out,
    g_in,
    rc_up,
    rc_dn,
    rc_out,
    rc_in,
    rp_up,
    rp_dn,
    rp_out,
    rp_in,
    rz_up,
    rz_dn,
    rz_out,
    rz_in,
    ar_one,
    ar_nodes,
    ar_tp,
    sv_one,
    sv_nodes,
    sv_tp,
    lsem,
    wsend,
    wrecv,
    gsend,
    grecv,
    asend,
    arecv,
    bsend,
    brecv,
):
    n, t = lax.axis_index("nodes"), lax.axis_index("tp")
    rows_here, width = tok.shape
    chunks = rows_here // CHUNK
    tiles = rows_here // TILE
    c = n % 2
    plane = (n // 2) % 4
    eighth = 4 * c + plane
    extra = [b for b in range(3, 12) if (1 << b) < nn]

    def node_peer(k):
        out = n
        for b in range(12):
            if (k >> b) & 1:
                bit = (n // (1 << b)) % 2
                out = out + (1 << b) * (1 - 2 * bit)
        return (out, t)

    def tp_peer(k):
        out = t
        for b in range(2):
            if (k >> b) & 1:
                bit = (t // (1 << b)) % 2
                out = out + (1 << b) * (1 - 2 * bit)
        return (n, out)

    def remote(src, dst, ssem, rsem, peer):
        return pltpu.make_async_remote_copy(
            src_ref=src, dst_ref=dst, send_sem=ssem, recv_sem=rsem, device_id=peer, device_id_type=MESH
        )

    qw = wq_hbm.shape[1]
    local = [
        pltpu.make_async_copy(wq_hbm, w_in.at[:, 0:qw], lsem.at[0]),
        pltpu.make_async_copy(wk_hbm, w_in.at[:, qw : 2 * qw], lsem.at[1]),
        pltpu.make_async_copy(wv_hbm, w_in.at[:, 2 * qw : 3 * qw], lsem.at[2]),
        pltpu.make_async_copy(tok_hbm, tok, lsem.at[3]),
        pltpu.make_async_copy(wo_hbm, w_od.at[0, 0:qw], lsem.at[4]),
        pltpu.make_async_copy(wd_hbm, w_od.at[0, qw:], lsem.at[5]),
        pltpu.make_async_copy(wu_hbm, w_up.at[:, 0 : wu_hbm.shape[1]], lsem.at[6]),
        pltpu.make_async_copy(cot_hbm, cot, lsem.at[7]),
    ]
    for copy in local:
        copy.start()

    barrier = pltpu.get_barrier_semaphore()
    greet = [node_peer(k) for k in range(1, 8)] + [node_peer(1 << b) for b in extra]
    greet += [tp_peer(k) for k in range(1, 4)]
    for peer in greet:
        pl.semaphore_signal(barrier, inc=1, device_id=peer, device_id_type=MESH)
    pl.semaphore_wait(barrier, len(greet))

    def weight_block(ref, off, size, d0, d1):
        rows = pl.ds(pl.multiple_of(off, 16), size)
        if len(ref.shape) == 3:
            return ref.at[d0:d1, rows]
        w = ref.shape[1] // 4
        return ref.at[rows, d0 * w : d1 * w]

    class Fetch:
        def __init__(self, ref, slots, base):
            total = ref.shape[1] if len(ref.shape) == 3 else ref.shape[0]
            part = total // 8
            d0, d1 = slots
            sems = iter(range(base, base + 8))

            def go(src, dst, peer):
                k = next(sems)
                return remote(src, dst, wsend.at[k], wrecv.at[k], peer)

            own = eighth * part
            self.z = [
                go(weight_block(ref, own, part, 0, 1), weight_block(ref, own, part, d, d + 1), tp_peer(d))
                for d in range(d0, d1)
            ]
            mine = weight_block(ref, own, part, d0, d1)
            self.plane = [go(mine, mine, node_peer(2 * e)) for e in (1, 2, 3)]
            lot = weight_block(ref, c * (total // 2), total // 2, d0, d1)
            self.core = [go(lot, lot, node_peer(1))]

        def start_z(self):
            for cp in self.z:
                cp.start()

        def start_plane(self):
            for cp in self.z:
                cp.wait()
            for cp in self.plane:
                cp.start()

        def start_core(self):
            for cp in self.plane:
                cp.wait()
            self.core[0].start()

        def end(self):
            self.core[0].wait()

    fetch_in = [None] + [Fetch(w_in, (d, d + 1), 8 * (d - 1)) for d in (1, 2, 3)]
    fetch_od = Fetch(w_od, (1, 4), 24)
    fetch_up = Fetch(w_up, (1, 4), 32)

    for i in (0, 1, 2):
        local[i].wait()
    for d in (1, 2, 3):
        fetch_in[d].start_z()

    gain1 = tokens_of(g1_ref)
    shift1 = tokens_of(s1_ref)
    gain2 = tokens_of(g2_ref)
    shift2 = tokens_of(s2_ref)
    hopw = tokens_of(hw_ref)
    hop16 = jnp.broadcast_to(hopw, (16, width)).astype(BF16)

    eye = iota((TILE, TILE), 0) == iota((TILE, TILE), 1)
    ones = jnp.ones((TILE, TILE), BF16)
    lane8 = iota((HOPS, TILE), 1)
    block8 = lane8 // HOPS
    eye16 = eye.astype(F32).astype(BF16)
    emask[...] = (iota((TILE, TILE), 0) // HOPS == iota((TILE, TILE), 1) // HOPS).astype(F32).astype(BF16)
    first = (iota((2 * TILE, TILE), 0) < TILE) == (iota((2 * TILE, TILE), 1) < HEAD)
    pmask[...] = first.astype(F32).astype(BF16)
    nodes_chunk = CHUNK // HOPS
    spread_c = (iota((CHUNK, nodes_chunk), 0) // HOPS == iota((CHUNK, nodes_chunk), 1)).astype(F32).astype(BF16)

    def rows_of(i, size):
        return pl.ds(pl.multiple_of(i * size, size), size)

    mask_f = mask_ref[...].astype(F32)
    for i in range(tiles):
        col = mm(jnp.where(eye, mask_f[i : i + 1, :], 0.0).astype(BF16), ones)
        vcol[i * TILE : (i + 1) * TILE, :] = col
        acc = jnp.zeros((HOPS, TILE), F32)
        col3 = col.reshape(TILE // HOPS, HOPS, TILE)
        for r in range(TILE // HOPS):
            acc = jnp.where(block8 == r, col3[r], acc)
        mt[i] = acc
    gcol = mm(jnp.where(eye, gid_ref[...].astype(F32), 0.0).astype(BF16), ones).astype(BF16)
    for i in range(chunks):
        gexp[i * CHUNK : (i + 1) * CHUNK, :] = mm(spread_c, gcol[i * nodes_chunk : (i + 1) * nodes_chunk])

    local[3].wait()

    def norm_one(i, carry):
        x = tok[rows_of(i, CHUNK), :].astype(F32)
        hat, _ = centred(x)
        n1[rows_of(i, CHUNK), :] = (hat * gain1 + shift1).astype(BF16)
        return carry

    lax.fori_loop(0, chunks, norm_one, 0)

    def project(d):
        base = d * 3 * qw

        def step(i, carry):
            r = rows_of(i, CHUNK)
            out = mm(n1[r, :], w_in[:, base : base + 3 * qw])
            qkv[r, base : base + qw] = (out[:, 0:qw] * (HEAD**-0.5)).astype(BF16)
            qkv[r, base + qw : base + 3 * qw] = out[:, qw:].astype(BF16)
            return carry

        lax.fori_loop(0, chunks, step, 0)

    def pair(x):
        return jnp.concatenate([x, x], axis=0) * pmask[...]

    bits = [((lane8 // (HOPS << b)) % 2) == 1 for b in range(4)]

    def compact(x):
        out = []
        for h in range(2):
            x3 = x[:, h * TILE : (h + 1) * TILE].reshape(TILE // HOPS, HOPS, TILE)
            parts = [x3[r] for r in range(TILE // HOPS)]
            for b in range(4):
                parts = [jnp.where(bits[b], parts[2 * m + 1], parts[2 * m]) for m in range(len(parts) // 2)]
            out.append(parts[0])
        return out

    def expand(x):
        twice = jnp.concatenate([x, x], axis=0).astype(BF16)
        return jnp.concatenate([twice] * (TILE // 16), axis=0) * emask[...]

    together = 4

    def attend(d):
        base = d * 3 * qw

        def step(i, carry):
            at = [i * together + m for m in range(together)]
            rs = [rows_of(a, TILE) for a in at]
            q2 = [pair(qkv[r, base : base + qw]) for r in rs]
            scores = [compact(mm_rt(qkv[r, base + qw : base + 2 * qw], x)) for r, x in zip(rs, q2, strict=True)]
            wide = []
            for m, a in enumerate(at):
                keep = mt[a] > 0.5
                for h in range(2):
                    wide.append(jnp.where(keep, scores[m][h], NEGATIVE))
            peaks = [jnp.max(x, axis=0, keepdims=True) for x in wide]
            wide = [jnp.exp(x - y) for x, y in zip(wide, peaks, strict=True)]
            totals = [jnp.sum(x, axis=0, keepdims=True) for x in wide]
            wide = [x / y for x, y in zip(wide, totals, strict=True)]
            for m, a in enumerate(at):
                for h in range(2):
                    pn[a * 8 + 2 * d + h] = wide[2 * m + h]
            turned = [
                mm_rt(eye16, jnp.concatenate([expand(wide[2 * m]), expand(wide[2 * m + 1])], axis=0)).astype(BF16)
                for m in range(together)
            ]
            v2 = [pair(qkv[r, base + 2 * qw : base + 3 * qw]) for r in rs]
            for m, r in enumerate(rs):
                ctx[r, d * qw : (d + 1) * qw] = mm(turned[m], v2[m]).astype(BF16)
            return carry

        lax.fori_loop(0, tiles // together, step, 0)

    project(0)
    fetch_in[1].start_plane()
    attend(0)
    for i in (4, 5, 6, 7):
        local[i].wait()
    fetch_in[2].start_plane()
    fetch_in[3].start_plane()
    fetch_od.start_z()
    fetch_up.start_z()
    fetch_in[1].start_core()
    fetch_in[1].end()
    project(1)
    fetch_in[2].start_core()
    attend(1)
    fetch_in[2].end()
    fetch_in[3].start_core()
    fetch_od.start_plane()
    project(2)
    attend(2)
    fetch_in[3].end()
    fetch_up.start_plane()
    project(3)
    fetch_od.start_core()
    attend(3)
    fetch_od.end()
    fetch_up.start_core()
    fetch_up.end()

    ow = w_od.shape[1]
    down_rows = ow - qw

    def w_out():
        return w_od[:, 0:qw, :].reshape(4 * qw, width)

    def w_down():
        return w_od[:, qw:ow, :].reshape(4 * down_rows, width)

    hop3 = iota((nodes_chunk, HOPS, TILE), 1)
    lane3 = iota((nodes_chunk, HOPS, TILE), 2)
    node3 = iota((nodes_chunk, HOPS, TILE), 0)
    lane_graph = (lane3 % GRAPHS).astype(F32)

    def feed(i, acc):
        r = rows_of(i, CHUNK)
        attended = mm(ctx[r, :], w_out())
        x = tok[r, :].astype(F32) + attended
        res[r, :] = x
        hat, _ = centred(x)
        normed = (hat * gain2 + shift2).astype(BF16)
        n2[r, :] = normed
        value, slope = gelu_both(mm(normed, w_up[...]))
        value = value.astype(BF16)
        act[r, :] = value
        gp[r, :] = slope.astype(BF16)
        out = x + mm(value, w_down())
        lay[r, :] = out
        dr = mm(spread_c, cot[rows_of(i, nodes_chunk), :])
        logit = jnp.sum(out * hopw, axis=-1, keepdims=True)
        gcoef = jnp.sum(out * dr, axis=-1, keepdims=True)
        shape = (nodes_chunk, HOPS, TILE)
        valid = vcol[r, :].reshape(shape)
        valid = jnp.where(hop3 > 0, valid, 0.0)
        logit = jnp.where(valid > 0.5, jnp.broadcast_to(logit, (CHUNK, TILE)).reshape(shape), NEGATIVE)
        e = jnp.exp(logit - jnp.max(logit, axis=1, keepdims=True))
        e = jnp.where(hop3 > 0, e, 0.0)
        weight = e / jnp.sum(e, axis=1, keepdims=True)
        direct = valid * jnp.broadcast_to(gcoef, (CHUNK, TILE)).reshape(shape)
        wcol[r, :] = weight.reshape(CHUNK, TILE)
        dcol[r, :] = direct.reshape(CHUNK, TILE)
        mine = gexp[r, :].reshape(shape) == lane_graph
        both = jnp.where(lane3 < GRAPHS, jnp.where(hop3 == 0, 1.0, weight), -direct)
        return acc + jnp.sum(jnp.where(mine, both, 0.0), axis=0)

    sums = lax.fori_loop(0, chunks, feed, jnp.zeros((HOPS, TILE), F32))

    def reduce_all(value, one, by_nodes, by_tp, ssem, rsem, overlap=None):
        one[0] = value
        copies = [
            remote(one.at[0], by_nodes.at[k - 1], ssem.at[k - 1], rsem.at[k - 1], node_peer(k)) for k in range(1, 8)
        ]
        for cp in copies:
            cp.start()
        if overlap is not None:
            overlap()
        for cp in copies:
            cp.wait()
        value = one[0]
        for k in range(7):
            value = value + by_nodes[k]
        at = 7
        for b in extra:
            one[at - 6] = value
            cp = remote(one.at[at - 6], by_nodes.at[at], ssem.at[at], rsem.at[at], node_peer(1 << b))
            cp.start()
            cp.wait()
            value = value + by_nodes[at]
            at += 1
        last = one.shape[0] - 1
        one[last] = value
        copies = [
            remote(one.at[last], by_tp.at[k - 1], ssem.at[at + k - 1], rsem.at[at + k - 1], tp_peer(k))
            for k in range(1, 4)
        ]
        for cp in copies:
            cp.start()
        return copies, lambda: one[last] + by_tp[0] + by_tp[1] + by_tp[2]

    def small_products():
        drdown = mm_rt(cot[...], w_down()).astype(BF16)
        hopdown = mm_rt(hop16, w_down()).astype(BF16)
        for i in range(chunks):
            piece = drdown[i * nodes_chunk : (i + 1) * nodes_chunk]
            ab[i, 0:nodes_chunk] = piece
            ab[i, nodes_chunk : 2 * nodes_chunk] = piece
            ab[i, 2 * nodes_chunk : 2 * nodes_chunk + 16] = hopdown
            ab[i, 2 * nodes_chunk + 16 :] = jnp.zeros((TILE - 2 * nodes_chunk - 16, ab.shape[2]), BF16)

    copies, total = reduce_all(sums, ar_one, ar_nodes, ar_tp, asend, arecv, small_products)
    for cp in copies:
        cp.wait()
    sums = total()
    row = jnp.broadcast_to(sums[0:1, :], (HOPS, TILE))
    counts = jnp.where(lane8 < GRAPHS, row, pltpu.roll(row, GRAPHS, 1))
    means = (sums / (counts + 1.0))[None]

    def back_one(i, carry):
        gain_acc, shift_acc, hop_acc, zed_acc = carry
        r = rows_of(i, CHUNK)
        shape = (nodes_chunk, HOPS, TILE)
        picked = jnp.where(gexp[r, :].reshape(shape) == lane_graph, means, 0.0)
        mean_r = jnp.sum(jnp.where(lane3 < GRAPHS, picked, 0.0), axis=-1, keepdims=True)
        grad_mean = jnp.sum(jnp.where(lane3 < GRAPHS, 0.0, picked), axis=-1, keepdims=True)
        weight = wcol[r, :].reshape(shape)
        valid = vcol[r, :].reshape(shape)
        coef = jnp.where(hop3 > 0, valid * (weight - mean_r), 1.0)
        grad_w = dcol[r, :].reshape(shape) + grad_mean
        glog = weight * (grad_w - jnp.sum(weight * grad_w, axis=1, keepdims=True))
        coef_hi = coef.astype(BF16).astype(F32)
        glog_hi = glog.astype(BF16).astype(F32)
        zero = jnp.zeros_like(coef)
        mix = jnp.where(lane3 == node3, coef_hi, zero)
        mix = jnp.where(lane3 == node3 + nodes_chunk, coef - coef_hi, mix)
        mix = jnp.where(lane3 == 2 * nodes_chunk, glog_hi, mix)
        mix = jnp.where(lane3 == 2 * nodes_chunk + 1, glog - glog_hi, mix)
        mix = mix.reshape(CHUNK, TILE).astype(BF16)

        dr = cot[rows_of(i, nodes_chunk), :]
        rest = jnp.zeros((TILE - 2 * nodes_chunk - 16, width), BF16)
        dh = jnp.concatenate([dr, dr, hop16, rest], axis=0)
        grad_layer = mm(mix, dh)
        gl[r, :] = grad_layer
        before_back = (mm(mix, ab[i]) * gp[r, :].astype(F32)).astype(BF16)
        gbef[r, :] = before_back

        seen = mm_lt(mix, lay[r, :].astype(BF16))
        readout_ref[rows_of(i, nodes_chunk), :] = (seen[0:nodes_chunk] + seen[nodes_chunk : 2 * nodes_chunk]).astype(
            BF16
        )
        hop_acc = hop_acc + seen[2 * nodes_chunk : 2 * nodes_chunk + 8]
        fold = mm_lt(mix, act[r, :])
        zed[rows_of(i, nodes_chunk), :] = (fold[0:nodes_chunk] + fold[nodes_chunk : 2 * nodes_chunk]).astype(BF16)
        zed_acc = zed_acc + fold[2 * nodes_chunk : 2 * nodes_chunk + 8]

        dy = mm_rt(before_back, w_up[...])
        hat, inv = centred(res[r, :])
        gain_acc = gain_acc + jnp.sum((dy * hat).reshape(nodes_chunk, HOPS, width), axis=0)
        shift_acc = shift_acc + jnp.sum(dy.reshape(nodes_chunk, HOPS, width), axis=0)
        g = dy * gain2
        back = inv * (
            g - jnp.mean(g, axis=-1, keepdims=True) - hat * jnp.mean(g * hat, axis=-1, keepdims=True)
        )
        grad_res = grad_layer + back
        gl[r, :] = grad_res
        att = grad_res.astype(BF16)
        datt[r, :] = att
        dctx[r, :] = mm_rt(att, w_out()).astype(BF16)
        return gain_acc, shift_acc, hop_acc, zed_acc

    zero8 = jnp.zeros((HOPS, width), F32)
    gain_two, shift_two, hop_sum, zed_sum = lax.fori_loop(
        0, chunks, back_one, (zero8, zero8, zero8, jnp.zeros((HOPS, zed.shape[1]), F32))
    )

    def group(at, array, wide, cols, rc, rp, rz, final):
        return Group(array, wide, cols, rc, rp, rz, final, gsend, grecv, at * (11 + len(extra)))

    dn = group(0, g_dn, False, (0, 4), rc_dn, rp_dn, rz_dn, fin_dn_ref)
    up = group(1, g_up, True, (0, 4), rc_up, rp_up, rz_up, fin_up_ref)
    ot = group(2, g_out, False, (0, 4), rc_out, rp_out, rz_out, fin_out_ref)
    qk = [
        group(3 + d, g_in, True, (d, d + 1), rc_in.at[d], rp_in.at[d], rz_in, fin_in_ref) for d in range(4)
    ]

    def plane_of(e):
        out = plane
        for b in range(2):
            if (e >> b) & 1:
                out = out + (1 << b) * (1 - 2 * ((plane // (1 << b)) % 2))
        return out

    def core_copy(g):
        s, r = g.sems(0)
        return remote(g.block(g.rows(1 - c)), g.recv_core, s, r, node_peer(1))

    def plane_copies(g):
        return [
            remote(g.block(g.rows(c, plane_of(e))), g.recv_plane.at[e - 1], *g.sems(e), node_peer(2 * e))
            for e in (1, 2, 3)
        ]

    def z_copies(g, slots):
        return [
            remote(g.slot(g.rows(c, plane), d), g.recv_z.at[d - 1], *g.sems(3 + d), tp_peer(d)) for d in slots
        ]

    def final_copies(g):
        mine = g.final.at[g.rows(c, plane)]
        return [remote(mine, mine, *g.sems(6 + e), node_peer(2 * e)) for e in (1, 2, 3)]

    def last_copy(g):
        mine = g.final.at[g.rows(c)]
        return remote(mine, mine, *g.sems(10), node_peer(1))

    def go_core(g):
        core_copy(g).start()

    def go_plane(g):
        core_copy(g).wait()
        mine = g.block(g.rows(c))
        mine[...] = (mine[...].astype(F32) + g.recv_core[...].astype(F32)).astype(BF16)
        for cp in plane_copies(g):
            cp.start()

    def go_z(g, slots):
        for cp in plane_copies(g):
            cp.wait()
        mine = g.block(g.rows(c, plane))
        total = mine[...].astype(F32)
        for e in range(3):
            total = total + g.recv_plane[e].astype(F32)
        mine[...] = total.astype(BF16)
        for cp in z_copies(g, slots):
            cp.start()

    def go_final(g, waits):
        for cp in waits:
            cp.wait()
        total = g.slot(g.rows(c, plane), 0)[...].astype(F32)
        for d in range(3):
            total = total + g.recv_z[d].astype(F32)
        for j, b in enumerate(extra):
            g.recv_z[3 + 2 * j] = total.astype(BF16)
            cp = remote(g.recv_z.at[3 + 2 * j], g.recv_z.at[4 + 2 * j], *g.sems(11 + j), node_peer(1 << b))
            cp.start()
            cp.wait()
            total = total + g.recv_z[4 + 2 * j].astype(F32)
        g.final.at[g.rows(c, plane)][...] = total.astype(BF16)
        for cp in final_copies(g):
            cp.start()

    def go_last(g):
        for cp in final_copies(g):
            cp.wait()
        last_copy(g).start()

    def finish(g):
        last_copy(g).wait()

    every = (1, 2, 3)

    zed[rows_here // HOPS :, :] = jnp.concatenate([zed_sum, jnp.zeros_like(zed_sum)], axis=0).astype(BF16)
    drh = jnp.concatenate([cot[...], hop16], axis=0)
    g_dn[...] = mm_lt(zed[...], drh).astype(BF16).reshape(g_dn.shape)
    go_core(dn)
    g_up[...] = mm_lt(n2[...], gbef[...]).astype(BF16)
    go_core(up)
    go_plane(dn)
    g_out[...] = mm_lt(ctx[...], datt[...]).astype(BF16).reshape(g_out.shape)
    go_core(ot)
    go_plane(up)

    def attend_back(d):
        base = d * 3 * qw

        def step(i, carry):
            at = [i * together + m for m in range(together)]
            rs = [rows_of(a, TILE) for a in at]
            do2 = [pair(dctx[r, d * qw : (d + 1) * qw]) for r in rs]
            grads = [
                compact(mm_rt(qkv[r, base + 2 * qw : base + 3 * qw], x)) for r, x in zip(rs, do2, strict=True)
            ]
            probs = [[pn[a * 8 + 2 * d + h] for h in range(2)] for a in at]
            probs_wide = [jnp.concatenate([expand(p) for p in ps], axis=1) for ps in probs]
            for m, r in enumerate(rs):
                dqkv[r, base + 2 * qw : base + 3 * qw] = mm(probs_wide[m], do2[m]).astype(BF16)
            inner = [[jnp.sum(p * g, axis=0, keepdims=True) for p, g in zip(*x, strict=True)] for x in zip(probs, grads, strict=True)]
            back = [
                [expand(probs[m][h] * (grads[m][h] - inner[m][h])) for h in range(2)] for m in range(together)
            ]
            q2 = [pair(qkv[r, base : base + qw]) for r in rs]
            for m, r in enumerate(rs):
                wide = jnp.concatenate(back[m], axis=1)
                dqkv[r, base + qw : base + 2 * qw] = mm(wide, q2[m]).astype(BF16)
            turned = [mm_rt(eye16, jnp.concatenate(x, axis=0)).astype(BF16) for x in back]
            k2 = [pair(qkv[r, base + qw : base + 2 * qw]) for r in rs]
            for m, r in enumerate(rs):
                dqkv[r, base : base + qw] = (mm(turned[m], k2[m]) * (HEAD**-0.5)).astype(BF16)
            return carry

        lax.fori_loop(0, tiles // together, step, 0)
        g_in[:, base : base + 3 * qw] = mm_lt(n1[...], dqkv[:, base : base + 3 * qw]).astype(BF16)
        go_core(qk[d])

    attend_back(3)
    go_plane(ot)
    go_z(dn, every)
    attend_back(2)
    go_plane(qk[3])
    go_z(up, every)
    go_z(ot, every)
    attend_back(1)
    go_plane(qk[2])
    go_z(qk[3], (3,))
    go_final(dn, z_copies(dn, every))
    attend_back(0)

    def back_two(i, carry):
        gain_acc, shift_acc = carry
        r = rows_of(i, CHUNK)
        dy = mm_rt(dqkv[r, :], w_in[...])
        hat, inv = centred(tok[r, :].astype(F32))
        gain_acc = gain_acc + jnp.sum((dy * hat).reshape(nodes_chunk, HOPS, width), axis=0)
        shift_acc = shift_acc + jnp.sum(dy.reshape(nodes_chunk, HOPS, width), axis=0)
        g = dy * gain1
        back = inv * (
            g - jnp.mean(g, axis=-1, keepdims=True) - hat * jnp.mean(g * hat, axis=-1, keepdims=True)
        )
        gtok_ref[r, :] = (gl[r, :] + back).astype(BF16)
        return gain_acc, shift_acc

    go_plane(qk[1])
    go_z(qk[2], (2,))
    go_final(up, z_copies(up, every))
    go_plane(qk[0])
    norm_sums = lax.fori_loop(0, chunks // 2, back_two, (zero8, zero8))
    go_z(qk[1], (1,))
    go_final(ot, z_copies(ot, every))
    go_last(dn)
    gain_one, shift_one = lax.fori_loop(chunks // 2, chunks, back_two, norm_sums)

    def fold8(x):
        return jnp.sum(x, axis=0, keepdims=True)

    small = jnp.concatenate(
        [fold8(gain_one), fold8(shift_one), fold8(gain_two), fold8(shift_two), fold8(hop_sum[0:2]), zero8[0:3]], axis=0
    )

    def rest_of():
        go_z(qk[0], ())
        go_final(qk[0], [z_copies(qk[d], (d,))[0] for d in every])

    copies, total_small = reduce_all(small, sv_one, sv_nodes, sv_tp, bsend, brecv, rest_of)
    go_last(up)
    go_last(ot)
    for cp in copies:
        cp.wait()
    small_ref[...] = total_small()
    go_last(qk[0])
    finish(dn)
    finish(up)
    finish(ot)
    finish(qk[0])


def results_kernel(readout, gtok, small, fin_in, fin_out, fin_up, fin_dn, o_read, o_tok, o_g1, o_s1, o_q, o_k, o_v, o_out, o_g2, o_s2, o_up, o_dn, o_hop):
    o_tok[...] = gtok[...]
    o_read[...] = readout[...]
    width = small.shape[1]
    for i, o in enumerate((o_g1, o_s1, o_g2, o_s2, o_hop)):
        o[...] = small[i : i + 1, :].reshape(width)
    qw = o_q.shape[1]
    for i, o in enumerate((o_q, o_k, o_v)):
        o[...] = fin_in[:, i * qw : (i + 1) * qw].astype(F32)
    o_out[...] = fin_out[...].astype(F32)
    o_up[...] = fin_up[...].astype(F32)
    o_dn[...] = fin_dn[...].astype(F32)


def shards(
    nn,
    tokens,
    hop_mask,
    graph_ids,
    norm1_gain,
    norm1_shift,
    w_query,
    w_key,
    w_value,
    w_out,
    norm2_gain,
    norm2_shift,
    w_up,
    w_down,
    hop_weight,
    cotangent,
):
    rows, width = tokens.shape
    nodes = rows // HOPS
    qw, uw = w_query.shape[1], w_up.shape[1]
    vm = pl.BlockSpec(memory_space=pltpu.VMEM)
    hbm = pl.BlockSpec(memory_space=pl.ANY)
    extra = len([b for b in range(3, 12) if (1 << b) < nn])

    def v(*shape, dtype=BF16):
        return pltpu.VMEM(shape, dtype)

    tiles, chunks = rows // TILE, rows // CHUNK
    half = width // 2
    scratch = [
        v(width, 12 * qw),
        v(width, 4 * uw),
        v(4, qw + uw, width),
        v(rows, width),
        v(nodes, width),
        v(rows, width),
        v(rows, 12 * qw),
        v(tiles * 8, HOPS, TILE, dtype=F32),
        v(rows, width),
        v(rows, width, dtype=F32),
        v(rows, width),
        v(rows, 4 * uw),
        v(rows, 4 * uw),
        v(rows, width, dtype=F32),
        v(TILE, TILE),
        v(2 * TILE, TILE),
        v(rows, TILE, dtype=F32),
        v(tiles, HOPS, TILE, dtype=F32),
        v(rows, TILE, dtype=F32),
        v(rows, TILE, dtype=F32),
        v(rows, TILE, dtype=F32),
        v(chunks, TILE, 4 * uw),
        v(nodes + 16, 4 * uw),
        v(rows, 4 * uw),
        v(rows, width, dtype=F32),
        v(rows, width),
        v(rows, width),
        v(rows, 12 * qw),
        v(width, 4 * uw),
        v(4, uw, width),
        v(4, qw, width),
        v(width, 12 * qw),
        v(half, 4 * uw),
        v(4, uw // 2, width),
        v(4, qw // 2, width),
        v(4, half, 3 * qw),
        v(3, half // 4, 4 * uw),
        v(3, 4, uw // 8, width),
        v(3, 4, qw // 8, width),
        v(4, 3, half // 4, 3 * qw),
        v(3 + 2 * extra, half // 4, uw),
        v(3 + 2 * extra, uw // 8, width),
        v(3 + 2 * extra, qw // 8, width),
        v(3 + 2 * extra, half // 4, 3 * qw),
        v(2 + extra, HOPS, TILE, dtype=F32),
        v(7 + extra, HOPS, TILE, dtype=F32),
        v(3, HOPS, TILE, dtype=F32),
        v(2 + extra, 8, width, dtype=F32),
        v(7 + extra, 8, width, dtype=F32),
        v(3, 8, width, dtype=F32),
        pltpu.SemaphoreType.DMA((8,)),
        pltpu.SemaphoreType.DMA((40,)),
        pltpu.SemaphoreType.DMA((40,)),
        pltpu.SemaphoreType.DMA((7 * (11 + extra),)),
        pltpu.SemaphoreType.DMA((7 * (11 + extra),)),
        pltpu.SemaphoreType.DMA((10 + extra,)),
        pltpu.SemaphoreType.DMA((10 + extra,)),
        pltpu.SemaphoreType.DMA((10 + extra,)),
        pltpu.SemaphoreType.DMA((10 + extra,)),
    ]
    outs = [
        jax.ShapeDtypeStruct((nodes, width), BF16),
        jax.ShapeDtypeStruct((rows, width), BF16),
        jax.ShapeDtypeStruct((8, width), F32),
        jax.ShapeDtypeStruct((width, 3 * qw), BF16),
        jax.ShapeDtypeStruct((qw, width), BF16),
        jax.ShapeDtypeStruct((width, uw), BF16),
        jax.ShapeDtypeStruct((uw, width), BF16),
    ]
    readout, gtok, small, fin_in, fin_out, fin_up, fin_dn = pl.pallas_call(
        functools.partial(kernel, nn),
        out_shape=outs,
        in_specs=[hbm, vm, vm, vm, vm, hbm, hbm, hbm, hbm, vm, vm, hbm, hbm, vm, hbm],
        out_specs=[vm] * 7,
        scratch_shapes=scratch,
        compiler_params=pltpu.CompilerParams(
            collective_id=0, has_side_effects=True, vmem_limit_bytes=60 * 1024 * 1024
        ),
        name="layer",
    )(
        tokens,
        hop_mask.reshape(tiles, TILE),
        graph_ids.reshape(1, nodes),
        norm1_gain,
        norm1_shift,
        w_query,
        w_key,
        w_value,
        w_out,
        norm2_gain,
        norm2_shift,
        w_up,
        w_down,
        hop_weight,
        cotangent,
    )
    line = jax.ShapeDtypeStruct((width,), F32)
    square = jax.ShapeDtypeStruct((width, qw), F32)
    return pl.pallas_call(
        results_kernel,
        out_shape=[
            jax.ShapeDtypeStruct((nodes, width), BF16),
            jax.ShapeDtypeStruct((rows, width), BF16),
            line,
            line,
            square,
            square,
            square,
            jax.ShapeDtypeStruct((qw, width), F32),
            line,
            line,
            jax.ShapeDtypeStruct((width, uw), F32),
            jax.ShapeDtypeStruct((uw, width), F32),
            line,
        ],
        in_specs=[vm] * 7,
        out_specs=[vm] * 13,
        name="results",
    )(readout, gtok, small, fin_in, fin_out, fin_up, fin_dn)


def solution(mesh):
    spread = P(("nodes", "tp"), None)
    flat = P(("nodes", "tp"))
    cols, rows = P(None, "tp"), P("tp", None)
    return jax.shard_map(
        functools.partial(shards, mesh.shape["nodes"]),
        mesh=mesh,
        in_specs=(spread, flat, flat, P(), P(), cols, cols, cols, rows, P(), P(), cols, rows, P(), spread),
        out_specs=(spread, spread, P(), P(), cols, cols, cols, rows, P(), P(), cols, rows, P()),
        check_vma=False,
    )
```

```python
import functools

import jax
import jax.numpy as jnp
from jax import lax
from jax.experimental import pallas as pl
from jax.experimental.pallas import tpu as pltpu
from jax.sharding import PartitionSpec as P

HOPS = 8
HEAD = 64
GRAPHS = 64
EPSILON = 1e-05
NEGATIVE = -1000000000.0
MESH = pl.DeviceIdType.MESH
F32 = jnp.float32
BF16 = jnp.bfloat16
CHUNK = 256
TILE = 128


def mm(a, b):
    return lax.dot_general(a, b, (((1,), (0,)), ((), ())), preferred_element_type=F32)


def mm_rt(a, b):
    return lax.dot_general(a, b, (((1,), (1,)), ((), ())), preferred_element_type=F32)


def mm_lt(a, b):
    return lax.dot_general(a, b, (((0,), (0,)), ((), ())), preferred_element_type=F32)


def iota(shape, axis):
    return lax.broadcasted_iota(jnp.int32, shape, axis)


def centred(values):
    centre = values - jnp.mean(values, axis=-1, keepdims=True)
    spread = jnp.mean(centre * centre, axis=-1, keepdims=True)
    return centre * lax.rsqrt(spread + EPSILON), lax.rsqrt(spread + EPSILON)


def gelu_both(x):
    size = jnp.abs(x)
    t = 1.0 / (1.0 + (0.3275911 * 0.7071067811865476) * size)
    bell = jnp.exp(-0.5 * (x * x))
    poly = 1.061405429 * t - 1.453152027
    poly = poly * t + 1.421413741
    poly = poly * t - 0.284496736
    poly = poly * t + 0.254829592
    tail = (0.5 * t) * poly * bell
    phi = jnp.where(x >= 0, 1.0 - tail, tail)
    return x * phi, phi + x * (bell * 0.3989422804014327)


def tokens_of(ref):
    return ref[...].astype(F32).reshape(1, ref.shape[0])


class Group:
    def __init__(self, array, wide, cols, recv_core, recv_plane, recv_z, final, more, send, recv, base):
        self.array, self.wide = array, wide
        self.cols = cols
        self.recv_core, self.recv_plane, self.recv_z = recv_core, recv_plane, recv_z
        self.final = final
        self.more = more
        self.send, self.recv, self.base = send, recv, base
        rows = final.shape[0]
        self.half_rows = rows // 2
        self.piece_rows = rows // 8
        self.width = final.shape[1]

    def sems(self, k):
        return self.send.at[self.base + k], self.recv.at[self.base + k]

    def rows(self, c, p=None):
        if p is None:
            return pl.ds(pl.multiple_of(c * self.half_rows, 16), self.half_rows)
        return pl.ds(pl.multiple_of(c * self.half_rows + p * self.piece_rows, 16), self.piece_rows)

    def block(self, rows):
        if self.wide:
            return self.array.at[rows, self.cols[0] * self.width : self.cols[1] * self.width]
        return self.array.at[:, rows]

    def slot(self, rows, d):
        if self.wide:
            return self.array.at[rows, d * self.width : (d + 1) * self.width]
        return self.array.at[d, rows]


def kernel(
    nn,
    tok_hbm,
    mask_ref,
    gid_ref,
    g1_ref,
    s1_ref,
    wq_hbm,
    wk_hbm,
    wv_hbm,
    wo_hbm,
    g2_ref,
    s2_ref,
    wu_hbm,
    wd_hbm,
    hw_ref,
    cot_hbm,
    readout_ref,
    gtok_ref,
    small_ref,
    fin_in_ref,
    fin_out_ref,
    fin_up_ref,
    fin_dn_ref,
    w_in,
    w_up,
    w_ot,
    w_dn,
    tok,
    cot,
    n1,
    qkv,
    pn,
    ctx,
    res,
    n2,
    act,
    gp,
    lay,
    emask,
    pmask,
    vcol,
    mt,
    gexp,
    wcol,
    dcol,
    ab,
    zed,
    gbef,
    gl,
    datt,
    dctx,
    dqkv,
    g_up,
    g_dn,
    g_out,
    g_in,
    rc_up,
    rc_dn,
    rc_out,
    rc_in,
    rp_up,
    rp_dn,
    rp_out,
    rp_in,
    rz_up,
    rz_dn,
    rz_out,
    rz_in,
    mo_up,
    mo_dn,
    mo_out,
    mo_in,
    ar_one,
    ar_nodes,
    ar_tp,
    sv_one,
    sv_nodes,
    sv_tp,
    lsem,
    wsend,
    wrecv,
    gsend,
    grecv,
    asend,
    arecv,
    bsend,
    brecv,
):
    n, t = lax.axis_index("nodes"), lax.axis_index("tp")
    rows_here, width = tok.shape
    chunks = rows_here // CHUNK
    tiles = rows_here // TILE
    c = n % 2
    plane = (n // 2) % 4
    eighth = 4 * c + plane
    side = (plane % 2 + plane // 2) % 2
    extra = [b for b in range(3, 12) if (1 << b) < nn]

    def node_peer(k):
        out = n
        for b in range(12):
            if (k >> b) & 1:
                bit = (n // (1 << b)) % 2
                out = out + (1 << b) * (1 - 2 * bit)
        return (out, t)

    def tp_peer(k):
        out = t
        for b in range(2):
            if (k >> b) & 1:
                bit = (t // (1 << b)) % 2
                out = out + (1 << b) * (1 - 2 * bit)
        return (n, out)

    def remote(src, dst, ssem, rsem, peer):
        return pltpu.make_async_remote_copy(
            src_ref=src, dst_ref=dst, send_sem=ssem, recv_sem=rsem, device_id=peer, device_id_type=MESH
        )

    qw = wq_hbm.shape[1]
    local = [
        pltpu.make_async_copy(wq_hbm, w_in.at[:, 0:qw], lsem.at[0]),
        pltpu.make_async_copy(wk_hbm, w_in.at[:, qw : 2 * qw], lsem.at[1]),
        pltpu.make_async_copy(wv_hbm, w_in.at[:, 2 * qw : 3 * qw], lsem.at[2]),
        pltpu.make_async_copy(tok_hbm, tok, lsem.at[3]),
        pltpu.make_async_copy(wo_hbm, w_ot.at[0], lsem.at[4]),
        pltpu.make_async_copy(wd_hbm, w_dn.at[0], lsem.at[5]),
        pltpu.make_async_copy(wu_hbm, w_up.at[:, 0 : wu_hbm.shape[1]], lsem.at[6]),
        pltpu.make_async_copy(cot_hbm, cot, lsem.at[7]),
    ]
    for copy in local:
        copy.start()

    barrier = pltpu.get_barrier_semaphore()
    greet = [node_peer(k) for k in range(1, 8)] + [node_peer(1 << b) for b in extra]
    greet += [tp_peer(k) for k in range(1, 4)]
    for peer in greet:
        pl.semaphore_signal(barrier, inc=1, device_id=peer, device_id_type=MESH)
    pl.semaphore_wait(barrier, len(greet))

    def weight_block(ref, off, size, d0, d1):
        rows = pl.ds(pl.multiple_of(off, 16), size)
        if len(ref.shape) == 3:
            return ref.at[d0:d1, rows]
        w = ref.shape[1] // 4
        return ref.at[rows, d0 * w : d1 * w]

    class Fetch:
        def __init__(self, ref, slots, base, halves=False):
            total = ref.shape[1] if len(ref.shape) == 3 else ref.shape[0]
            d0, d1 = slots
            sems = iter(range(base, base + 8))

            def go(src, dst, peer):
                k = next(sems)
                return remote(src, dst, wsend.at[k], wrecv.at[k], peer)

            def rows(off, size):
                return weight_block(ref, off, size, d0, d1)

            part = total // 4 if halves else total // 8
            own = (2 * side + c if halves else eighth) * part
            self.z = [
                go(weight_block(ref, own, part, 0, 1), weight_block(ref, own, part, d, d + 1), tp_peer(d))
                for d in range(d0, d1)
            ]
            if halves:
                some = [rows(own + e * (part // 2), part // 2) for e in range(2)]
                self.plane = [go(x, x, node_peer(2 << e)) for e, x in enumerate(some)]
                lots = [rows(own, part), rows((2 * (1 - side) + c) * part, part)]
            else:
                self.plane = [go(rows(own, part), rows(own, part), node_peer(2 * e)) for e in (1, 2, 3)]
                lots = [rows(c * (total // 2), total // 2)]
            self.core = [go(x, x, node_peer(1)) for x in lots]

        def start_z(self):
            for cp in self.z:
                cp.start()

        def start_plane(self):
            for cp in self.z:
                cp.wait()
            for cp in self.plane:
                cp.start()

        def start_core(self):
            for cp in self.plane:
                cp.wait()
            for cp in self.core:
                cp.start()

        def end(self):
            for cp in self.core:
                cp.wait()

    fetch_in = [None] + [Fetch(w_in, (d, d + 1), 8 * (d - 1)) for d in (1, 2, 3)]
    fetch_ot = Fetch(w_ot, (1, 4), 24)
    fetch_up = Fetch(w_up, (1, 4), 32, halves=True)
    fetch_dn = Fetch(w_dn, (1, 4), 40)

    for i in (0, 1, 2):
        local[i].wait()
    for d in (1, 2, 3):
        fetch_in[d].start_z()

    gain1 = tokens_of(g1_ref)
    shift1 = tokens_of(s1_ref)
    gain2 = tokens_of(g2_ref)
    shift2 = tokens_of(s2_ref)
    hopw = tokens_of(hw_ref)
    hop16 = jnp.broadcast_to(hopw, (16, width)).astype(BF16)

    eye = iota((TILE, TILE), 0) == iota((TILE, TILE), 1)
    ones = jnp.ones((TILE, TILE), BF16)
    lane8 = iota((HOPS, TILE), 1)
    block8 = lane8 // HOPS
    eye16 = eye.astype(F32).astype(BF16)
    emask[...] = (iota((TILE, TILE), 0) // HOPS == iota((TILE, TILE), 1) // HOPS).astype(F32).astype(BF16)
    first = (iota((2 * TILE, TILE), 0) < TILE) == (iota((2 * TILE, TILE), 1) < HEAD)
    pmask[...] = first.astype(F32).astype(BF16)
    nodes_chunk = CHUNK // HOPS
    spread_c = (iota((CHUNK, nodes_chunk), 0) // HOPS == iota((CHUNK, nodes_chunk), 1)).astype(F32).astype(BF16)

    def rows_of(i, size):
        return pl.ds(pl.multiple_of(i * size, size), size)

    mask_f = mask_ref[...].astype(F32)
    for i in range(tiles):
        col = mm(jnp.where(eye, mask_f[i : i + 1, :], 0.0).astype(BF16), ones)
        vcol[i * TILE : (i + 1) * TILE, :] = col
        acc = jnp.zeros((HOPS, TILE), F32)
        col3 = col.reshape(TILE // HOPS, HOPS, TILE)
        for r in range(TILE // HOPS):
            acc = jnp.where(block8 == r, col3[r], acc)
        mt[i] = acc
    gcol = mm(jnp.where(eye, gid_ref[...].astype(F32), 0.0).astype(BF16), ones).astype(BF16)
    for i in range(chunks):
        gexp[i * CHUNK : (i + 1) * CHUNK, :] = mm(spread_c, gcol[i * nodes_chunk : (i + 1) * nodes_chunk])

    local[3].wait()

    def norm_one(i, carry):
        x = tok[rows_of(i, CHUNK), :].astype(F32)
        hat, _ = centred(x)
        n1[rows_of(i, CHUNK), :] = (hat * gain1 + shift1).astype(BF16)
        return carry

    lax.fori_loop(0, chunks, norm_one, 0)

    def project(d):
        base = d * 3 * qw

        def step(i, carry):
            r = rows_of(i, CHUNK)
            out = mm(n1[r, :], w_in[:, base : base + 3 * qw])
            qkv[r, base : base + qw] = (out[:, 0:qw] * (HEAD**-0.5)).astype(BF16)
            qkv[r, base + qw : base + 3 * qw] = out[:, qw:].astype(BF16)
            return carry

        lax.fori_loop(0, chunks, step, 0)

    def pair(x):
        return jnp.concatenate([x, x], axis=0) * pmask[...]

    bits = [((lane8 // (HOPS << b)) % 2) == 1 for b in range(4)]

    def compact(x):
        out = []
        for h in range(2):
            x3 = x[:, h * TILE : (h + 1) * TILE].reshape(TILE // HOPS, HOPS, TILE)
            parts = [x3[r] for r in range(TILE // HOPS)]
            for b in range(4):
                parts = [jnp.where(bits[b], parts[2 * m + 1], parts[2 * m]) for m in range(len(parts) // 2)]
            out.append(parts[0])
        return out

    def expand(x):
        twice = jnp.concatenate([x, x], axis=0).astype(BF16)
        return jnp.concatenate([twice] * (TILE // 16), axis=0) * emask[...]

    together = 4

    steps = tiles // together
    mid = steps // 2

    def attend(d, lo, hi):
        base = d * 3 * qw

        def step(i, carry):
            at = [i * together + m for m in range(together)]
            rs = [rows_of(a, TILE) for a in at]
            q2 = [pair(qkv[r, base : base + qw]) for r in rs]
            scores = [compact(mm_rt(qkv[r, base + qw : base + 2 * qw], x)) for r, x in zip(rs, q2, strict=True)]
            wide = []
            for m, a in enumerate(at):
                keep = mt[a] > 0.5
                for h in range(2):
                    wide.append(jnp.where(keep, scores[m][h], NEGATIVE))
            peaks = [jnp.max(x, axis=0, keepdims=True) for x in wide]
            wide = [jnp.exp(x - y) for x, y in zip(wide, peaks, strict=True)]
            totals = [jnp.sum(x, axis=0, keepdims=True) for x in wide]
            wide = [x / y for x, y in zip(wide, totals, strict=True)]
            for m, a in enumerate(at):
                for h in range(2):
                    pn[a * 8 + 2 * d + h] = wide[2 * m + h]
            turned = [
                mm_rt(eye16, jnp.concatenate([expand(wide[2 * m]), expand(wide[2 * m + 1])], axis=0)).astype(BF16)
                for m in range(together)
            ]
            v2 = [pair(qkv[r, base + 2 * qw : base + 3 * qw]) for r in rs]
            for m, r in enumerate(rs):
                ctx[r, d * qw : (d + 1) * qw] = mm(turned[m], v2[m]).astype(BF16)
            return carry

        lax.fori_loop(lo, hi, step, 0)

    fetch_in[1].start_plane()
    for i in (4, 5, 6, 7):
        local[i].wait()
    fetch_ot.start_z()
    project(0)
    fetch_in[2].start_plane()
    attend(0, 0, mid)
    fetch_in[3].start_plane()
    fetch_up.start_z()
    attend(0, mid, steps)
    fetch_in[1].start_core()
    fetch_ot.start_plane()
    fetch_in[1].end()
    project(1)
    fetch_in[2].start_core()
    attend(1, 0, mid)
    fetch_in[3].start_core()
    fetch_dn.start_z()
    fetch_in[2].end()
    attend(1, mid, steps)
    project(2)
    fetch_ot.start_core()
    attend(2, 0, mid)
    fetch_up.start_plane()
    attend(2, mid, steps)
    fetch_in[3].end()
    project(3)
    attend(3, 0, mid)
    fetch_dn.start_plane()
    attend(3, mid, steps)
    fetch_ot.end()
    fetch_up.start_core()
    fetch_up.end()

    def w_out():
        return w_ot[...].reshape(4 * qw, width)

    def w_down():
        return w_dn[...].reshape(4 * w_dn.shape[1], width)

    hop3 = iota((nodes_chunk, HOPS, TILE), 1)
    lane3 = iota((nodes_chunk, HOPS, TILE), 2)
    node3 = iota((nodes_chunk, HOPS, TILE), 0)
    lane_graph = (lane3 % GRAPHS).astype(F32)

    def feed_up(i, carry):
        r = rows_of(i, CHUNK)
        attended = mm(ctx[r, :], w_out())
        x = tok[r, :].astype(F32) + attended
        res[r, :] = x
        hat, _ = centred(x)
        normed = (hat * gain2 + shift2).astype(BF16)
        n2[r, :] = normed
        value, slope = gelu_both(mm(normed, w_up[...]))
        value = value.astype(BF16)
        act[r, :] = value
        gp[r, :] = slope.astype(BF16)
        return carry

    def feed_down(i, acc):
        r = rows_of(i, CHUNK)
        out = res[r, :] + mm(act[r, :], w_down())
        lay[r, :] = out
        dr = mm(spread_c, cot[rows_of(i, nodes_chunk), :])
        logit = jnp.sum(out * hopw, axis=-1, keepdims=True)
        gcoef = jnp.sum(out * dr, axis=-1, keepdims=True)
        shape = (nodes_chunk, HOPS, TILE)
        valid = vcol[r, :].reshape(shape)
        valid = jnp.where(hop3 > 0, valid, 0.0)
        logit = jnp.where(valid > 0.5, jnp.broadcast_to(logit, (CHUNK, TILE)).reshape(shape), NEGATIVE)
        e = jnp.exp(logit - jnp.max(logit, axis=1, keepdims=True))
        e = jnp.where(hop3 > 0, e, 0.0)
        weight = e / jnp.sum(e, axis=1, keepdims=True)
        direct = valid * jnp.broadcast_to(gcoef, (CHUNK, TILE)).reshape(shape)
        wcol[r, :] = weight.reshape(CHUNK, TILE)
        dcol[r, :] = direct.reshape(CHUNK, TILE)
        mine = gexp[r, :].reshape(shape) == lane_graph
        both = jnp.where(lane3 < GRAPHS, jnp.where(hop3 == 0, 1.0, weight), -direct)
        return acc + jnp.sum(jnp.where(mine, both, 0.0), axis=0)

    lax.fori_loop(0, chunks // 2, feed_up, 0)
    fetch_dn.start_core()
    lax.fori_loop(chunks // 2, chunks, feed_up, 0)
    fetch_dn.end()
    sums = lax.fori_loop(0, chunks, feed_down, jnp.zeros((HOPS, TILE), F32))

    def reduce_all(value, one, by_nodes, by_tp, ssem, rsem, overlap=None):
        one[0] = value
        copies = [
            remote(one.at[0], by_nodes.at[k - 1], ssem.at[k - 1], rsem.at[k - 1], node_peer(k)) for k in range(1, 8)
        ]
        for cp in copies:
            cp.start()
        if overlap is not None:
            overlap()
        for cp in copies:
            cp.wait()
        value = one[0]
        for k in range(7):
            value = value + by_nodes[k]
        at = 7
        for b in extra:
            one[at - 6] = value
            cp = remote(one.at[at - 6], by_nodes.at[at], ssem.at[at], rsem.at[at], node_peer(1 << b))
            cp.start()
            cp.wait()
            value = value + by_nodes[at]
            at += 1
        last = one.shape[0] - 1
        one[last] = value
        copies = [
            remote(one.at[last], by_tp.at[k - 1], ssem.at[at + k - 1], rsem.at[at + k - 1], tp_peer(k))
            for k in range(1, 4)
        ]
        for cp in copies:
            cp.start()
        return copies, lambda: one[last] + by_tp[0] + by_tp[1] + by_tp[2]

    def small_products():
        drdown = mm_rt(cot[...], w_down()).astype(BF16)
        hopdown = mm_rt(hop16, w_down()).astype(BF16)
        for i in range(chunks):
            piece = drdown[i * nodes_chunk : (i + 1) * nodes_chunk]
            ab[i, 0:nodes_chunk] = piece
            ab[i, nodes_chunk : 2 * nodes_chunk] = piece
            ab[i, 2 * nodes_chunk : 2 * nodes_chunk + 16] = hopdown
            ab[i, 2 * nodes_chunk + 16 :] = jnp.zeros((TILE - 2 * nodes_chunk - 16, ab.shape[2]), BF16)

    copies, total = reduce_all(sums, ar_one, ar_nodes, ar_tp, asend, arecv, small_products)
    for cp in copies:
        cp.wait()
    sums = total()
    row = jnp.broadcast_to(sums[0:1, :], (HOPS, TILE))
    counts = jnp.where(lane8 < GRAPHS, row, pltpu.roll(row, GRAPHS, 1))
    means = (sums / (counts + 1.0))[None]

    def back_one(i, carry):
        gain_acc, shift_acc, hop_acc, zed_acc = carry
        r = rows_of(i, CHUNK)
        shape = (nodes_chunk, HOPS, TILE)
        picked = jnp.where(gexp[r, :].reshape(shape) == lane_graph, means, 0.0)
        mean_r = jnp.sum(jnp.where(lane3 < GRAPHS, picked, 0.0), axis=-1, keepdims=True)
        grad_mean = jnp.sum(jnp.where(lane3 < GRAPHS, 0.0, picked), axis=-1, keepdims=True)
        weight = wcol[r, :].reshape(shape)
        valid = vcol[r, :].reshape(shape)
        coef = jnp.where(hop3 > 0, valid * (weight - mean_r), 1.0)
        grad_w = dcol[r, :].reshape(shape) + grad_mean
        glog = weight * (grad_w - jnp.sum(weight * grad_w, axis=1, keepdims=True))
        coef_hi = coef.astype(BF16).astype(F32)
        glog_hi = glog.astype(BF16).astype(F32)
        zero = jnp.zeros_like(coef)
        mix = jnp.where(lane3 == node3, coef_hi, zero)
        mix = jnp.where(lane3 == node3 + nodes_chunk, coef - coef_hi, mix)
        mix = jnp.where(lane3 == 2 * nodes_chunk, glog_hi, mix)
        mix = jnp.where(lane3 == 2 * nodes_chunk + 1, glog - glog_hi, mix)
        mix = mix.reshape(CHUNK, TILE).astype(BF16)

        dr = cot[rows_of(i, nodes_chunk), :]
        rest = jnp.zeros((TILE - 2 * nodes_chunk - 16, width), BF16)
        dh = jnp.concatenate([dr, dr, hop16, rest], axis=0)
        grad_layer = mm(mix, dh)
        gl[r, :] = grad_layer
        before_back = (mm(mix, ab[i]) * gp[r, :].astype(F32)).astype(BF16)
        gbef[r, :] = before_back

        seen = mm_lt(mix, lay[r, :].astype(BF16))
        readout_ref[rows_of(i, nodes_chunk), :] = (seen[0:nodes_chunk] + seen[nodes_chunk : 2 * nodes_chunk]).astype(
            BF16
        )
        hop_acc = hop_acc + seen[2 * nodes_chunk : 2 * nodes_chunk + 8]
        fold = mm_lt(mix, act[r, :])
        zed[rows_of(i, nodes_chunk), :] = (fold[0:nodes_chunk] + fold[nodes_chunk : 2 * nodes_chunk]).astype(BF16)
        zed_acc = zed_acc + fold[2 * nodes_chunk : 2 * nodes_chunk + 8]

        dy = mm_rt(before_back, w_up[...])
        hat, inv = centred(res[r, :])
        gain_acc = gain_acc + jnp.sum((dy * hat).reshape(nodes_chunk, HOPS, width), axis=0)
        shift_acc = shift_acc + jnp.sum(dy.reshape(nodes_chunk, HOPS, width), axis=0)
        g = dy * gain2
        back = inv * (
            g - jnp.mean(g, axis=-1, keepdims=True) - hat * jnp.mean(g * hat, axis=-1, keepdims=True)
        )
        grad_res = grad_layer + back
        gl[r, :] = grad_res
        att = grad_res.astype(BF16)
        datt[r, :] = att
        dctx[r, :] = mm_rt(att, w_out()).astype(BF16)
        return gain_acc, shift_acc, hop_acc, zed_acc

    zero8 = jnp.zeros((HOPS, width), F32)
    gain_two, shift_two, hop_sum, zed_sum = lax.fori_loop(
        0, chunks, back_one, (zero8, zero8, zero8, jnp.zeros((HOPS, zed.shape[1]), F32))
    )

    def group(at, array, wide, cols, rc, rp, rz, final, more):
        return Group(array, wide, cols, rc, rp, rz, final, more, gsend, grecv, at * (15 + len(extra)))

    dn = group(0, g_dn, False, (0, 4), rc_dn, rp_dn, rz_dn, fin_dn_ref, mo_dn)
    up = group(1, g_up, True, (0, 4), rc_up, rp_up, rz_up, fin_up_ref, mo_up)
    ot = group(2, g_out, False, (0, 4), rc_out, rp_out, rz_out, fin_out_ref, mo_out)
    qk = [
        group(3 + d, g_in, True, (d, d + 1), rc_in.at[d], rp_in.at[d], rz_in, fin_in_ref, mo_in) for d in range(4)
    ]
    every = (1, 2, 3)

    def plane_of(e):
        out = plane
        for b in range(2):
            if (e >> b) & 1:
                out = out + (1 << b) * (1 - 2 * ((plane // (1 << b)) % 2))
        return out

    def core_copy(g):
        s, r = g.sems(0)
        return remote(g.block(g.rows(1 - c)), g.recv_core, s, r, node_peer(1))

    def go_core(g):
        core_copy(g).start()

    def add_core(g):
        core_copy(g).wait()
        mine = g.block(g.rows(c))
        mine[...] = (mine[...].astype(F32) + g.recv_core[...].astype(F32)).astype(BF16)

    def plane_copies(g):
        return [
            remote(g.block(g.rows(c, plane_of(e))), g.recv_plane.at[e - 1], *g.sems(e), node_peer(2 * e))
            for e in (1, 2, 3)
        ]

    def go_plane(g):
        add_core(g)
        for cp in plane_copies(g):
            cp.start()

    def cut(g, rows, e):
        w = (g.cols[1] - g.cols[0]) * g.width // 2
        base = g.cols[0] * g.width + e * w
        return g.array.at[rows, base : base + w]

    def fold_copies(g):
        w = (g.cols[1] - g.cols[0]) * g.width // 2
        out = []
        for e in range(2):
            away = plane_of(1 << e)
            for m, far in enumerate((away, plane_of(3))):
                dst = g.recv_plane.at[m, :, e * w : (e + 1) * w]
                out.append(remote(cut(g, g.rows(c, far), e), dst, *g.sems(11 + 2 * e + m), node_peer(2 << e)))
        return out

    def go_fold(g):
        add_core(g)
        for cp in fold_copies(g):
            cp.start()

    def fold_last(g):
        w = (g.cols[1] - g.cols[0]) * g.width // 2
        out = []
        for e in range(2):
            dst = g.recv_plane.at[2, :, e * w : (e + 1) * w]
            far = plane_of(2 >> e)
            out.append(remote(cut(g, g.rows(c, far), e), dst, *g.sems(1 + e), node_peer(4 >> e)))
        return out

    def go_fold_last(g):
        for cp in fold_copies(g):
            cp.wait()
        w = (g.cols[1] - g.cols[0]) * g.width // 2
        for e in range(2):
            for m, keep in enumerate((plane, plane_of(2 >> e))):
                mine = cut(g, g.rows(c, keep), e)
                got = g.recv_plane[m, :, e * w : (e + 1) * w]
                mine[...] = (mine[...].astype(F32) + got.astype(F32)).astype(BF16)
        for cp in fold_last(g):
            cp.start()

    def go_z_fold(g, slots):
        for cp in fold_last(g):
            cp.wait()
        mine = g.block(g.rows(c, plane))
        mine[...] = (mine[...].astype(F32) + g.recv_plane[2].astype(F32)).astype(BF16)
        for cp in z_copies(g, slots):
            cp.start()

    def z_copies(g, slots):
        return [
            remote(g.slot(g.rows(c, plane), d), g.recv_z.at[d - 1], *g.sems(3 + d), tp_peer(d)) for d in slots
        ]

    def go_z(g, slots):
        for cp in plane_copies(g):
            cp.wait()
        mine = g.block(g.rows(c, plane))
        total = mine[...].astype(F32)
        for e in range(3):
            total = total + g.recv_plane[e].astype(F32)
        mine[...] = total.astype(BF16)
        for cp in z_copies(g, slots):
            cp.start()

    def z_first(g):
        return [remote(g.slot(g.rows(c), d), g.recv_z.at[d - 1], *g.sems(3 + d), tp_peer(d)) for d in every]

    def go_z_first(g):
        add_core(g)
        for cp in z_first(g):
            cp.start()

    def own_pieces(g):
        return [
            remote(g.slot(g.rows(c, plane_of(e)), 0), g.recv_plane.at[e - 1], *g.sems(e), node_peer(2 * e))
            for e in (1, 2, 3)
        ]

    def go_own_plane(g):
        for cp in z_first(g):
            cp.wait()
        mine = g.slot(g.rows(c), 0)
        total = mine[...].astype(F32)
        for d in range(3):
            total = total + g.recv_z[d].astype(F32)
        mine[...] = total.astype(BF16)
        for cp in own_pieces(g):
            cp.start()

    def go_own_final(g):
        for cp in own_pieces(g):
            cp.wait()
        total = g.slot(g.rows(c, plane), 0)[...].astype(F32)
        for e in range(3):
            total = total + g.recv_plane[e].astype(F32)
        share(g, total)

    def final_copies(g):
        mine = g.final.at[g.rows(c, plane)]
        return [remote(mine, mine, *g.sems(6 + e), node_peer(2 * e)) for e in (1, 2, 3)]

    def last_copy(g):
        mine = g.final.at[g.rows(c)]
        return remote(mine, mine, *g.sems(10), node_peer(1))

    def go_final(g, waits):
        for cp in waits:
            cp.wait()
        total = g.slot(g.rows(c, plane), 0)[...].astype(F32)
        for d in range(3):
            total = total + g.recv_z[d].astype(F32)
        share(g, total)

    def share(g, total):
        for j, b in enumerate(extra):
            g.more[2 * j] = total.astype(BF16)
            cp = remote(g.more.at[2 * j], g.more.at[2 * j + 1], *g.sems(15 + j), node_peer(1 << b))
            cp.start()
            cp.wait()
            total = total + g.more[2 * j + 1].astype(F32)
        g.final.at[g.rows(c, plane)][...] = total.astype(BF16)
        for cp in final_copies(g):
            cp.start()

    def go_last(g):
        for cp in final_copies(g):
            cp.wait()
        last_copy(g).start()

    def finish(g):
        last_copy(g).wait()

    zed[rows_here // HOPS :, :] = jnp.concatenate([zed_sum, jnp.zeros_like(zed_sum)], axis=0).astype(BF16)
    drh = jnp.concatenate([cot[...], hop16], axis=0)
    g_dn[...] = mm_lt(zed[...], drh).astype(BF16).reshape(g_dn.shape)
    go_core(dn)
    g_up[...] = mm_lt(n2[...], gbef[...]).astype(BF16)
    go_core(up)
    go_z_first(dn)
    g_out[...] = mm_lt(ctx[...], datt[...]).astype(BF16).reshape(g_out.shape)
    go_core(ot)
    go_fold(up)

    def attend_back(d):
        base = d * 3 * qw

        def step(i, carry):
            at = [i * together + m for m in range(together)]
            rs = [rows_of(a, TILE) for a in at]
            do2 = [pair(dctx[r, d * qw : (d + 1) * qw]) for r in rs]
            grads = [
                compact(mm_rt(qkv[r, base + 2 * qw : base + 3 * qw], x)) for r, x in zip(rs, do2, strict=True)
            ]
            probs = [[pn[a * 8 + 2 * d + h] for h in range(2)] for a in at]
            probs_wide = [jnp.concatenate([expand(p) for p in ps], axis=1) for ps in probs]
            for m, r in enumerate(rs):
                dqkv[r, base + 2 * qw : base + 3 * qw] = mm(probs_wide[m], do2[m]).astype(BF16)
            inner = [[jnp.sum(p * g, axis=0, keepdims=True) for p, g in zip(*x, strict=True)] for x in zip(probs, grads, strict=True)]
            back = [
                [expand(probs[m][h] * (grads[m][h] - inner[m][h])) for h in range(2)] for m in range(together)
            ]
            q2 = [pair(qkv[r, base : base + qw]) for r in rs]
            for m, r in enumerate(rs):
                wide = jnp.concatenate(back[m], axis=1)
                dqkv[r, base + qw : base + 2 * qw] = mm(wide, q2[m]).astype(BF16)
            turned = [mm_rt(eye16, jnp.concatenate(x, axis=0)).astype(BF16) for x in back]
            k2 = [pair(qkv[r, base + qw : base + 2 * qw]) for r in rs]
            for m, r in enumerate(rs):
                dqkv[r, base : base + qw] = (mm(turned[m], k2[m]) * (HEAD**-0.5)).astype(BF16)
            return carry

        lax.fori_loop(0, tiles // together, step, 0)
        g_in[:, base : base + 3 * qw] = mm_lt(n1[...], dqkv[:, base : base + 3 * qw]).astype(BF16)
        go_core(qk[d])

    def back_two(i, carry):
        gain_acc, shift_acc = carry
        r = rows_of(i, CHUNK)
        dy = mm_rt(dqkv[r, :], w_in[...])
        hat, inv = centred(tok[r, :].astype(F32))
        gain_acc = gain_acc + jnp.sum((dy * hat).reshape(nodes_chunk, HOPS, width), axis=0)
        shift_acc = shift_acc + jnp.sum(dy.reshape(nodes_chunk, HOPS, width), axis=0)
        g = dy * gain1
        back = inv * (
            g - jnp.mean(g, axis=-1, keepdims=True) - hat * jnp.mean(g * hat, axis=-1, keepdims=True)
        )
        gtok_ref[r, :] = (gl[r, :] + back).astype(BF16)
        return gain_acc, shift_acc

    attend_back(3)
    go_plane(ot)
    attend_back(2)
    go_fold_last(up)
    go_plane(qk[3])
    attend_back(1)
    go_plane(qk[2])
    go_z_fold(up, every)
    attend_back(0)
    go_plane(qk[1])
    go_z(ot, every)
    go_own_plane(dn)
    go_z(qk[3], (3,))
    quarter = chunks // 4
    norm_sums = lax.fori_loop(0, quarter, back_two, (zero8, zero8))
    go_plane(qk[0])
    go_z(qk[2], (2,))
    norm_sums = lax.fori_loop(quarter, 2 * quarter, back_two, norm_sums)
    go_z(qk[1], (1,))
    go_final(up, z_copies(up, every))
    go_own_final(dn)
    go_final(ot, z_copies(ot, every))
    gain_one, shift_one = lax.fori_loop(2 * quarter, chunks, back_two, norm_sums)

    def fold8(x):
        return jnp.sum(x, axis=0, keepdims=True)

    small = jnp.concatenate(
        [fold8(gain_one), fold8(shift_one), fold8(gain_two), fold8(shift_two), fold8(hop_sum[0:2]), zero8[0:3]], axis=0
    )

    def rest_of():
        go_z(qk[0], ())
        go_final(qk[0], [z_copies(qk[d], (d,))[0] for d in every])

    copies, total_small = reduce_all(small, sv_one, sv_nodes, sv_tp, bsend, brecv, rest_of)
    go_last(up)
    go_last(dn)
    go_last(ot)
    go_last(qk[0])
    for cp in copies:
        cp.wait()
    small_ref[...] = total_small()
    finish(dn)
    finish(up)
    finish(ot)
    finish(qk[0])


def results_kernel(readout, gtok, small, fin_in, fin_out, fin_up, fin_dn, *rest):
    o_read, o_tok, o_g1, o_s1, o_q, o_k, o_v, o_out, o_g2, o_s2, o_up, o_dn, o_hop = rest[:13]
    v_q, v_k, v_v, v_out, v_up, v_dn, sems = rest[13:]
    moves = []

    def send(src, dst):
        moves.append(pltpu.make_async_copy(src, dst, sems.at[len(moves)]))
        moves[-1].start()

    send(gtok, o_tok)
    send(readout, o_read)
    v_up[...] = fin_up[...].astype(F32)
    send(v_up, o_up)
    v_dn[...] = fin_dn[...].astype(F32)
    send(v_dn, o_dn)
    qw = o_q.shape[1]
    for i, (x, o) in enumerate(((v_q, o_q), (v_k, o_k), (v_v, o_v))):
        x[...] = fin_in[:, i * qw : (i + 1) * qw].astype(F32)
        send(x, o)
    v_out[...] = fin_out[...].astype(F32)
    send(v_out, o_out)
    width = small.shape[1]
    for i, o in enumerate((o_g1, o_s1, o_g2, o_s2, o_hop)):
        o[...] = small[i : i + 1, :].reshape(width)
    for cp in moves:
        cp.wait()


def shards(
    nn,
    tokens,
    hop_mask,
    graph_ids,
    norm1_gain,
    norm1_shift,
    w_query,
    w_key,
    w_value,
    w_out,
    norm2_gain,
    norm2_shift,
    w_up,
    w_down,
    hop_weight,
    cotangent,
):
    rows, width = tokens.shape
    nodes = rows // HOPS
    qw, uw = w_query.shape[1], w_up.shape[1]
    vm = pl.BlockSpec(memory_space=pltpu.VMEM)
    hbm = pl.BlockSpec(memory_space=pl.ANY)
    extra = len([b for b in range(3, 12) if (1 << b) < nn])

    def v(*shape, dtype=BF16):
        return pltpu.VMEM(shape, dtype)

    tiles, chunks = rows // TILE, rows // CHUNK
    half = width // 2
    more = max(2 * extra, 1)
    scratch = [
        v(width, 12 * qw),
        v(width, 4 * uw),
        v(4, qw, width),
        v(4, uw, width),
        v(rows, width),
        v(nodes, width),
        v(rows, width),
        v(rows, 12 * qw),
        v(tiles * 8, HOPS, TILE, dtype=F32),
        v(rows, width),
        v(rows, width, dtype=F32),
        v(rows, width),
        v(rows, 4 * uw),
        v(rows, 4 * uw),
        v(rows, width, dtype=F32),
        v(TILE, TILE),
        v(2 * TILE, TILE),
        v(rows, TILE, dtype=F32),
        v(tiles, HOPS, TILE, dtype=F32),
        v(rows, TILE, dtype=F32),
        v(rows, TILE, dtype=F32),
        v(rows, TILE, dtype=F32),
        v(chunks, TILE, 4 * uw),
        v(nodes + 16, 4 * uw),
        v(rows, 4 * uw),
        v(rows, width, dtype=F32),
        v(rows, width),
        v(rows, width),
        v(rows, 12 * qw),
        v(width, 4 * uw),
        v(4, uw, width),
        v(4, qw, width),
        v(width, 12 * qw),
        v(half, 4 * uw),
        v(4, uw // 2, width),
        v(4, qw // 2, width),
        v(4, half, 3 * qw),
        v(3, half // 4, 4 * uw),
        v(3, uw // 8, width),
        v(3, 4, qw // 8, width),
        v(4, 3, half // 4, 3 * qw),
        v(3, half // 4, uw),
        v(3, uw // 2, width),
        v(3, qw // 8, width),
        v(3, half // 4, 3 * qw),
        v(more, half // 4, uw),
        v(more, uw // 8, width),
        v(more, qw // 8, width),
        v(more, half // 4, 3 * qw),
        v(2 + extra, HOPS, TILE, dtype=F32),
        v(7 + extra, HOPS, TILE, dtype=F32),
        v(3, HOPS, TILE, dtype=F32),
        v(2 + extra, 8, width, dtype=F32),
        v(7 + extra, 8, width, dtype=F32),
        v(3, 8, width, dtype=F32),
        pltpu.SemaphoreType.DMA((8,)),
        pltpu.SemaphoreType.DMA((48,)),
        pltpu.SemaphoreType.DMA((48,)),
        pltpu.SemaphoreType.DMA((7 * (15 + extra),)),
        pltpu.SemaphoreType.DMA((7 * (15 + extra),)),
        pltpu.SemaphoreType.DMA((10 + extra,)),
        pltpu.SemaphoreType.DMA((10 + extra,)),
        pltpu.SemaphoreType.DMA((10 + extra,)),
        pltpu.SemaphoreType.DMA((10 + extra,)),
    ]
    outs = [
        pltpu.VMEM((nodes, width), BF16),
        pltpu.VMEM((rows, width), BF16),
        pltpu.VMEM((8, width), F32),
        pltpu.VMEM((width, 3 * qw), BF16),
        pltpu.VMEM((qw, width), BF16),
        pltpu.VMEM((width, uw), BF16),
        pltpu.VMEM((uw, width), BF16),
    ]
    readout, gtok, small, fin_in, fin_out, fin_up, fin_dn = pl.pallas_call(
        functools.partial(kernel, nn),
        out_shape=outs,
        in_specs=[hbm, vm, vm, vm, vm, hbm, hbm, hbm, hbm, vm, vm, hbm, hbm, vm, hbm],
        out_specs=[vm] * 7,
        scratch_shapes=scratch,
        compiler_params=pltpu.CompilerParams(
            collective_id=0, has_side_effects=True, vmem_limit_bytes=52 * 1024 * 1024
        ),
        name="layer",
    )(
        tokens,
        hop_mask.reshape(tiles, TILE),
        graph_ids.reshape(1, nodes),
        norm1_gain,
        norm1_shift,
        w_query,
        w_key,
        w_value,
        w_out,
        norm2_gain,
        norm2_shift,
        w_up,
        w_down,
        hop_weight,
        cotangent,
    )
    line = jax.ShapeDtypeStruct((width,), F32)
    square = jax.ShapeDtypeStruct((width, qw), F32)
    return pl.pallas_call(
        results_kernel,
        out_shape=[
            jax.ShapeDtypeStruct((nodes, width), BF16),
            jax.ShapeDtypeStruct((rows, width), BF16),
            line,
            line,
            square,
            square,
            square,
            jax.ShapeDtypeStruct((qw, width), F32),
            line,
            line,
            jax.ShapeDtypeStruct((width, uw), F32),
            jax.ShapeDtypeStruct((uw, width), F32),
            line,
        ],
        in_specs=[vm] * 7,
        out_specs=[hbm, hbm, vm, vm, hbm, hbm, hbm, hbm, vm, vm, hbm, hbm, vm],
        scratch_shapes=[v(width, qw, dtype=F32)] * 3
        + [
            v(qw, width, dtype=F32),
            v(width, uw, dtype=F32),
            v(uw, width, dtype=F32),
            pltpu.SemaphoreType.DMA((8,)),
        ],
        compiler_params=pltpu.CompilerParams(vmem_limit_bytes=16 * 1024 * 1024),
        name="results",
    )(readout, gtok, small, fin_in, fin_out, fin_up, fin_dn)


def solution(mesh):
    spread = P(("nodes", "tp"), None)
    flat = P(("nodes", "tp"))
    cols, rows = P(None, "tp"), P("tp", None)
    return jax.shard_map(
        functools.partial(shards, mesh.shape["nodes"]),
        mesh=mesh,
        in_specs=(spread, flat, flat, P(), P(), cols, cols, cols, rows, P(), P(), cols, rows, P(), spread),
        out_specs=(spread, spread, P(), P(), cols, cols, cols, rows, P(), P(), cols, rows, P()),
        check_vma=False,
    )
```

```python
import functools

import jax
import jax.numpy as jnp
from jax import lax
from jax.experimental import pallas as pl
from jax.experimental.pallas import tpu as pltpu
from jax.sharding import PartitionSpec as P

HOPS = 8
HEAD = 64
GRAPHS = 64
EPSILON = 1e-05
NEGATIVE = -1000000000.0
MESH = pl.DeviceIdType.MESH
F32 = jnp.float32
BF16 = jnp.bfloat16
CHUNK = 256
TILE = 128


def mm(a, b):
    return lax.dot_general(a, b, (((1,), (0,)), ((), ())), preferred_element_type=F32)


def mm_rt(a, b):
    return lax.dot_general(a, b, (((1,), (1,)), ((), ())), preferred_element_type=F32)


def mm_lt(a, b):
    return lax.dot_general(a, b, (((0,), (0,)), ((), ())), preferred_element_type=F32)


def iota(shape, axis):
    return lax.broadcasted_iota(jnp.int32, shape, axis)


def centred(values):
    centre = values - jnp.mean(values, axis=-1, keepdims=True)
    spread = jnp.mean(centre * centre, axis=-1, keepdims=True)
    return centre * lax.rsqrt(spread + EPSILON), lax.rsqrt(spread + EPSILON)


def gelu_both(x):
    size = jnp.abs(x)
    t = 1.0 / (1.0 + (0.3275911 * 0.7071067811865476) * size)
    bell = jnp.exp(-0.5 * (x * x))
    poly = 1.061405429 * t - 1.453152027
    poly = poly * t + 1.421413741
    poly = poly * t - 0.284496736
    poly = poly * t + 0.254829592
    tail = (0.5 * t) * poly * bell
    phi = jnp.where(x >= 0, 1.0 - tail, tail)
    return x * phi, phi + x * (bell * 0.3989422804014327)


def tokens_of(ref):
    return ref[...].astype(F32).reshape(1, ref.shape[0])


class Group:
    def __init__(self, array, wide, cols, recv_core, recv_plane, recv_z, final, more, send, recv, base):
        self.array, self.wide = array, wide
        self.cols = cols
        self.recv_core, self.recv_plane, self.recv_z = recv_core, recv_plane, recv_z
        self.final = final
        self.more = more
        self.send, self.recv, self.base = send, recv, base
        rows = final.shape[0]
        self.half_rows = rows // 2
        self.piece_rows = rows // 8
        self.width = final.shape[1]

    def sems(self, k):
        return self.send.at[self.base + k], self.recv.at[self.base + k]

    def rows(self, c, p=None):
        if p is None:
            return pl.ds(pl.multiple_of(c * self.half_rows, 16), self.half_rows)
        return pl.ds(pl.multiple_of(c * self.half_rows + p * self.piece_rows, 16), self.piece_rows)

    def block(self, rows):
        if self.wide:
            return self.array.at[rows, self.cols[0] * self.width : self.cols[1] * self.width]
        return self.array.at[:, rows]

    def slot(self, rows, d):
        if self.wide:
            return self.array.at[rows, d * self.width : (d + 1) * self.width]
        return self.array.at[d, rows]


def kernel(
    nn,
    tok_hbm,
    mask_ref,
    gid_ref,
    g1_ref,
    s1_ref,
    wq_hbm,
    wk_hbm,
    wv_hbm,
    wo_hbm,
    g2_ref,
    s2_ref,
    wu_hbm,
    wd_hbm,
    hw_ref,
    cot_hbm,
    readout_ref,
    gtok_ref,
    small_ref,
    fin_in_ref,
    fin_out_ref,
    fin_up_ref,
    fin_dn_ref,
    mask_v,
    gid_v,
    g1_v,
    s1_v,
    g2_v,
    s2_v,
    hw_v,
    w_in,
    w_up,
    w_ot,
    w_dn,
    tok,
    cot,
    n1,
    qkv,
    pn,
    ctx,
    res,
    n2,
    act,
    gp,
    lay,
    emask,
    pmask,
    n1t,
    n2t,
    ctxt,
    vcol,
    mt,
    gexp,
    wcol,
    dcol,
    ab,
    zed,
    gbef,
    gl,
    datt,
    dctx,
    dqkv,
    g_up,
    g_dn,
    g_out,
    g_in,
    rc_up,
    rc_dn,
    rc_out,
    rc_in,
    rp_up,
    rp_dn,
    rp_out,
    rp_in,
    rz_up,
    rz_dn,
    rz_out,
    rz_in,
    mo_up,
    mo_dn,
    mo_out,
    mo_in,
    ar_one,
    ar_nodes,
    ar_tp,
    sv_one,
    sv_nodes,
    sv_tp,
    lsem,
    wsend,
    wrecv,
    gsend,
    grecv,
    asend,
    arecv,
    bsend,
    brecv,
):
    n, t = lax.axis_index("nodes"), lax.axis_index("tp")
    rows_here, width = tok.shape
    chunks = rows_here // CHUNK
    tiles = rows_here // TILE
    c = n % 2
    plane = (n // 2) % 4
    eighth = 4 * c + plane
    side = (plane % 2 + plane // 2) % 2
    extra = [b for b in range(3, 12) if (1 << b) < nn]

    def node_peer(k):
        out = n
        for b in range(12):
            if (k >> b) & 1:
                bit = (n // (1 << b)) % 2
                out = out + (1 << b) * (1 - 2 * bit)
        return (out, t)

    def tp_peer(k):
        out = t
        for b in range(2):
            if (k >> b) & 1:
                bit = (t // (1 << b)) % 2
                out = out + (1 << b) * (1 - 2 * bit)
        return (n, out)

    def remote(src, dst, ssem, rsem, peer):
        return pltpu.make_async_remote_copy(
            src_ref=src, dst_ref=dst, send_sem=ssem, recv_sem=rsem, device_id=peer, device_id_type=MESH
        )

    qw = wq_hbm.shape[1]
    local = [
        pltpu.make_async_copy(wq_hbm, w_in.at[:, 0:qw], lsem.at[0]),
        pltpu.make_async_copy(wk_hbm, w_in.at[:, qw : 2 * qw], lsem.at[1]),
        pltpu.make_async_copy(wv_hbm, w_in.at[:, 2 * qw : 3 * qw], lsem.at[2]),
        pltpu.make_async_copy(tok_hbm, tok, lsem.at[3]),
        pltpu.make_async_copy(wo_hbm, w_ot.at[0], lsem.at[4]),
        pltpu.make_async_copy(wd_hbm, w_dn.at[0], lsem.at[5]),
        pltpu.make_async_copy(wu_hbm, w_up.at[:, 0 : wu_hbm.shape[1]], lsem.at[6]),
        pltpu.make_async_copy(cot_hbm, cot, lsem.at[7]),
    ]
    tiny = ((mask_ref, mask_v), (gid_ref, gid_v), (g1_ref, g1_v), (s1_ref, s1_v), (g2_ref, g2_v), (s2_ref, s2_v))
    for i, (src, dst) in enumerate(tiny + ((hw_ref, hw_v),)):
        local.append(pltpu.make_async_copy(src, dst, lsem.at[8 + i]))
    for copy in local:
        copy.start()

    barrier = pltpu.get_barrier_semaphore()
    greet = [node_peer(k) for k in range(1, 8)] + [node_peer(1 << b) for b in extra]
    greet += [tp_peer(k) for k in range(1, 4)]
    for peer in greet:
        pl.semaphore_signal(barrier, inc=1, device_id=peer, device_id_type=MESH)
    pl.semaphore_wait(barrier, len(greet))

    def weight_block(ref, off, size, d0, d1):
        rows = pl.ds(pl.multiple_of(off, 16), size)
        if len(ref.shape) == 3:
            return ref.at[d0:d1, rows]
        w = ref.shape[1] // 4
        return ref.at[rows, d0 * w : d1 * w]

    class Fetch:
        def __init__(self, ref, slots, base, halves=False):
            total = ref.shape[1] if len(ref.shape) == 3 else ref.shape[0]
            d0, d1 = slots
            sems = iter(range(base, base + 8))

            def go(src, dst, peer):
                k = next(sems)
                return remote(src, dst, wsend.at[k], wrecv.at[k], peer)

            def rows(off, size):
                return weight_block(ref, off, size, d0, d1)

            part = total // 4 if halves else total // 8
            own = (2 * side + c if halves else eighth) * part
            self.z = [
                go(weight_block(ref, own, part, 0, 1), weight_block(ref, own, part, d, d + 1), tp_peer(d))
                for d in range(d0, d1)
            ]
            if halves:
                some = [rows(own + e * (part // 2), part // 2) for e in range(2)]
                self.plane = [go(x, x, node_peer(2 << e)) for e, x in enumerate(some)]
                lots = [rows(own, part), rows((2 * (1 - side) + c) * part, part)]
            else:
                self.plane = [go(rows(own, part), rows(own, part), node_peer(2 * e)) for e in (1, 2, 3)]
                lots = [rows(c * (total // 2), total // 2)]
            self.core = [go(x, x, node_peer(1)) for x in lots]

        def start_z(self):
            for cp in self.z:
                cp.start()

        def start_plane(self):
            for cp in self.z:
                cp.wait()
            for cp in self.plane:
                cp.start()

        def start_core(self):
            for cp in self.plane:
                cp.wait()
            for cp in self.core:
                cp.start()

        def end(self):
            for cp in self.core:
                cp.wait()

    fetch_in = [None] + [Fetch(w_in, (d, d + 1), 8 * (d - 1)) for d in (1, 2, 3)]
    fetch_ot = Fetch(w_ot, (1, 4), 24)
    fetch_up = Fetch(w_up, (1, 4), 32)
    fetch_dn = Fetch(w_dn, (1, 4), 40)

    for i in (0, 1, 2):
        local[i].wait()
    for d in (1, 2, 3):
        fetch_in[d].start_z()

    for i in range(8, 15):
        local[i].wait()
    gain1 = tokens_of(g1_v)
    shift1 = tokens_of(s1_v)
    gain2 = tokens_of(g2_v)
    shift2 = tokens_of(s2_v)
    hopw = tokens_of(hw_v)
    hop16 = jnp.broadcast_to(hopw, (16, width)).astype(BF16)

    eye = iota((TILE, TILE), 0) == iota((TILE, TILE), 1)
    ones = jnp.ones((TILE, TILE), BF16)
    lane8 = iota((HOPS, TILE), 1)
    block8 = lane8 // HOPS
    eye16 = eye.astype(F32).astype(BF16)
    emask[...] = (iota((TILE, TILE), 0) // HOPS == iota((TILE, TILE), 1) // HOPS).astype(F32).astype(BF16)
    first = (iota((2 * TILE, TILE), 0) < TILE) == (iota((2 * TILE, TILE), 1) < HEAD)
    pmask[...] = first.astype(F32).astype(BF16)
    nodes_chunk = CHUNK // HOPS
    spread_c = (iota((CHUNK, nodes_chunk), 0) // HOPS == iota((CHUNK, nodes_chunk), 1)).astype(F32).astype(BF16)

    def rows_of(i, size):
        return pl.ds(pl.multiple_of(i * size, size), size)

    mask_f = mask_v[...].astype(F32)
    for i in range(tiles):
        col = mm(jnp.where(eye, mask_f[i : i + 1, :], 0.0).astype(BF16), ones)
        vcol[i * TILE : (i + 1) * TILE, :] = col
        acc = jnp.zeros((HOPS, TILE), F32)
        col3 = col.reshape(TILE // HOPS, HOPS, TILE)
        for r in range(TILE // HOPS):
            acc = jnp.where(block8 == r, col3[r], acc)
        mt[i] = acc

    local[3].wait()

    def norm_one(i, carry):
        x = tok[rows_of(i, CHUNK), :].astype(F32)
        hat, _ = centred(x)
        n1[rows_of(i, CHUNK), :] = (hat * gain1 + shift1).astype(BF16)
        return carry

    lax.fori_loop(0, chunks, norm_one, 0)

    def project(d, lo, hi):
        base = d * 3 * qw

        def step(i, carry):
            r = rows_of(i, CHUNK)
            out = mm(n1[r, :], w_in[:, base : base + 3 * qw])
            qkv[r, base : base + qw] = (out[:, 0:qw] * (HEAD**-0.5)).astype(BF16)
            qkv[r, base + qw : base + 3 * qw] = out[:, qw:].astype(BF16)
            return carry

        lax.fori_loop(lo, hi, step, 0)

    def pair(x):
        return jnp.concatenate([x, x], axis=0) * pmask[...]

    bits = [((lane8 // (HOPS << b)) % 2) == 1 for b in range(4)]

    def compact(x):
        out = []
        for h in range(2):
            x3 = x[:, h * TILE : (h + 1) * TILE].reshape(TILE // HOPS, HOPS, TILE)
            parts = [x3[r] for r in range(TILE // HOPS)]
            for b in range(4):
                parts = [jnp.where(bits[b], parts[2 * m + 1], parts[2 * m]) for m in range(len(parts) // 2)]
            out.append(parts[0])
        return out

    def expand(x):
        twice = jnp.concatenate([x, x], axis=0).astype(BF16)
        return jnp.concatenate([twice] * (TILE // 16), axis=0) * emask[...]

    together = 4

    steps = tiles // together
    mid = steps // 2

    def attend(d, lo, hi):
        base = d * 3 * qw

        def step(i, carry):
            at = [i * together + m for m in range(together)]
            rs = [rows_of(a, TILE) for a in at]
            q2 = [pair(qkv[r, base : base + qw]) for r in rs]
            scores = [compact(mm_rt(qkv[r, base + qw : base + 2 * qw], x)) for r, x in zip(rs, q2, strict=True)]
            wide = []
            for m, a in enumerate(at):
                keep = mt[a] > 0.5
                for h in range(2):
                    wide.append(jnp.where(keep, scores[m][h], NEGATIVE))
            peaks = [jnp.max(x, axis=0, keepdims=True) for x in wide]
            wide = [jnp.exp(x - y) for x, y in zip(wide, peaks, strict=True)]
            totals = [jnp.sum(x, axis=0, keepdims=True) for x in wide]
            wide = [x / y for x, y in zip(wide, totals, strict=True)]
            for m, a in enumerate(at):
                for h in range(2):
                    pn[a * 8 + 2 * d + h] = wide[2 * m + h]
            turned = [
                mm_rt(eye16, jnp.concatenate([expand(wide[2 * m]), expand(wide[2 * m + 1])], axis=0)).astype(BF16)
                for m in range(together)
            ]
            v2 = [pair(qkv[r, base + 2 * qw : base + 3 * qw]) for r in rs]
            for m, r in enumerate(rs):
                ctx[r, d * qw : (d + 1) * qw] = mm(turned[m], v2[m]).astype(BF16)
            return carry

        lax.fori_loop(lo, hi, step, 0)

    gcol = mm(jnp.where(eye, gid_v[...].astype(F32), 0.0).astype(BF16), ones).astype(BF16)
    for i in range(chunks):
        gexp[i * CHUNK : (i + 1) * CHUNK, :] = mm(spread_c, gcol[i * nodes_chunk : (i + 1) * nodes_chunk])
    cmid = chunks // 2
    fetch_in[1].start_plane()
    project(0, 0, cmid)
    fetch_in[2].start_plane()
    project(0, cmid, chunks)
    fetch_in[3].start_plane()
    for i in (4, 5, 6, 7):
        local[i].wait()
    fetch_ot.start_z()
    fetch_up.start_z()
    fetch_dn.start_z()
    attend(0, 0, mid)
    fetch_ot.start_plane()
    fetch_in[1].start_core()
    attend(0, mid, steps)
    fetch_in[1].end()
    fetch_in[2].start_core()
    project(1, 0, cmid)
    fetch_up.start_plane()
    project(1, cmid, chunks)
    attend(1, 0, mid)
    fetch_in[3].start_core()
    attend(1, mid, steps)
    fetch_in[2].end()
    project(2, 0, cmid)
    fetch_dn.start_plane()
    project(2, cmid, chunks)
    attend(2, 0, mid)
    fetch_ot.start_core()
    attend(2, mid, steps)
    fetch_in[3].end()
    project(3, 0, chunks)
    attend(3, 0, mid)
    attend(3, mid, steps)
    fetch_ot.end()

    def w_out():
        return w_ot[...].reshape(4 * qw, width)

    def w_down():
        return w_dn[...].reshape(4 * w_dn.shape[1], width)

    hop3 = iota((nodes_chunk, HOPS, TILE), 1)
    lane3 = iota((nodes_chunk, HOPS, TILE), 2)
    node3 = iota((nodes_chunk, HOPS, TILE), 0)
    lane_graph = (lane3 % GRAPHS).astype(F32)

    def feed_norm(i, carry):
        r = rows_of(i, CHUNK)
        x = tok[r, :].astype(F32) + mm(ctx[r, :], w_out())
        res[r, :] = x
        hat, _ = centred(x)
        n2[r, :] = (hat * gain2 + shift2).astype(BF16)
        return carry

    uw = wu_hbm.shape[1]

    def feed_up(lo, hi):
        cols = slice(lo * uw, hi * uw)

        def step(i, carry):
            r = rows_of(i, CHUNK)
            value, slope = gelu_both(mm(n2[r, :], w_up[:, cols]))
            act[r, cols] = value.astype(BF16)
            gp[r, cols] = slope.astype(BF16)
            return carry

        return step

    def feed_down(i, acc):
        r = rows_of(i, CHUNK)
        out = res[r, :] + mm(act[r, :], w_down())
        lay[r, :] = out
        dr = mm(spread_c, cot[rows_of(i, nodes_chunk), :])
        logit = jnp.sum(out * hopw, axis=-1, keepdims=True)
        gcoef = jnp.sum(out * dr, axis=-1, keepdims=True)
        shape = (nodes_chunk, HOPS, TILE)
        valid = vcol[r, :].reshape(shape)
        valid = jnp.where(hop3 > 0, valid, 0.0)
        logit = jnp.where(valid > 0.5, jnp.broadcast_to(logit, (CHUNK, TILE)).reshape(shape), NEGATIVE)
        e = jnp.exp(logit - jnp.max(logit, axis=1, keepdims=True))
        e = jnp.where(hop3 > 0, e, 0.0)
        weight = e / jnp.sum(e, axis=1, keepdims=True)
        direct = valid * jnp.broadcast_to(gcoef, (CHUNK, TILE)).reshape(shape)
        wcol[r, :] = weight.reshape(CHUNK, TILE)
        dcol[r, :] = direct.reshape(CHUNK, TILE)
        mine = gexp[r, :].reshape(shape) == lane_graph
        both = jnp.where(lane3 < GRAPHS, jnp.where(hop3 == 0, 1.0, weight), -direct)
        return acc + jnp.sum(jnp.where(mine, both, 0.0), axis=0)

    lax.fori_loop(0, chunks, feed_norm, 0)
    fetch_up.start_core()
    lax.fori_loop(0, chunks, feed_up(0, 1), 0)
    fetch_up.end()
    lax.fori_loop(0, cmid, feed_up(1, 4), 0)
    fetch_dn.start_core()
    lax.fori_loop(cmid, chunks, feed_up(1, 4), 0)
    fetch_dn.end()
    sums = lax.fori_loop(0, chunks, feed_down, jnp.zeros((HOPS, TILE), F32))

    def reduce_all(value, one, by_nodes, by_tp, ssem, rsem, overlap=None):
        one[0] = value
        copies = [
            remote(one.at[0], by_nodes.at[k - 1], ssem.at[k - 1], rsem.at[k - 1], node_peer(k)) for k in range(1, 8)
        ]
        for cp in copies:
            cp.start()
        if overlap is not None:
            overlap()
        for cp in copies:
            cp.wait()
        value = one[0]
        for k in range(7):
            value = value + by_nodes[k]
        at = 7
        for b in extra:
            one[at - 6] = value
            cp = remote(one.at[at - 6], by_nodes.at[at], ssem.at[at], rsem.at[at], node_peer(1 << b))
            cp.start()
            cp.wait()
            value = value + by_nodes[at]
            at += 1
        last = one.shape[0] - 1
        one[last] = value
        copies = [
            remote(one.at[last], by_tp.at[k - 1], ssem.at[at + k - 1], rsem.at[at + k - 1], tp_peer(k))
            for k in range(1, 4)
        ]
        for cp in copies:
            cp.start()
        return copies, lambda: one[last] + by_tp[0] + by_tp[1] + by_tp[2]

    def small_products():
        drdown = mm_rt(cot[...], w_down()).astype(BF16)
        hopdown = mm_rt(hop16, w_down()).astype(BF16)
        for i in range(chunks):
            piece = drdown[i * nodes_chunk : (i + 1) * nodes_chunk]
            ab[i, 0:nodes_chunk] = piece
            ab[i, nodes_chunk : 2 * nodes_chunk] = piece
            ab[i, 2 * nodes_chunk : 2 * nodes_chunk + 16] = hopdown
            ab[i, 2 * nodes_chunk + 16 :] = jnp.zeros((TILE - 2 * nodes_chunk - 16, ab.shape[2]), BF16)
        for i in range(chunks):
            at = slice(i * CHUNK, (i + 1) * CHUNK)
            for src, dst in ((n2, n2t), (ctx, ctxt), (n1, n1t)):
                dst[:, at] = src[at, :].T

    copies, total = reduce_all(sums, ar_one, ar_nodes, ar_tp, asend, arecv, small_products)
    for cp in copies:
        cp.wait()
    sums = total()
    row = jnp.broadcast_to(sums[0:1, :], (HOPS, TILE))
    counts = jnp.where(lane8 < GRAPHS, row, pltpu.roll(row, GRAPHS, 1))
    means = (sums / (counts + 1.0))[None]

    def back_one(i, carry):
        hop_acc, zed_acc = carry
        r = rows_of(i, CHUNK)
        shape = (nodes_chunk, HOPS, TILE)
        picked = jnp.where(gexp[r, :].reshape(shape) == lane_graph, means, 0.0)
        mean_r = jnp.sum(jnp.where(lane3 < GRAPHS, picked, 0.0), axis=-1, keepdims=True)
        grad_mean = jnp.sum(jnp.where(lane3 < GRAPHS, 0.0, picked), axis=-1, keepdims=True)
        weight = wcol[r, :].reshape(shape)
        valid = vcol[r, :].reshape(shape)
        coef = jnp.where(hop3 > 0, valid * (weight - mean_r), 1.0)
        grad_w = dcol[r, :].reshape(shape) + grad_mean
        glog = weight * (grad_w - jnp.sum(weight * grad_w, axis=1, keepdims=True))
        coef_hi = coef.astype(BF16).astype(F32)
        glog_hi = glog.astype(BF16).astype(F32)
        zero = jnp.zeros_like(coef)
        mix = jnp.where(lane3 == node3, coef_hi, zero)
        mix = jnp.where(lane3 == node3 + nodes_chunk, coef - coef_hi, mix)
        mix = jnp.where(lane3 == 2 * nodes_chunk, glog_hi, mix)
        mix = jnp.where(lane3 == 2 * nodes_chunk + 1, glog - glog_hi, mix)
        mix = mix.reshape(CHUNK, TILE).astype(BF16)

        dr = cot[rows_of(i, nodes_chunk), :]
        rest = jnp.zeros((TILE - 2 * nodes_chunk - 16, width), BF16)
        dh = jnp.concatenate([dr, dr, hop16, rest], axis=0)
        gl[r, :] = mm(mix, dh)
        gbef[r, :] = (mm(mix, ab[i]) * gp[r, :].astype(F32)).astype(BF16)

        seen = mm_lt(mix, lay[r, :].astype(BF16))
        readout_ref[rows_of(i, nodes_chunk), :] = (seen[0:nodes_chunk] + seen[nodes_chunk : 2 * nodes_chunk]).astype(
            BF16
        )
        hop_acc = hop_acc + seen[2 * nodes_chunk : 2 * nodes_chunk + 8]
        fold = mm_lt(mix, act[r, :])
        zed[rows_of(i, nodes_chunk), :] = (fold[0:nodes_chunk] + fold[nodes_chunk : 2 * nodes_chunk]).astype(BF16)
        zed_acc = zed_acc + fold[2 * nodes_chunk : 2 * nodes_chunk + 8]

        return hop_acc, zed_acc

    def back_norm(i, carry):
        gain_acc, shift_acc = carry
        r = rows_of(i, CHUNK)
        dy = mm_rt(gbef[r, :], w_up[...])
        hat, inv = centred(res[r, :])
        gain_acc = gain_acc + jnp.sum((dy * hat).reshape(nodes_chunk, HOPS, width), axis=0)
        shift_acc = shift_acc + jnp.sum(dy.reshape(nodes_chunk, HOPS, width), axis=0)
        g = dy * gain2
        back = inv * (
            g - jnp.mean(g, axis=-1, keepdims=True) - hat * jnp.mean(g * hat, axis=-1, keepdims=True)
        )
        grad_res = gl[r, :] + back
        gl[r, :] = grad_res
        att = grad_res.astype(BF16)
        datt[r, :] = att
        dctx[r, :] = mm_rt(att, w_out()).astype(BF16)
        return gain_acc, shift_acc

    zero8 = jnp.zeros((HOPS, width), F32)
    hop_sum, zed_sum = lax.fori_loop(0, chunks, back_one, (zero8, jnp.zeros((HOPS, zed.shape[1]), F32)))

    def group(at, array, wide, cols, rc, rp, rz, final, more):
        return Group(array, wide, cols, rc, rp, rz, final, more, gsend, grecv, at * (15 + len(extra)))

    dn = group(0, g_dn, False, (0, 4), rc_dn, rp_dn, rz_dn, fin_dn_ref, mo_dn)
    up = group(1, g_up, True, (0, 4), rc_up, rp_up, rz_up, fin_up_ref, mo_up)
    ot = group(2, g_out, False, (0, 4), rc_out, rp_out, rz_out, fin_out_ref, mo_out)
    qk = [
        group(3 + d, g_in, True, (d, d + 1), rc_in.at[d], rp_in.at[d], rz_in, fin_in_ref, mo_in) for d in range(4)
    ]
    every = (1, 2, 3)

    def plane_of(e):
        out = plane
        for b in range(2):
            if (e >> b) & 1:
                out = out + (1 << b) * (1 - 2 * ((plane // (1 << b)) % 2))
        return out

    def core_copy(g):
        s, r = g.sems(0)
        return remote(g.block(g.rows(1 - c)), g.recv_core, s, r, node_peer(1))

    def go_core(g):
        core_copy(g).start()

    def add_core(g):
        core_copy(g).wait()
        mine = g.block(g.rows(c))
        mine[...] = (mine[...].astype(F32) + g.recv_core[...].astype(F32)).astype(BF16)

    def plane_copies(g):
        return [
            remote(g.block(g.rows(c, plane_of(e))), g.recv_plane.at[e - 1], *g.sems(e), node_peer(2 * e))
            for e in (1, 2, 3)
        ]

    def go_plane(g):
        add_core(g)
        for cp in plane_copies(g):
            cp.start()

    def cut(g, p, e):
        if g.wide:
            w = g.piece_rows // 2
            rows = pl.ds(pl.multiple_of(c * g.half_rows + p * g.piece_rows + e * w, 16), w)
            return g.array.at[rows, g.cols[0] * g.width : g.cols[1] * g.width]
        w = g.width // 2
        return g.array.at[:, g.rows(c, p), e * w : (e + 1) * w]

    def landing(g, m, e):
        if g.wide:
            w = g.piece_rows // 2
            return g.recv_plane.at[m, e * w : (e + 1) * w]
        w = g.width // 2
        return g.recv_plane.at[m, :, :, e * w : (e + 1) * w]

    def fold_copies(g):
        out = []
        for e in range(2):
            for m, far in enumerate((plane_of(1 << e), plane_of(3))):
                sems = g.sems(11 + 2 * e + m)
                out.append(remote(cut(g, far, e), landing(g, m, e), *sems, node_peer(2 << e)))
        return out

    def go_fold(g):
        add_core(g)
        for cp in fold_copies(g):
            cp.start()

    def fold_last(g):
        return [
            remote(cut(g, plane_of(2 >> e), e), landing(g, 2, e), *g.sems(1 + e), node_peer(4 >> e)) for e in range(2)
        ]

    def go_fold_last(g):
        for cp in fold_copies(g):
            cp.wait()
        for e in range(2):
            for m, keep in enumerate((plane, plane_of(2 >> e))):
                mine = cut(g, keep, e)
                mine[...] = (mine[...].astype(F32) + landing(g, m, e)[...].astype(F32)).astype(BF16)
        for cp in fold_last(g):
            cp.start()

    def go_z_fold(g, slots):
        for cp in fold_last(g):
            cp.wait()
        mine = g.block(g.rows(c, plane))
        mine[...] = (mine[...].astype(F32) + g.recv_plane[2].astype(F32)).astype(BF16)
        for cp in z_copies(g, slots):
            cp.start()

    def z_copies(g, slots):
        return [
            remote(g.slot(g.rows(c, plane), d), g.recv_z.at[d - 1], *g.sems(3 + d), tp_peer(d)) for d in slots
        ]

    def go_z(g, slots):
        for cp in plane_copies(g):
            cp.wait()
        mine = g.block(g.rows(c, plane))
        total = mine[...].astype(F32)
        for e in range(3):
            total = total + g.recv_plane[e].astype(F32)
        mine[...] = total.astype(BF16)
        for cp in z_copies(g, slots):
            cp.start()

    def z_first(g):
        return [remote(g.slot(g.rows(c), d), g.recv_z.at[d - 1], *g.sems(3 + d), tp_peer(d)) for d in every]

    def go_z_first(g):
        add_core(g)
        for cp in z_first(g):
            cp.start()

    def own_pieces(g):
        return [
            remote(g.slot(g.rows(c, plane_of(e)), 0), g.recv_plane.at[e - 1], *g.sems(e), node_peer(2 * e))
            for e in (1, 2, 3)
        ]

    def go_own_plane(g):
        for cp in z_first(g):
            cp.wait()
        mine = g.slot(g.rows(c), 0)
        total = mine[...].astype(F32)
        for d in range(3):
            total = total + g.recv_z[d].astype(F32)
        mine[...] = total.astype(BF16)
        for cp in own_pieces(g):
            cp.start()

    def go_own_final(g):
        for cp in own_pieces(g):
            cp.wait()
        total = g.slot(g.rows(c, plane), 0)[...].astype(F32)
        for e in range(3):
            total = total + g.recv_plane[e].astype(F32)
        share(g, total)

    def final_copies(g):
        mine = g.final.at[g.rows(c, plane)]
        return [remote(mine, mine, *g.sems(6 + e), node_peer(2 * e)) for e in (1, 2, 3)]

    def last_copy(g):
        mine = g.final.at[g.rows(c)]
        return remote(mine, mine, *g.sems(10), node_peer(1))

    def go_final(g, waits):
        for cp in waits:
            cp.wait()
        total = g.slot(g.rows(c, plane), 0)[...].astype(F32)
        for d in range(3):
            total = total + g.recv_z[d].astype(F32)
        share(g, total)

    def share(g, total):
        for j, b in enumerate(extra):
            g.more[2 * j] = total.astype(BF16)
            cp = remote(g.more.at[2 * j], g.more.at[2 * j + 1], *g.sems(15 + j), node_peer(1 << b))
            cp.start()
            cp.wait()
            total = total + g.more[2 * j + 1].astype(F32)
        g.final.at[g.rows(c, plane)][...] = total.astype(BF16)
        for cp in final_copies(g):
            cp.start()

    def go_last(g):
        for cp in final_copies(g):
            cp.wait()
        last_copy(g).start()

    def finish(g):
        last_copy(g).wait()

    zed[rows_here // HOPS :, :] = jnp.concatenate([zed_sum, jnp.zeros_like(zed_sum)], axis=0).astype(BF16)
    drh = jnp.concatenate([cot[...], hop16], axis=0)
    g_dn[...] = mm_lt(zed[...], drh).astype(BF16).reshape(g_dn.shape)
    go_core(dn)
    g_up[...] = mm(n2t[...], gbef[...]).astype(BF16)
    go_core(up)
    norm_sums = lax.fori_loop(0, cmid, back_norm, (zero8, zero8))
    go_z_first(dn)
    gain_two, shift_two = lax.fori_loop(cmid, chunks, back_norm, norm_sums)
    go_fold(up)
    g_out[...] = mm(ctxt[...], datt[...]).astype(BF16).reshape(g_out.shape)
    go_core(ot)

    def attend_back(d):
        base = d * 3 * qw

        def step(i, carry):
            at = [i * together + m for m in range(together)]
            rs = [rows_of(a, TILE) for a in at]
            do2 = [pair(dctx[r, d * qw : (d + 1) * qw]) for r in rs]
            grads = [
                compact(mm_rt(qkv[r, base + 2 * qw : base + 3 * qw], x)) for r, x in zip(rs, do2, strict=True)
            ]
            probs = [[pn[a * 8 + 2 * d + h] for h in range(2)] for a in at]
            probs_wide = [jnp.concatenate([expand(p) for p in ps], axis=1) for ps in probs]
            for m, r in enumerate(rs):
                dqkv[r, base + 2 * qw : base + 3 * qw] = mm(probs_wide[m], do2[m]).astype(BF16)
            inner = [[jnp.sum(p * g, axis=0, keepdims=True) for p, g in zip(*x, strict=True)] for x in zip(probs, grads, strict=True)]
            back = [
                [expand(probs[m][h] * (grads[m][h] - inner[m][h])) for h in range(2)] for m in range(together)
            ]
            q2 = [pair(qkv[r, base : base + qw]) for r in rs]
            for m, r in enumerate(rs):
                wide = jnp.concatenate(back[m], axis=1)
                dqkv[r, base + qw : base + 2 * qw] = mm(wide, q2[m]).astype(BF16)
            turned = [mm_rt(eye16, jnp.concatenate(x, axis=0)).astype(BF16) for x in back]
            k2 = [pair(qkv[r, base + qw : base + 2 * qw]) for r in rs]
            for m, r in enumerate(rs):
                dqkv[r, base : base + qw] = (mm(turned[m], k2[m]) * (HEAD**-0.5)).astype(BF16)
            return carry

        lax.fori_loop(0, tiles // together, step, 0)
        g_in[:, base : base + 3 * qw] = mm(n1t[...], dqkv[:, base : base + 3 * qw]).astype(BF16)
        go_core(qk[d])

    def back_two(i, carry):
        gain_acc, shift_acc = carry
        r = rows_of(i, CHUNK)
        dy = mm_rt(dqkv[r, :], w_in[...])
        hat, inv = centred(tok[r, :].astype(F32))
        gain_acc = gain_acc + jnp.sum((dy * hat).reshape(nodes_chunk, HOPS, width), axis=0)
        shift_acc = shift_acc + jnp.sum(dy.reshape(nodes_chunk, HOPS, width), axis=0)
        g = dy * gain1
        back = inv * (
            g - jnp.mean(g, axis=-1, keepdims=True) - hat * jnp.mean(g * hat, axis=-1, keepdims=True)
        )
        gtok_ref[r, :] = (gl[r, :] + back).astype(BF16)
        return gain_acc, shift_acc

    attend_back(3)
    go_fold(ot)
    attend_back(2)
    go_fold(qk[3])
    go_fold_last(up)
    attend_back(1)
    go_fold(qk[2])
    go_fold_last(ot)
    attend_back(0)
    go_plane(qk[1])
    go_z_fold(up, every)
    go_fold_last(qk[3])
    quarter = chunks // 4
    norm_sums = lax.fori_loop(0, quarter, back_two, (zero8, zero8))
    go_plane(qk[0])
    go_z_fold(ot, every)
    go_fold_last(qk[2])
    norm_sums = lax.fori_loop(quarter, 2 * quarter, back_two, norm_sums)
    go_own_plane(dn)
    go_z_fold(qk[3], (3,))
    norm_sums = lax.fori_loop(2 * quarter, 3 * quarter, back_two, norm_sums)
    go_z(qk[1], (1,))
    go_z_fold(qk[2], (2,))
    gain_one, shift_one = lax.fori_loop(3 * quarter, chunks, back_two, norm_sums)

    def fold8(x):
        return jnp.sum(x, axis=0, keepdims=True)

    small = jnp.concatenate(
        [fold8(gain_one), fold8(shift_one), fold8(gain_two), fold8(shift_two), fold8(hop_sum[0:2]), zero8[0:3]], axis=0
    )

    def rest_of():
        go_final(up, z_copies(up, every))
        go_final(ot, z_copies(ot, every))
        go_own_final(dn)
        go_z(qk[0], ())
        go_final(qk[0], [z_copies(qk[d], (d,))[0] for d in every])

    copies, total_small = reduce_all(small, sv_one, sv_nodes, sv_tp, bsend, brecv, rest_of)
    go_last(up)
    go_last(dn)
    go_last(ot)
    go_last(qk[0])
    for cp in copies:
        cp.wait()
    small_ref[...] = total_small()
    finish(dn)
    finish(up)
    finish(ot)
    finish(qk[0])


def results_kernel(readout, gtok, small, fin_in, fin_out, fin_up, fin_dn, *rest):
    o_read, o_tok, o_g1, o_s1, o_q, o_k, o_v, o_out, o_g2, o_s2, o_up, o_dn, o_hop = rest[:13]
    v_q, v_k, v_v, v_out, v_up, v_dn, sems = rest[13:]
    moves = []

    def send(src, dst):
        moves.append(pltpu.make_async_copy(src, dst, sems.at[len(moves)]))
        moves[-1].start()

    send(gtok, o_tok)
    send(readout, o_read)
    v_up[...] = fin_up[...].astype(F32)
    send(v_up, o_up)
    v_dn[...] = fin_dn[...].astype(F32)
    send(v_dn, o_dn)
    qw = o_q.shape[1]
    for i, (x, o) in enumerate(((v_q, o_q), (v_k, o_k), (v_v, o_v))):
        x[...] = fin_in[:, i * qw : (i + 1) * qw].astype(F32)
        send(x, o)
    v_out[...] = fin_out[...].astype(F32)
    send(v_out, o_out)
    width = small.shape[1]
    for i, o in enumerate((o_g1, o_s1, o_g2, o_s2, o_hop)):
        o[...] = small[i : i + 1, :].reshape(width)
    for cp in moves:
        cp.wait()


def shards(
    nn,
    tokens,
    hop_mask,
    graph_ids,
    norm1_gain,
    norm1_shift,
    w_query,
    w_key,
    w_value,
    w_out,
    norm2_gain,
    norm2_shift,
    w_up,
    w_down,
    hop_weight,
    cotangent,
):
    rows, width = tokens.shape
    nodes = rows // HOPS
    qw, uw = w_query.shape[1], w_up.shape[1]
    vm = pl.BlockSpec(memory_space=pltpu.VMEM)
    hbm = pl.BlockSpec(memory_space=pl.ANY)
    extra = len([b for b in range(3, 12) if (1 << b) < nn])

    def v(*shape, dtype=BF16):
        return pltpu.VMEM(shape, dtype)

    tiles, chunks = rows // TILE, rows // CHUNK
    half = width // 2
    more = max(2 * extra, 1)
    scratch = [
        v(tiles, TILE, dtype=jnp.int32),
        v(1, nodes, dtype=jnp.int32),
        v(width),
        v(width),
        v(width),
        v(width),
        v(width),
        v(width, 12 * qw),
        v(width, 4 * uw),
        v(4, qw, width),
        v(4, uw, width),
        v(rows, width),
        v(nodes, width),
        v(rows, width),
        v(rows, 12 * qw),
        v(tiles * 8, HOPS, TILE, dtype=F32),
        v(rows, width),
        v(rows, width, dtype=F32),
        v(rows, width),
        v(rows, 4 * uw),
        v(rows, 4 * uw),
        v(rows, width, dtype=F32),
        v(TILE, TILE),
        v(2 * TILE, TILE),
        v(width, rows),
        v(width, rows),
        v(width, rows),
        v(rows, TILE, dtype=F32),
        v(tiles, HOPS, TILE, dtype=F32),
        v(rows, TILE, dtype=F32),
        v(rows, TILE, dtype=F32),
        v(rows, TILE, dtype=F32),
        v(chunks, TILE, 4 * uw),
        v(nodes + 16, 4 * uw),
        v(rows, 4 * uw),
        v(rows, width, dtype=F32),
        v(rows, width),
        v(rows, width),
        v(rows, 12 * qw),
        v(width, 4 * uw),
        v(4, uw, width),
        v(4, qw, width),
        v(width, 12 * qw),
        v(half, 4 * uw),
        v(4, uw // 2, width),
        v(4, qw // 2, width),
        v(4, half, 3 * qw),
        v(3, half // 4, 4 * uw),
        v(3, uw // 8, width),
        v(3, 4, qw // 8, width),
        v(4, 3, half // 4, 3 * qw),
        v(3, half // 4, uw),
        v(3, uw // 2, width),
        v(3, qw // 8, width),
        v(3, half // 4, 3 * qw),
        v(more, half // 4, uw),
        v(more, uw // 8, width),
        v(more, qw // 8, width),
        v(more, half // 4, 3 * qw),
        v(2 + extra, HOPS, TILE, dtype=F32),
        v(7 + extra, HOPS, TILE, dtype=F32),
        v(3, HOPS, TILE, dtype=F32),
        v(2 + extra, 8, width, dtype=F32),
        v(7 + extra, 8, width, dtype=F32),
        v(3, 8, width, dtype=F32),
        pltpu.SemaphoreType.DMA((15,)),
        pltpu.SemaphoreType.DMA((48,)),
        pltpu.SemaphoreType.DMA((48,)),
        pltpu.SemaphoreType.DMA((7 * (15 + extra),)),
        pltpu.SemaphoreType.DMA((7 * (15 + extra),)),
        pltpu.SemaphoreType.DMA((10 + extra,)),
        pltpu.SemaphoreType.DMA((10 + extra,)),
        pltpu.SemaphoreType.DMA((10 + extra,)),
        pltpu.SemaphoreType.DMA((10 + extra,)),
    ]
    outs = [
        pltpu.VMEM((nodes, width), BF16),
        pltpu.VMEM((rows, width), BF16),
        pltpu.VMEM((8, width), F32),
        pltpu.VMEM((width, 3 * qw), BF16),
        pltpu.VMEM((qw, width), BF16),
        pltpu.VMEM((width, uw), BF16),
        pltpu.VMEM((uw, width), BF16),
    ]
    readout, gtok, small, fin_in, fin_out, fin_up, fin_dn = pl.pallas_call(
        functools.partial(kernel, nn),
        out_shape=outs,
        in_specs=[hbm] * 15,
        out_specs=[vm] * 7,
        scratch_shapes=scratch,
        compiler_params=pltpu.CompilerParams(
            collective_id=0, has_side_effects=True, vmem_limit_bytes=56 * 1024 * 1024
        ),
        name="layer",
    )(
        tokens,
        hop_mask.reshape(tiles, TILE),
        graph_ids.reshape(1, nodes),
        norm1_gain,
        norm1_shift,
        w_query,
        w_key,
        w_value,
        w_out,
        norm2_gain,
        norm2_shift,
        w_up,
        w_down,
        hop_weight,
        cotangent,
    )
    line = jax.ShapeDtypeStruct((width,), F32)
    square = jax.ShapeDtypeStruct((width, qw), F32)
    return pl.pallas_call(
        results_kernel,
        out_shape=[
            jax.ShapeDtypeStruct((nodes, width), BF16),
            jax.ShapeDtypeStruct((rows, width), BF16),
            line,
            line,
            square,
            square,
            square,
            jax.ShapeDtypeStruct((qw, width), F32),
            line,
            line,
            jax.ShapeDtypeStruct((width, uw), F32),
            jax.ShapeDtypeStruct((uw, width), F32),
            line,
        ],
        in_specs=[vm] * 7,
        out_specs=[hbm, hbm, vm, vm, hbm, hbm, hbm, hbm, vm, vm, hbm, hbm, vm],
        scratch_shapes=[v(width, qw, dtype=F32)] * 3
        + [
            v(qw, width, dtype=F32),
            v(width, uw, dtype=F32),
            v(uw, width, dtype=F32),
            pltpu.SemaphoreType.DMA((8,)),
        ],
        compiler_params=pltpu.CompilerParams(vmem_limit_bytes=16 * 1024 * 1024),
        name="results",
    )(readout, gtok, small, fin_in, fin_out, fin_up, fin_dn)


def solution(mesh):
    spread = P(("nodes", "tp"), None)
    flat = P(("nodes", "tp"))
    cols, rows = P(None, "tp"), P("tp", None)
    return jax.shard_map(
        functools.partial(shards, mesh.shape["nodes"]),
        mesh=mesh,
        in_specs=(spread, flat, flat, P(), P(), cols, cols, cols, rows, P(), P(), cols, rows, P(), spread),
        out_specs=(spread, spread, P(), P(), cols, cols, cols, rows, P(), P(), cols, rows, P()),
        check_vma=False,
    )
```

```python
import functools

import jax
import jax.numpy as jnp
from jax import lax
from jax.experimental import pallas as pl
from jax.experimental.pallas import tpu as pltpu
from jax.sharding import PartitionSpec as P

HOPS = 8
HEAD = 64
GRAPHS = 64
EPSILON = 1e-05
NEGATIVE = -1000000000.0
MESH = pl.DeviceIdType.MESH
F32 = jnp.float32
BF16 = jnp.bfloat16
CHUNK = 256
WIDE = 512
TILE = 128


def mm(a, b):
    return lax.dot_general(a, b, (((1,), (0,)), ((), ())), preferred_element_type=F32)


def mm_rt(a, b):
    return lax.dot_general(a, b, (((1,), (1,)), ((), ())), preferred_element_type=F32)


def mm_lt(a, b):
    return lax.dot_general(a, b, (((0,), (0,)), ((), ())), preferred_element_type=F32)


def iota(shape, axis):
    return lax.broadcasted_iota(jnp.int32, shape, axis)


def centred(values):
    centre = values - jnp.mean(values, axis=-1, keepdims=True)
    spread = jnp.mean(centre * centre, axis=-1, keepdims=True)
    return centre * lax.rsqrt(spread + EPSILON), lax.rsqrt(spread + EPSILON)


def gelu_both(x):
    phi = 0.5 + 0.5 * lax.erf(x * 0.7071067811865476)
    bell = jnp.exp2((-0.5 * 1.4426950408889634) * (x * x))
    return x * phi, phi + x * (bell * 0.3989422804014327)


def tokens_of(ref):
    return ref[...].astype(F32).reshape(1, ref.shape[0])


class Group:
    def __init__(self, array, wide, cols, recv_core, recv_plane, recv_z, final, more, send, recv, base):
        self.array, self.wide = array, wide
        self.cols = cols
        self.recv_core, self.recv_plane, self.recv_z = recv_core, recv_plane, recv_z
        self.final = final
        self.more = more
        self.send, self.recv, self.base = send, recv, base
        rows = final.shape[0]
        self.half_rows = rows // 2
        self.piece_rows = rows // 8
        self.width = final.shape[1]

    def sems(self, k):
        return self.send.at[self.base + k], self.recv.at[self.base + k]

    def rows(self, c, p=None):
        if p is None:
            return pl.ds(pl.multiple_of(c * self.half_rows, 16), self.half_rows)
        return pl.ds(pl.multiple_of(c * self.half_rows + p * self.piece_rows, 16), self.piece_rows)

    def block(self, rows):
        if self.wide:
            return self.array.at[rows, self.cols[0] * self.width : self.cols[1] * self.width]
        return self.array.at[:, rows]

    def slot(self, rows, d):
        if self.wide:
            return self.array.at[rows, d * self.width : (d + 1) * self.width]
        return self.array.at[d, rows]


def kernel(
    nn,
    tok_hbm,
    mask_ref,
    gid_ref,
    g1_ref,
    s1_ref,
    wq_hbm,
    wk_hbm,
    wv_hbm,
    wo_hbm,
    g2_ref,
    s2_ref,
    wu_hbm,
    wd_hbm,
    hw_ref,
    cot_hbm,
    readout_ref,
    gtok_ref,
    small_ref,
    fin_in_ref,
    fin_out_ref,
    fin_up_ref,
    fin_dn_ref,
    mask_v,
    gid_v,
    g1_v,
    s1_v,
    g2_v,
    s2_v,
    hw_v,
    w_in,
    w_up,
    w_ot,
    w_dn,
    tok,
    cot,
    n1,
    qkv,
    pn,
    ctx,
    res,
    n2,
    act,
    gp,
    lay,
    emask,
    pmask,
    n1t,
    n2t,
    ctxt,
    vcol,
    mt,
    gexp,
    wcol,
    dcol,
    ab,
    zed,
    mixes,
    gbef,
    gl,
    datt,
    dctx,
    dqkv,
    g_up,
    g_dn,
    g_out,
    g_in,
    rc_up,
    rc_dn,
    rc_out,
    rc_in,
    rp_up,
    rp_dn,
    rp_out,
    rp_in,
    rz_up,
    rz_dn,
    rz_out,
    rz_in,
    mo_up,
    mo_dn,
    mo_out,
    mo_in,
    ar_one,
    ar_nodes,
    ar_tp,
    sv_one,
    sv_nodes,
    sv_tp,
    lsem,
    wsend,
    wrecv,
    gsend,
    grecv,
    asend,
    arecv,
    bsend,
    brecv,
):
    n, t = lax.axis_index("nodes"), lax.axis_index("tp")
    rows_here, width = tok.shape
    chunks = rows_here // CHUNK
    wides = rows_here // WIDE
    tiles = rows_here // TILE
    c = n % 2
    plane = (n // 2) % 4
    eighth = 4 * c + plane
    side = (plane % 2 + plane // 2) % 2
    extra = [b for b in range(3, 12) if (1 << b) < nn]

    def node_peer(k):
        out = n
        for b in range(12):
            if (k >> b) & 1:
                bit = (n // (1 << b)) % 2
                out = out + (1 << b) * (1 - 2 * bit)
        return (out, t)

    def tp_peer(k):
        out = t
        for b in range(2):
            if (k >> b) & 1:
                bit = (t // (1 << b)) % 2
                out = out + (1 << b) * (1 - 2 * bit)
        return (n, out)

    def remote(src, dst, ssem, rsem, peer):
        return pltpu.make_async_remote_copy(
            src_ref=src, dst_ref=dst, send_sem=ssem, recv_sem=rsem, device_id=peer, device_id_type=MESH
        )

    qw = wq_hbm.shape[1]
    local = [
        pltpu.make_async_copy(wq_hbm, w_in.at[:, 0:qw], lsem.at[0]),
        pltpu.make_async_copy(wk_hbm, w_in.at[:, qw : 2 * qw], lsem.at[1]),
        pltpu.make_async_copy(wv_hbm, w_in.at[:, 2 * qw : 3 * qw], lsem.at[2]),
        pltpu.make_async_copy(tok_hbm, tok, lsem.at[3]),
        pltpu.make_async_copy(wo_hbm, w_ot.at[0], lsem.at[4]),
        pltpu.make_async_copy(wd_hbm, w_dn.at[0], lsem.at[5]),
        pltpu.make_async_copy(wu_hbm, w_up.at[:, 0 : wu_hbm.shape[1]], lsem.at[6]),
        pltpu.make_async_copy(cot_hbm, cot, lsem.at[7]),
    ]
    tiny = ((mask_ref, mask_v), (gid_ref, gid_v), (g1_ref, g1_v), (s1_ref, s1_v), (g2_ref, g2_v), (s2_ref, s2_v))
    for i, (src, dst) in enumerate(tiny + ((hw_ref, hw_v),)):
        local.append(pltpu.make_async_copy(src, dst, lsem.at[8 + i]))
    for copy in local:
        copy.start()

    barrier = pltpu.get_barrier_semaphore()
    greet = [node_peer(k) for k in range(1, 8)] + [node_peer(1 << b) for b in extra]
    greet += [tp_peer(k) for k in range(1, 4)]
    for peer in greet:
        pl.semaphore_signal(barrier, inc=1, device_id=peer, device_id_type=MESH)
    pl.semaphore_wait(barrier, len(greet))

    def weight_block(ref, off, size, d0, d1):
        rows = pl.ds(pl.multiple_of(off, 16), size)
        if len(ref.shape) == 3:
            return ref.at[d0:d1, rows]
        w = ref.shape[1] // 4
        return ref.at[rows, d0 * w : d1 * w]

    class Fetch:
        def __init__(self, ref, slots, base, halves=False):
            total = ref.shape[1] if len(ref.shape) == 3 else ref.shape[0]
            d0, d1 = slots
            sems = iter(range(base, base + 8))

            def go(src, dst, peer):
                k = next(sems)
                return remote(src, dst, wsend.at[k], wrecv.at[k], peer)

            def rows(off, size):
                return weight_block(ref, off, size, d0, d1)

            part = total // 4 if halves else total // 8
            own = (2 * side + c if halves else eighth) * part
            self.z = [
                go(weight_block(ref, own, part, 0, 1), weight_block(ref, own, part, d, d + 1), tp_peer(d))
                for d in range(d0, d1)
            ]
            if halves:
                some = [rows(own + e * (part // 2), part // 2) for e in range(2)]
                self.plane = [go(x, x, node_peer(2 << e)) for e, x in enumerate(some)]
                lots = [rows(own, part), rows((2 * (1 - side) + c) * part, part)]
            else:
                self.plane = [go(rows(own, part), rows(own, part), node_peer(2 * e)) for e in (1, 2, 3)]
                lots = [rows(c * (total // 2), total // 2)]
            self.core = [go(x, x, node_peer(1)) for x in lots]

        def start_z(self):
            for cp in self.z:
                cp.start()

        def start_plane(self):
            for cp in self.z:
                cp.wait()
            for cp in self.plane:
                cp.start()

        def start_core(self):
            for cp in self.plane:
                cp.wait()
            for cp in self.core:
                cp.start()

        def end(self):
            for cp in self.core:
                cp.wait()

    fetch_in = [None] + [Fetch(w_in, (d, d + 1), 8 * (d - 1)) for d in (1, 2, 3)]
    fetch_ot = Fetch(w_ot, (1, 4), 24)
    fetch_up = Fetch(w_up, (1, 4), 32)
    fetch_dn = Fetch(w_dn, (1, 4), 40)

    for i in (0, 1, 2):
        local[i].wait()
    for d in (1, 2, 3):
        fetch_in[d].start_z()

    for i in range(8, 15):
        local[i].wait()
    gain1 = tokens_of(g1_v)
    shift1 = tokens_of(s1_v)
    gain2 = tokens_of(g2_v)
    shift2 = tokens_of(s2_v)
    hopw = tokens_of(hw_v)
    hop16 = jnp.broadcast_to(hopw, (16, width)).astype(BF16)

    eye = iota((TILE, TILE), 0) == iota((TILE, TILE), 1)
    ones = jnp.ones((TILE, TILE), BF16)
    lane8 = iota((HOPS, TILE), 1)
    block8 = lane8 // HOPS
    eye16 = eye.astype(F32).astype(BF16)
    emask[...] = (iota((TILE, TILE), 0) // HOPS == iota((TILE, TILE), 1) // HOPS).astype(F32).astype(BF16)
    first = (iota((2 * TILE, TILE), 0) < TILE) == (iota((2 * TILE, TILE), 1) < HEAD)
    pmask[...] = first.astype(F32).astype(BF16)
    nodes_chunk = CHUNK // HOPS
    spread_c = (iota((CHUNK, nodes_chunk), 0) // HOPS == iota((CHUNK, nodes_chunk), 1)).astype(F32).astype(BF16)

    def rows_of(i, size):
        return pl.ds(pl.multiple_of(i * size, size), size)

    mask_f = mask_v[...].astype(F32)
    for i in range(tiles):
        col = mm(jnp.where(eye, mask_f[i : i + 1, :], 0.0).astype(BF16), ones)
        vcol[i * TILE : (i + 1) * TILE, :] = col
        acc = jnp.zeros((HOPS, TILE), F32)
        col3 = col.reshape(TILE // HOPS, HOPS, TILE)
        for r in range(TILE // HOPS):
            acc = jnp.where(block8 == r, col3[r], acc)
        mt[i] = acc

    local[3].wait()

    def norm_one(i, carry):
        x = tok[rows_of(i, CHUNK), :].astype(F32)
        hat, _ = centred(x)
        n1[rows_of(i, CHUNK), :] = (hat * gain1 + shift1).astype(BF16)
        return carry

    lax.fori_loop(0, chunks, norm_one, 0)

    def project(d, lo, hi):
        base = d * 3 * qw

        def step(i, carry):
            r = rows_of(i, WIDE)
            out = mm(n1[r, :], w_in[:, base : base + 3 * qw])
            qkv[r, base : base + qw] = (out[:, 0:qw] * (HEAD**-0.5)).astype(BF16)
            qkv[r, base + qw : base + 3 * qw] = out[:, qw:].astype(BF16)
            return carry

        lax.fori_loop(lo, hi, step, 0)

    def pair(x):
        return jnp.concatenate([x, x], axis=0) * pmask[...]

    bits = [((lane8 // (HOPS << b)) % 2) == 1 for b in range(4)]

    def compact(x):
        out = []
        for h in range(2):
            x3 = x[:, h * TILE : (h + 1) * TILE].reshape(TILE // HOPS, HOPS, TILE)
            parts = [x3[r] for r in range(TILE // HOPS)]
            for b in range(4):
                parts = [jnp.where(bits[b], parts[2 * m + 1], parts[2 * m]) for m in range(len(parts) // 2)]
            out.append(parts[0])
        return out

    def expand(x):
        twice = jnp.concatenate([x, x], axis=0).astype(BF16)
        return jnp.concatenate([twice] * (TILE // 16), axis=0) * emask[...]

    together = 8

    steps = tiles // together
    mid = steps // 2

    def attend(d, lo, hi):
        base = d * 3 * qw

        def step(i, carry):
            at = [i * together + m for m in range(together)]
            rs = [rows_of(a, TILE) for a in at]
            q2 = [pair(qkv[r, base : base + qw]) for r in rs]
            scores = [compact(mm_rt(qkv[r, base + qw : base + 2 * qw], x)) for r, x in zip(rs, q2, strict=True)]
            wide = []
            for m, a in enumerate(at):
                keep = mt[a] > 0.5
                for h in range(2):
                    wide.append(jnp.where(keep, scores[m][h], NEGATIVE))
            peaks = [jnp.max(x, axis=0, keepdims=True) for x in wide]
            wide = [jnp.exp(x - y) for x, y in zip(wide, peaks, strict=True)]
            totals = [jnp.sum(x, axis=0, keepdims=True) for x in wide]
            wide = [x / y for x, y in zip(wide, totals, strict=True)]
            for m, a in enumerate(at):
                for h in range(2):
                    pn[a * 8 + 2 * d + h] = wide[2 * m + h]
            turned = [
                mm_rt(eye16, jnp.concatenate([expand(wide[2 * m]), expand(wide[2 * m + 1])], axis=0)).astype(BF16)
                for m in range(together)
            ]
            v2 = [pair(qkv[r, base + 2 * qw : base + 3 * qw]) for r in rs]
            for m, r in enumerate(rs):
                ctx[r, d * qw : (d + 1) * qw] = mm(turned[m], v2[m]).astype(BF16)
            return carry

        lax.fori_loop(lo, hi, step, 0)

    gcol = mm(jnp.where(eye, gid_v[...].astype(F32), 0.0).astype(BF16), ones).astype(BF16)
    for i in range(chunks):
        gexp[i * CHUNK : (i + 1) * CHUNK, :] = mm(spread_c, gcol[i * nodes_chunk : (i + 1) * nodes_chunk])
    fetch_in[1].start_plane()
    project(0, 0, wides // 2)
    fetch_in[2].start_plane()
    project(0, wides // 2, wides)
    fetch_in[3].start_plane()
    for i in (4, 5, 6, 7):
        local[i].wait()
    fetch_ot.start_z()
    fetch_up.start_z()
    fetch_dn.start_z()
    attend(0, 0, mid)
    fetch_ot.start_plane()
    fetch_in[1].start_core()
    attend(0, mid, steps)
    fetch_in[1].end()
    fetch_in[2].start_core()
    project(1, 0, wides // 2)
    fetch_up.start_plane()
    project(1, wides // 2, wides)
    attend(1, 0, mid)
    fetch_in[3].start_core()
    attend(1, mid, steps)
    fetch_in[2].end()
    project(2, 0, wides // 2)
    fetch_dn.start_plane()
    project(2, wides // 2, wides)
    attend(2, 0, mid)
    fetch_ot.start_core()
    attend(2, mid, steps)
    fetch_in[3].end()
    project(3, 0, wides)
    attend(3, 0, mid)
    attend(3, mid, steps)
    fetch_ot.end()

    def w_out():
        return w_ot[...].reshape(4 * qw, width)

    def w_down():
        return w_dn[...].reshape(4 * w_dn.shape[1], width)

    hop3 = iota((nodes_chunk, HOPS, TILE), 1)
    lane3 = iota((nodes_chunk, HOPS, TILE), 2)
    node3 = iota((nodes_chunk, HOPS, TILE), 0)
    lane_graph = (lane3 % GRAPHS).astype(F32)

    def feed_norm(i, carry):
        r = rows_of(i, WIDE)
        x = tok[r, :].astype(F32) + mm(ctx[r, :], w_out())
        res[r, :] = x
        hat, _ = centred(x)
        n2[r, :] = (hat * gain2 + shift2).astype(BF16)
        return carry

    uw = wu_hbm.shape[1]

    def feed_up(lo, hi):
        cols = slice(lo * uw, hi * uw)

        def step(i, carry):
            r = rows_of(i, WIDE)
            value, slope = gelu_both(mm(n2[r, :], w_up[:, cols]))
            act[r, cols] = value.astype(BF16)
            gp[r, cols] = slope.astype(BF16)
            return carry

        return step

    def feed_down(i, acc):
        r = rows_of(i, WIDE)
        lay[r, :] = res[r, :] + mm(act[r, :], w_down())
        for m in range(WIDE // CHUNK):
            acc = hops(i * (WIDE // CHUNK) + m, acc)
        return acc

    def hops(i, acc):
        r = rows_of(i, CHUNK)
        out = lay[r, :]
        dr = mm(spread_c, cot[rows_of(i, nodes_chunk), :])
        logit = jnp.sum(out * hopw, axis=-1, keepdims=True)
        gcoef = jnp.sum(out * dr, axis=-1, keepdims=True)
        shape = (nodes_chunk, HOPS, TILE)
        valid = vcol[r, :].reshape(shape)
        valid = jnp.where(hop3 > 0, valid, 0.0)
        logit = jnp.where(valid > 0.5, jnp.broadcast_to(logit, (CHUNK, TILE)).reshape(shape), NEGATIVE)
        e = jnp.exp(logit - jnp.max(logit, axis=1, keepdims=True))
        e = jnp.where(hop3 > 0, e, 0.0)
        weight = e / jnp.sum(e, axis=1, keepdims=True)
        direct = valid * jnp.broadcast_to(gcoef, (CHUNK, TILE)).reshape(shape)
        wcol[r, :] = weight.reshape(CHUNK, TILE)
        dcol[r, :] = direct.reshape(CHUNK, TILE)
        mine = gexp[r, :].reshape(shape) == lane_graph
        both = jnp.where(lane3 < GRAPHS, jnp.where(hop3 == 0, 1.0, weight), -direct)
        return acc + jnp.sum(jnp.where(mine, both, 0.0), axis=0)

    lax.fori_loop(0, wides, feed_norm, 0)
    fetch_up.start_core()
    lax.fori_loop(0, wides, feed_up(0, 1), 0)
    fetch_up.end()
    lax.fori_loop(0, wides // 2, feed_up(1, 4), 0)
    fetch_dn.start_core()
    lax.fori_loop(wides // 2, wides, feed_up(1, 4), 0)
    fetch_dn.end()
    sums = lax.fori_loop(0, wides, feed_down, jnp.zeros((HOPS, TILE), F32))

    def reduce_all(value, one, by_nodes, by_tp, ssem, rsem, overlap=None):
        one[0] = value
        copies = [
            remote(one.at[0], by_nodes.at[k - 1], ssem.at[k - 1], rsem.at[k - 1], node_peer(k)) for k in range(1, 8)
        ]
        for cp in copies:
            cp.start()
        if overlap is not None:
            overlap()
        for cp in copies:
            cp.wait()
        value = one[0]
        for k in range(7):
            value = value + by_nodes[k]
        at = 7
        for b in extra:
            one[at - 6] = value
            cp = remote(one.at[at - 6], by_nodes.at[at], ssem.at[at], rsem.at[at], node_peer(1 << b))
            cp.start()
            cp.wait()
            value = value + by_nodes[at]
            at += 1
        last = one.shape[0] - 1
        one[last] = value
        copies = [
            remote(one.at[last], by_tp.at[k - 1], ssem.at[at + k - 1], rsem.at[at + k - 1], tp_peer(k))
            for k in range(1, 4)
        ]
        for cp in copies:
            cp.start()
        return copies, lambda: one[last] + by_tp[0] + by_tp[1] + by_tp[2]

    def small_products():
        drdown = mm_rt(cot[...], w_down()).astype(BF16)
        hopdown = mm_rt(hop16, w_down()).astype(BF16)
        for i in range(chunks):
            piece = drdown[i * nodes_chunk : (i + 1) * nodes_chunk]
            ab[i, 0:nodes_chunk] = piece
            ab[i, nodes_chunk : 2 * nodes_chunk] = piece
            ab[i, 2 * nodes_chunk : 2 * nodes_chunk + 16] = hopdown
            ab[i, 2 * nodes_chunk + 16 :] = jnp.zeros((TILE - 2 * nodes_chunk - 16, ab.shape[2]), BF16)
        for i in range(chunks):
            at = slice(i * CHUNK, (i + 1) * CHUNK)
            for src, dst in ((n2, n2t), (ctx, ctxt), (n1, n1t)):
                dst[:, at] = src[at, :].T

    copies, total = reduce_all(sums, ar_one, ar_nodes, ar_tp, asend, arecv, small_products)
    for cp in copies:
        cp.wait()
    sums = total()
    row = jnp.broadcast_to(sums[0:1, :], (HOPS, TILE))
    counts = jnp.where(lane8 < GRAPHS, row, pltpu.roll(row, GRAPHS, 1))
    means = (sums / (counts + 1.0))[None]

    def back_one(i, carry):
        zed_acc = carry
        r = rows_of(i, CHUNK)
        shape = (nodes_chunk, HOPS, TILE)
        picked = jnp.where(gexp[r, :].reshape(shape) == lane_graph, means, 0.0)
        mean_r = jnp.sum(jnp.where(lane3 < GRAPHS, picked, 0.0), axis=-1, keepdims=True)
        grad_mean = jnp.sum(jnp.where(lane3 < GRAPHS, 0.0, picked), axis=-1, keepdims=True)
        weight = wcol[r, :].reshape(shape)
        valid = vcol[r, :].reshape(shape)
        coef = jnp.where(hop3 > 0, valid * (weight - mean_r), 1.0)
        grad_w = dcol[r, :].reshape(shape) + grad_mean
        glog = weight * (grad_w - jnp.sum(weight * grad_w, axis=1, keepdims=True))
        coef_hi = coef.astype(BF16).astype(F32)
        glog_hi = glog.astype(BF16).astype(F32)
        zero = jnp.zeros_like(coef)
        mix = jnp.where(lane3 == node3, coef_hi, zero)
        mix = jnp.where(lane3 == node3 + nodes_chunk, coef - coef_hi, mix)
        mix = jnp.where(lane3 == 2 * nodes_chunk, glog_hi, mix)
        mix = jnp.where(lane3 == 2 * nodes_chunk + 1, glog - glog_hi, mix)
        mix = mix.reshape(CHUNK, TILE).astype(BF16)

        mixes[r, :] = mix
        gbef[r, :] = (mm(mix, ab[i]) * gp[r, :].astype(F32)).astype(BF16)

        fold = mm_lt(mix, act[r, :])
        zed[rows_of(i, nodes_chunk), :] = (fold[0:nodes_chunk] + fold[nodes_chunk : 2 * nodes_chunk]).astype(BF16)
        zed_acc = zed_acc + fold[2 * nodes_chunk : 2 * nodes_chunk + 8]

        return zed_acc

    def back_norm(i, carry):
        gain_acc, shift_acc, hop_acc = carry
        r = rows_of(i, WIDE)
        hop_acc = layer_grads(i, hop_acc)
        dy = mm_rt(gbef[r, :], w_up[...])
        hat, inv = centred(res[r, :])
        gain_acc = gain_acc + jnp.sum((dy * hat).reshape(WIDE // HOPS, HOPS, width), axis=0)
        shift_acc = shift_acc + jnp.sum(dy.reshape(WIDE // HOPS, HOPS, width), axis=0)
        g = dy * gain2
        back = inv * (
            g - jnp.mean(g, axis=-1, keepdims=True) - hat * jnp.mean(g * hat, axis=-1, keepdims=True)
        )
        grad_res = gl[r, :] + back
        gl[r, :] = grad_res
        att = grad_res.astype(BF16)
        datt[r, :] = att
        dctx[r, :] = mm_rt(att, w_out()).astype(BF16)
        return gain_acc, shift_acc, hop_acc

    def layer_grads(wide, hop_acc):
        for m in range(WIDE // CHUNK):
            i = wide * (WIDE // CHUNK) + m
            r = rows_of(i, CHUNK)
            mix = mixes[r, :]
            dr = cot[rows_of(i, nodes_chunk), :]
            rest = jnp.zeros((TILE - 2 * nodes_chunk - 16, width), BF16)
            gl[r, :] = mm(mix, jnp.concatenate([dr, dr, hop16, rest], axis=0))
            seen = mm_lt(mix, lay[r, :].astype(BF16))
            both = seen[0:nodes_chunk] + seen[nodes_chunk : 2 * nodes_chunk]
            readout_ref[rows_of(i, nodes_chunk), :] = both.astype(BF16)
            hop_acc = hop_acc + seen[2 * nodes_chunk : 2 * nodes_chunk + 8]
        return hop_acc

    zero8 = jnp.zeros((HOPS, width), F32)
    zed_sum = lax.fori_loop(0, chunks, back_one, jnp.zeros((HOPS, zed.shape[1]), F32))

    def group(at, array, wide, cols, rc, rp, rz, final, more):
        return Group(array, wide, cols, rc, rp, rz, final, more, gsend, grecv, at * (15 + len(extra)))

    dn = group(0, g_dn, False, (0, 4), rc_dn, rp_dn, rz_dn, fin_dn_ref, mo_dn)
    up = group(1, g_up, True, (0, 4), rc_up, rp_up, rz_up, fin_up_ref, mo_up)
    ot = group(2, g_out, False, (0, 4), rc_out, rp_out, rz_out, fin_out_ref, mo_out)
    qk = [
        group(3 + d, g_in, True, (d, d + 1), rc_in.at[d], rp_in.at[d], rz_in, fin_in_ref, mo_in) for d in range(4)
    ]
    every = (1, 2, 3)

    def plane_of(e):
        out = plane
        for b in range(2):
            if (e >> b) & 1:
                out = out + (1 << b) * (1 - 2 * ((plane // (1 << b)) % 2))
        return out

    def core_copy(g):
        s, r = g.sems(0)
        return remote(g.block(g.rows(1 - c)), g.recv_core, s, r, node_peer(1))

    def go_core(g):
        core_copy(g).start()

    def add_core(g):
        core_copy(g).wait()
        mine = g.block(g.rows(c))
        mine[...] = (mine[...].astype(F32) + g.recv_core[...].astype(F32)).astype(BF16)

    def plane_copies(g):
        return [
            remote(g.block(g.rows(c, plane_of(e))), g.recv_plane.at[e - 1], *g.sems(e), node_peer(2 * e))
            for e in (1, 2, 3)
        ]

    def go_plane(g):
        add_core(g)
        for cp in plane_copies(g):
            cp.start()

    def cut(g, p, e):
        if g.wide:
            w = g.piece_rows // 2
            rows = pl.ds(pl.multiple_of(c * g.half_rows + p * g.piece_rows + e * w, 16), w)
            return g.array.at[rows, g.cols[0] * g.width : g.cols[1] * g.width]
        w = g.width // 2
        return g.array.at[:, g.rows(c, p), e * w : (e + 1) * w]

    def landing(g, m, e):
        if g.wide:
            w = g.piece_rows // 2
            return g.recv_plane.at[m, e * w : (e + 1) * w]
        w = g.width // 2
        return g.recv_plane.at[m, :, :, e * w : (e + 1) * w]

    def fold_copies(g):
        out = []
        for e in range(2):
            for m, far in enumerate((plane_of(1 << e), plane_of(3))):
                sems = g.sems(11 + 2 * e + m)
                out.append(remote(cut(g, far, e), landing(g, m, e), *sems, node_peer(2 << e)))
        return out

    def go_fold(g):
        add_core(g)
        for cp in fold_copies(g):
            cp.start()

    def fold_last(g):
        return [
            remote(cut(g, plane_of(2 >> e), e), landing(g, 2, e), *g.sems(1 + e), node_peer(4 >> e)) for e in range(2)
        ]

    def go_fold_last(g):
        for cp in fold_copies(g):
            cp.wait()
        for e in range(2):
            for m, keep in enumerate((plane, plane_of(2 >> e))):
                mine = cut(g, keep, e)
                mine[...] = (mine[...].astype(F32) + landing(g, m, e)[...].astype(F32)).astype(BF16)
        for cp in fold_last(g):
            cp.start()

    def go_z_fold(g, slots):
        for cp in fold_last(g):
            cp.wait()
        mine = g.block(g.rows(c, plane))
        mine[...] = (mine[...].astype(F32) + g.recv_plane[2].astype(F32)).astype(BF16)
        for cp in z_copies(g, slots):
            cp.start()

    def z_copies(g, slots):
        return [
            remote(g.slot(g.rows(c, plane), d), g.recv_z.at[d - 1], *g.sems(3 + d), tp_peer(d)) for d in slots
        ]

    def go_z(g, slots):
        for cp in plane_copies(g):
            cp.wait()
        mine = g.block(g.rows(c, plane))
        total = mine[...].astype(F32)
        for e in range(3):
            total = total + g.recv_plane[e].astype(F32)
        mine[...] = total.astype(BF16)
        for cp in z_copies(g, slots):
            cp.start()

    def z_first(g):
        return [remote(g.slot(g.rows(c), d), g.recv_z.at[d - 1], *g.sems(3 + d), tp_peer(d)) for d in every]

    def go_z_first(g):
        add_core(g)
        for cp in z_first(g):
            cp.start()

    def own_pieces(g):
        return [
            remote(g.slot(g.rows(c, plane_of(e)), 0), g.recv_plane.at[e - 1], *g.sems(e), node_peer(2 * e))
            for e in (1, 2, 3)
        ]

    def go_own_plane(g):
        for cp in z_first(g):
            cp.wait()
        mine = g.slot(g.rows(c), 0)
        total = mine[...].astype(F32)
        for d in range(3):
            total = total + g.recv_z[d].astype(F32)
        mine[...] = total.astype(BF16)
        for cp in own_pieces(g):
            cp.start()

    def go_own_final(g):
        for cp in own_pieces(g):
            cp.wait()
        total = g.slot(g.rows(c, plane), 0)[...].astype(F32)
        for e in range(3):
            total = total + g.recv_plane[e].astype(F32)
        share(g, total)

    def final_copies(g):
        mine = g.final.at[g.rows(c, plane)]
        return [remote(mine, mine, *g.sems(6 + e), node_peer(2 * e)) for e in (1, 2, 3)]

    def last_copy(g):
        mine = g.final.at[g.rows(c)]
        return remote(mine, mine, *g.sems(10), node_peer(1))

    def go_final(g, waits):
        for cp in waits:
            cp.wait()
        total = g.slot(g.rows(c, plane), 0)[...].astype(F32)
        for d in range(3):
            total = total + g.recv_z[d].astype(F32)
        share(g, total)

    def share(g, total):
        for j, b in enumerate(extra):
            g.more[2 * j] = total.astype(BF16)
            cp = remote(g.more.at[2 * j], g.more.at[2 * j + 1], *g.sems(15 + j), node_peer(1 << b))
            cp.start()
            cp.wait()
            total = total + g.more[2 * j + 1].astype(F32)
        g.final.at[g.rows(c, plane)][...] = total.astype(BF16)
        for cp in final_copies(g):
            cp.start()

    def go_last(g):
        for cp in final_copies(g):
            cp.wait()
        last_copy(g).start()

    def finish(g):
        last_copy(g).wait()

    zed[rows_here // HOPS :, :] = jnp.concatenate([zed_sum, jnp.zeros_like(zed_sum)], axis=0).astype(BF16)
    drh = jnp.concatenate([cot[...], hop16], axis=0)
    g_dn[...] = mm_lt(zed[...], drh).astype(BF16).reshape(g_dn.shape)
    go_core(dn)
    g_up[...] = mm(n2t[...], gbef[...]).astype(BF16)
    go_core(up)
    norm_sums = lax.fori_loop(0, wides // 2, back_norm, (zero8, zero8, zero8))
    go_z_first(dn)
    gain_two, shift_two, hop_sum = lax.fori_loop(wides // 2, wides, back_norm, norm_sums)
    go_fold(up)
    g_out[...] = mm(ctxt[...], datt[...]).astype(BF16).reshape(g_out.shape)
    go_core(ot)

    def attend_back(d):
        base = d * 3 * qw

        def step(i, carry):
            at = [i * together + m for m in range(together)]
            rs = [rows_of(a, TILE) for a in at]
            do2 = [pair(dctx[r, d * qw : (d + 1) * qw]) for r in rs]
            grads = [
                compact(mm_rt(qkv[r, base + 2 * qw : base + 3 * qw], x)) for r, x in zip(rs, do2, strict=True)
            ]
            probs = [[pn[a * 8 + 2 * d + h] for h in range(2)] for a in at]
            probs_wide = [jnp.concatenate([expand(p) for p in ps], axis=1) for ps in probs]
            for m, r in enumerate(rs):
                dqkv[r, base + 2 * qw : base + 3 * qw] = mm(probs_wide[m], do2[m]).astype(BF16)
            inner = [[jnp.sum(p * g, axis=0, keepdims=True) for p, g in zip(*x, strict=True)] for x in zip(probs, grads, strict=True)]
            back = [
                [expand(probs[m][h] * (grads[m][h] - inner[m][h])) for h in range(2)] for m in range(together)
            ]
            q2 = [pair(qkv[r, base : base + qw]) for r in rs]
            for m, r in enumerate(rs):
                wide = jnp.concatenate(back[m], axis=1)
                dqkv[r, base + qw : base + 2 * qw] = mm(wide, q2[m]).astype(BF16)
            turned = [mm_rt(eye16, jnp.concatenate(x, axis=0)).astype(BF16) for x in back]
            k2 = [pair(qkv[r, base + qw : base + 2 * qw]) for r in rs]
            for m, r in enumerate(rs):
                dqkv[r, base : base + qw] = (mm(turned[m], k2[m]) * (HEAD**-0.5)).astype(BF16)
            return carry

        lax.fori_loop(0, tiles // together, step, 0)
        g_in[:, base : base + 3 * qw] = mm(n1t[...], dqkv[:, base : base + 3 * qw]).astype(BF16)
        go_core(qk[d])

    def back_two(i, carry):
        gain_acc, shift_acc = carry
        r = rows_of(i, WIDE)
        dy = mm_rt(dqkv[r, :], w_in[...])
        hat, inv = centred(tok[r, :].astype(F32))
        gain_acc = gain_acc + jnp.sum((dy * hat).reshape(WIDE // HOPS, HOPS, width), axis=0)
        shift_acc = shift_acc + jnp.sum(dy.reshape(WIDE // HOPS, HOPS, width), axis=0)
        g = dy * gain1
        back = inv * (
            g - jnp.mean(g, axis=-1, keepdims=True) - hat * jnp.mean(g * hat, axis=-1, keepdims=True)
        )
        gtok_ref[r, :] = (gl[r, :] + back).astype(BF16)
        return gain_acc, shift_acc

    attend_back(3)
    go_fold(ot)
    attend_back(2)
    go_fold(qk[3])
    go_fold_last(up)
    attend_back(1)
    go_fold(qk[2])
    go_fold_last(ot)
    attend_back(0)
    go_plane(qk[1])
    go_z_fold(up, every)
    go_fold_last(qk[3])
    norm_sums = lax.fori_loop(0, wides // 2, back_two, (zero8, zero8))
    go_plane(qk[0])
    go_z_fold(ot, every)
    go_fold_last(qk[2])
    go_own_plane(dn)
    go_z_fold(qk[3], (3,))
    gain_one, shift_one = lax.fori_loop(wides // 2, wides, back_two, norm_sums)
    go_z(qk[1], (1,))
    go_z_fold(qk[2], (2,))

    def fold8(x):
        return jnp.sum(x, axis=0, keepdims=True)

    small = jnp.concatenate(
        [fold8(gain_one), fold8(shift_one), fold8(gain_two), fold8(shift_two), fold8(hop_sum[0:2]), zero8[0:3]], axis=0
    )

    def rest_of():
        go_final(up, z_copies(up, every))
        go_final(ot, z_copies(ot, every))
        go_own_final(dn)
        go_z(qk[0], ())
        go_final(qk[0], [z_copies(qk[d], (d,))[0] for d in every])

    copies, total_small = reduce_all(small, sv_one, sv_nodes, sv_tp, bsend, brecv, rest_of)
    go_last(up)
    go_last(dn)
    go_last(ot)
    go_last(qk[0])
    for cp in copies:
        cp.wait()
    small_ref[...] = total_small()
    finish(dn)
    finish(up)
    finish(ot)
    finish(qk[0])


def results_kernel(readout, gtok, small, fin_in, fin_out, fin_up, fin_dn, *rest):
    o_read, o_tok, o_g1, o_s1, o_q, o_k, o_v, o_out, o_g2, o_s2, o_up, o_dn, o_hop = rest[:13]
    v_q, v_k, v_v, v_out, v_up, v_dn, sems = rest[13:]
    moves = []

    def send(src, dst):
        moves.append(pltpu.make_async_copy(src, dst, sems.at[len(moves)]))
        moves[-1].start()

    send(gtok, o_tok)
    send(readout, o_read)
    v_up[...] = fin_up[...].astype(F32)
    send(v_up, o_up)
    v_dn[...] = fin_dn[...].astype(F32)
    send(v_dn, o_dn)
    qw = o_q.shape[1]
    for i, (x, o) in enumerate(((v_q, o_q), (v_k, o_k), (v_v, o_v))):
        x[...] = fin_in[:, i * qw : (i + 1) * qw].astype(F32)
        send(x, o)
    v_out[...] = fin_out[...].astype(F32)
    send(v_out, o_out)
    width = small.shape[1]
    for i, o in enumerate((o_g1, o_s1, o_g2, o_s2, o_hop)):
        o[...] = small[i : i + 1, :].reshape(width)
    for cp in moves:
        cp.wait()


def shards(
    nn,
    tokens,
    hop_mask,
    graph_ids,
    norm1_gain,
    norm1_shift,
    w_query,
    w_key,
    w_value,
    w_out,
    norm2_gain,
    norm2_shift,
    w_up,
    w_down,
    hop_weight,
    cotangent,
):
    rows, width = tokens.shape
    nodes = rows // HOPS
    qw, uw = w_query.shape[1], w_up.shape[1]
    vm = pl.BlockSpec(memory_space=pltpu.VMEM)
    hbm = pl.BlockSpec(memory_space=pl.ANY)
    extra = len([b for b in range(3, 12) if (1 << b) < nn])

    def v(*shape, dtype=BF16):
        return pltpu.VMEM(shape, dtype)

    tiles, chunks = rows // TILE, rows // CHUNK
    half = width // 2
    more = max(2 * extra, 1)
    scratch = [
        v(tiles, TILE, dtype=jnp.int32),
        v(1, nodes, dtype=jnp.int32),
        v(width),
        v(width),
        v(width),
        v(width),
        v(width),
        v(width, 12 * qw),
        v(width, 4 * uw),
        v(4, qw, width),
        v(4, uw, width),
        v(rows, width),
        v(nodes, width),
        v(rows, width),
        v(rows, 12 * qw),
        v(tiles * 8, HOPS, TILE, dtype=F32),
        v(rows, width),
        v(rows, width, dtype=F32),
        v(rows, width),
        v(rows, 4 * uw),
        v(rows, 4 * uw),
        v(rows, width, dtype=F32),
        v(TILE, TILE),
        v(2 * TILE, TILE),
        v(width, rows),
        v(width, rows),
        v(width, rows),
        v(rows, TILE, dtype=F32),
        v(tiles, HOPS, TILE, dtype=F32),
        v(rows, TILE, dtype=F32),
        v(rows, TILE, dtype=F32),
        v(rows, TILE, dtype=F32),
        v(chunks, TILE, 4 * uw),
        v(nodes + 16, 4 * uw),
        v(rows, TILE),
        v(rows, 4 * uw),
        v(rows, width, dtype=F32),
        v(rows, width),
        v(rows, width),
        v(rows, 12 * qw),
        v(width, 4 * uw),
        v(4, uw, width),
        v(4, qw, width),
        v(width, 12 * qw),
        v(half, 4 * uw),
        v(4, uw // 2, width),
        v(4, qw // 2, width),
        v(4, half, 3 * qw),
        v(3, half // 4, 4 * uw),
        v(3, uw // 8, width),
        v(3, 4, qw // 8, width),
        v(4, 3, half // 4, 3 * qw),
        v(3, half // 4, uw),
        v(3, uw // 2, width),
        v(3, qw // 8, width),
        v(3, half // 4, 3 * qw),
        v(more, half // 4, uw),
        v(more, uw // 8, width),
        v(more, qw // 8, width),
        v(more, half // 4, 3 * qw),
        v(2 + extra, HOPS, TILE, dtype=F32),
        v(7 + extra, HOPS, TILE, dtype=F32),
        v(3, HOPS, TILE, dtype=F32),
        v(2 + extra, 8, width, dtype=F32),
        v(7 + extra, 8, width, dtype=F32),
        v(3, 8, width, dtype=F32),
        pltpu.SemaphoreType.DMA((15,)),
        pltpu.SemaphoreType.DMA((48,)),
        pltpu.SemaphoreType.DMA((48,)),
        pltpu.SemaphoreType.DMA((7 * (15 + extra),)),
        pltpu.SemaphoreType.DMA((7 * (15 + extra),)),
        pltpu.SemaphoreType.DMA((10 + extra,)),
        pltpu.SemaphoreType.DMA((10 + extra,)),
        pltpu.SemaphoreType.DMA((10 + extra,)),
        pltpu.SemaphoreType.DMA((10 + extra,)),
    ]
    outs = [
        pltpu.VMEM((nodes, width), BF16),
        pltpu.VMEM((rows, width), BF16),
        pltpu.VMEM((8, width), F32),
        pltpu.VMEM((width, 3 * qw), BF16),
        pltpu.VMEM((qw, width), BF16),
        pltpu.VMEM((width, uw), BF16),
        pltpu.VMEM((uw, width), BF16),
    ]
    readout, gtok, small, fin_in, fin_out, fin_up, fin_dn = pl.pallas_call(
        functools.partial(kernel, nn),
        out_shape=outs,
        in_specs=[hbm] * 15,
        out_specs=[vm] * 7,
        scratch_shapes=scratch,
        compiler_params=pltpu.CompilerParams(
            collective_id=0, has_side_effects=True, vmem_limit_bytes=56 * 1024 * 1024
        ),
        name="layer",
    )(
        tokens,
        hop_mask.reshape(tiles, TILE),
        graph_ids.reshape(1, nodes),
        norm1_gain,
        norm1_shift,
        w_query,
        w_key,
        w_value,
        w_out,
        norm2_gain,
        norm2_shift,
        w_up,
        w_down,
        hop_weight,
        cotangent,
    )
    line = jax.ShapeDtypeStruct((width,), F32)
    square = jax.ShapeDtypeStruct((width, qw), F32)
    return pl.pallas_call(
        results_kernel,
        out_shape=[
            jax.ShapeDtypeStruct((nodes, width), BF16),
            jax.ShapeDtypeStruct((rows, width), BF16),
            line,
            line,
            square,
            square,
            square,
            jax.ShapeDtypeStruct((qw, width), F32),
            line,
            line,
            jax.ShapeDtypeStruct((width, uw), F32),
            jax.ShapeDtypeStruct((uw, width), F32),
            line,
        ],
        in_specs=[vm] * 7,
        out_specs=[hbm, hbm, vm, vm, hbm, hbm, hbm, hbm, vm, vm, hbm, hbm, vm],
        scratch_shapes=[v(width, qw, dtype=F32)] * 3
        + [
            v(qw, width, dtype=F32),
            v(width, uw, dtype=F32),
            v(uw, width, dtype=F32),
            pltpu.SemaphoreType.DMA((8,)),
        ],
        compiler_params=pltpu.CompilerParams(vmem_limit_bytes=16 * 1024 * 1024),
        name="results",
    )(readout, gtok, small, fin_in, fin_out, fin_up, fin_dn)


def solution(mesh):
    spread = P(("nodes", "tp"), None)
    flat = P(("nodes", "tp"))
    cols, rows = P(None, "tp"), P("tp", None)
    return jax.shard_map(
        functools.partial(shards, mesh.shape["nodes"]),
        mesh=mesh,
        in_specs=(spread, flat, flat, P(), P(), cols, cols, cols, rows, P(), P(), cols, rows, P(), spread),
        out_specs=(spread, spread, P(), P(), cols, cols, cols, rows, P(), P(), cols, rows, P()),
        check_vma=False,
    )
```

```python
import functools

import jax
import jax.numpy as jnp
from jax import lax
from jax.experimental import pallas as pl
from jax.experimental.pallas import tpu as pltpu
from jax.sharding import PartitionSpec as P

HOPS = 8
HEAD = 64
GRAPHS = 64
EPSILON = 1e-05
NEGATIVE = -1000000000.0
MESH = pl.DeviceIdType.MESH
F32 = jnp.float32
BF16 = jnp.bfloat16
CHUNK = 256
WIDE = 512
TILE = 128


def mm(a, b):
    return lax.dot_general(a, b, (((1,), (0,)), ((), ())), preferred_element_type=F32)


def mm_rt(a, b):
    return lax.dot_general(a, b, (((1,), (1,)), ((), ())), preferred_element_type=F32)


def mm_lt(a, b):
    return lax.dot_general(a, b, (((0,), (0,)), ((), ())), preferred_element_type=F32)


def iota(shape, axis):
    return lax.broadcasted_iota(jnp.int32, shape, axis)


def centred(values):
    centre = values - jnp.mean(values, axis=-1, keepdims=True)
    spread = jnp.mean(centre * centre, axis=-1, keepdims=True)
    return centre * lax.rsqrt(spread + EPSILON), lax.rsqrt(spread + EPSILON)


def gelu_both(x):
    phi = 0.5 + 0.5 * lax.erf(x * 0.7071067811865476)
    bell = jnp.exp2((-0.5 * 1.4426950408889634) * (x * x))
    return x * phi, phi + x * (bell * 0.3989422804014327)


def tokens_of(ref):
    return ref[...].astype(F32).reshape(1, ref.shape[0])


class Group:
    def __init__(self, array, wide, cols, recv_core, recv_plane, recv_z, final, more, send, recv, base):
        self.array, self.wide = array, wide
        self.cols = cols
        self.recv_core, self.recv_plane, self.recv_z = recv_core, recv_plane, recv_z
        self.final = final
        self.more = more
        self.send, self.recv, self.base = send, recv, base
        rows = final.shape[0]
        self.half_rows = rows // 2
        self.piece_rows = rows // 8
        self.width = final.shape[1]

    def sems(self, k):
        return self.send.at[self.base + k], self.recv.at[self.base + k]

    def rows(self, c, p=None):
        if p is None:
            return pl.ds(pl.multiple_of(c * self.half_rows, 16), self.half_rows)
        return pl.ds(pl.multiple_of(c * self.half_rows + p * self.piece_rows, 16), self.piece_rows)

    def block(self, rows):
        if self.wide:
            return self.array.at[rows, self.cols[0] * self.width : self.cols[1] * self.width]
        return self.array.at[:, rows]

    def slot(self, rows, d):
        if self.wide:
            return self.array.at[rows, d * self.width : (d + 1) * self.width]
        return self.array.at[d, rows]


def kernel(
    nn,
    tok_hbm,
    mask_ref,
    gid_ref,
    g1_ref,
    s1_ref,
    wq_hbm,
    wk_hbm,
    wv_hbm,
    wo_hbm,
    g2_ref,
    s2_ref,
    wu_hbm,
    wd_hbm,
    hw_ref,
    cot_hbm,
    readout_ref,
    gtok_ref,
    small_ref,
    fin_in_ref,
    wide_out_ref,
    wide_up_ref,
    wide_dn_ref,
    fin_out_ref,
    fin_up_ref,
    fin_dn_ref,
    mask_v,
    gid_v,
    g1_v,
    s1_v,
    g2_v,
    s2_v,
    hw_v,
    w_in,
    w_up,
    w_ot,
    w_dn,
    tok,
    cot,
    n1,
    qkv,
    pn,
    ctx,
    res,
    n2,
    act,
    gp,
    lay,
    emask,
    pmask,
    n1t,
    n2t,
    ctxt,
    vcol,
    mt,
    gexp,
    wcol,
    dcol,
    ab,
    zed,
    mixes,
    gbef,
    gl,
    datt,
    dctx,
    dqkv,
    g_up,
    g_dn,
    g_out,
    g_in,
    rc_up,
    rc_dn,
    rc_out,
    rc_in,
    rp_up,
    rp_dn,
    rp_out,
    rp_in,
    rz_up,
    rz_dn,
    rz_out,
    rz_in,
    mo_up,
    mo_dn,
    mo_out,
    mo_in,
    ar_one,
    ar_nodes,
    ar_tp,
    sv_one,
    sv_nodes,
    sv_tp,
    lsem,
    wsend,
    wrecv,
    gsend,
    grecv,
    asend,
    arecv,
    bsend,
    brecv,
):
    n, t = lax.axis_index("nodes"), lax.axis_index("tp")
    rows_here, width = tok.shape
    chunks = rows_here // CHUNK
    wides = rows_here // WIDE
    tiles = rows_here // TILE
    c = n % 2
    plane = (n // 2) % 4
    eighth = 4 * c + plane
    extra = [b for b in range(3, 12) if (1 << b) < nn]

    def node_peer(k):
        out = n
        for b in range(12):
            if (k >> b) & 1:
                bit = (n // (1 << b)) % 2
                out = out + (1 << b) * (1 - 2 * bit)
        return (out, t)

    def tp_peer(k):
        out = t
        for b in range(2):
            if (k >> b) & 1:
                bit = (t // (1 << b)) % 2
                out = out + (1 << b) * (1 - 2 * bit)
        return (n, out)

    def remote(src, dst, ssem, rsem, peer):
        return pltpu.make_async_remote_copy(
            src_ref=src, dst_ref=dst, send_sem=ssem, recv_sem=rsem, device_id=peer, device_id_type=MESH
        )

    qw = wq_hbm.shape[1]
    local = [
        pltpu.make_async_copy(wq_hbm, w_in.at[:, 0:qw], lsem.at[0]),
        pltpu.make_async_copy(wk_hbm, w_in.at[:, qw : 2 * qw], lsem.at[1]),
        pltpu.make_async_copy(wv_hbm, w_in.at[:, 2 * qw : 3 * qw], lsem.at[2]),
        pltpu.make_async_copy(tok_hbm, tok, lsem.at[3]),
        pltpu.make_async_copy(wo_hbm, w_ot.at[0], lsem.at[4]),
        pltpu.make_async_copy(wd_hbm, w_dn.at[0], lsem.at[5]),
        pltpu.make_async_copy(wu_hbm, w_up.at[:, 0 : wu_hbm.shape[1]], lsem.at[6]),
        pltpu.make_async_copy(cot_hbm, cot, lsem.at[7]),
    ]
    tiny = ((mask_ref, mask_v), (gid_ref, gid_v), (g1_ref, g1_v), (s1_ref, s1_v), (g2_ref, g2_v), (s2_ref, s2_v))
    for i, (src, dst) in enumerate(tiny + ((hw_ref, hw_v),)):
        local.append(pltpu.make_async_copy(src, dst, lsem.at[8 + i]))
    for copy in local:
        copy.start()

    barrier = pltpu.get_barrier_semaphore()
    greet = [node_peer(k) for k in range(1, 8)] + [node_peer(1 << b) for b in extra]
    greet += [tp_peer(k) for k in range(1, 4)]
    for peer in greet:
        pl.semaphore_signal(barrier, inc=1, device_id=peer, device_id_type=MESH)
    pl.semaphore_wait(barrier, len(greet))

    def plane_of(e):
        out = plane
        for b in range(2):
            if (e >> b) & 1:
                out = out + (1 << b) * (1 - 2 * ((plane // (1 << b)) % 2))
        return out

    def weight_block(ref, off, size, d0, d1):
        rows = pl.ds(pl.multiple_of(off, 16), size)
        if len(ref.shape) == 3:
            return ref.at[d0:d1, rows]
        w = ref.shape[1] // 4
        return ref.at[rows, d0 * w : d1 * w]

    class Fetch:
        def __init__(self, ref, slots, base, relay=False):
            total = ref.shape[1] if len(ref.shape) == 3 else ref.shape[0]
            d0, d1 = slots
            sems = iter(range(base, base + 8))

            def go(src, dst, peer):
                k = next(sems)
                return remote(src, dst, wsend.at[k], wrecv.at[k], peer)

            def rows(off, size):
                return weight_block(ref, off, size, d0, d1)

            part = total // 8
            own = eighth * part
            self.z = [
                go(weight_block(ref, own, part, 0, 1), weight_block(ref, own, part, d, d + 1), tp_peer(d))
                for d in range(d0, d1)
            ]
            self.more = []
            lots = [rows(c * (total // 2), total // 2)]
            if relay:
                self.plane = [go(rows(own, part), rows(own, part), node_peer(2 << e)) for e in range(2)]
                for e in range(2):
                    got = rows((4 * c + plane_of(1 << e)) * part + e * (part // 2), part // 2)
                    self.more.append(go(got, got, node_peer(4 >> e)))
            else:
                self.plane = [go(rows(own, part), rows(own, part), node_peer(2 * e)) for e in (1, 2, 3)]
            self.core = [go(x, x, node_peer(1)) for x in lots]

        def start_z(self):
            for cp in self.z:
                cp.start()

        def start_plane(self):
            for cp in self.z:
                cp.wait()
            for cp in self.plane:
                cp.start()

        def start_relay(self):
            for cp in self.plane:
                cp.wait()
            for cp in self.more:
                cp.start()

        def start_core(self):
            for cp in self.more or self.plane:
                cp.wait()
            for cp in self.core:
                cp.start()

        def end(self):
            for cp in self.core:
                cp.wait()

    fetch_in = [None] + [Fetch(w_in, (d, d + 1), 8 * (d - 1)) for d in (1, 2, 3)]
    fetch_ot = Fetch(w_ot, (1, 4), 24)
    fetch_up = Fetch(w_up, (1, 4), 32)
    fetch_dn = Fetch(w_dn, (1, 4), 40)

    for i in (0, 1, 2):
        local[i].wait()
    for d in (1, 2, 3):
        fetch_in[d].start_z()

    for i in range(8, 15):
        local[i].wait()
    gain1 = tokens_of(g1_v)
    shift1 = tokens_of(s1_v)
    gain2 = tokens_of(g2_v)
    shift2 = tokens_of(s2_v)
    hopw = tokens_of(hw_v)
    hop16 = jnp.broadcast_to(hopw, (16, width)).astype(BF16)

    eye = iota((TILE, TILE), 0) == iota((TILE, TILE), 1)
    ones = jnp.ones((TILE, TILE), BF16)
    lane8 = iota((HOPS, TILE), 1)
    block8 = lane8 // HOPS
    eye16 = eye.astype(F32).astype(BF16)
    emask[...] = (iota((TILE, TILE), 0) // HOPS == iota((TILE, TILE), 1) // HOPS).astype(F32).astype(BF16)
    first = (iota((2 * TILE, TILE), 0) < TILE) == (iota((2 * TILE, TILE), 1) < HEAD)
    pmask[...] = first.astype(F32).astype(BF16)
    nodes_chunk = CHUNK // HOPS
    spread_c = (iota((CHUNK, nodes_chunk), 0) // HOPS == iota((CHUNK, nodes_chunk), 1)).astype(F32).astype(BF16)

    def rows_of(i, size):
        return pl.ds(pl.multiple_of(i * size, size), size)

    mask_f = mask_v[...].astype(F32)
    for i in range(tiles):
        col = mm(jnp.where(eye, mask_f[i : i + 1, :], 0.0).astype(BF16), ones)
        vcol[i * TILE : (i + 1) * TILE, :] = col
        acc = jnp.zeros((HOPS, TILE), F32)
        col3 = col.reshape(TILE // HOPS, HOPS, TILE)
        for r in range(TILE // HOPS):
            acc = jnp.where(block8 == r, col3[r], acc)
        mt[i] = acc

    local[3].wait()

    def norm_one(i, carry):
        x = tok[rows_of(i, CHUNK), :].astype(F32)
        hat, _ = centred(x)
        n1[rows_of(i, CHUNK), :] = (hat * gain1 + shift1).astype(BF16)
        return carry

    lax.fori_loop(0, chunks, norm_one, 0)

    def project(d, lo, hi):
        base = d * 3 * qw

        def step(i, carry):
            r = rows_of(i, WIDE)
            out = mm(n1[r, :], w_in[:, base : base + 3 * qw])
            qkv[r, base : base + qw] = (out[:, 0:qw] * (HEAD**-0.5)).astype(BF16)
            qkv[r, base + qw : base + 3 * qw] = out[:, qw:].astype(BF16)
            return carry

        lax.fori_loop(lo, hi, step, 0)

    def pair(x):
        return jnp.concatenate([x, x], axis=0) * pmask[...]

    bits = [((lane8 // (HOPS << b)) % 2) == 1 for b in range(4)]

    def compact(x):
        out = []
        for h in range(2):
            x3 = x[:, h * TILE : (h + 1) * TILE].reshape(TILE // HOPS, HOPS, TILE)
            parts = [x3[r] for r in range(TILE // HOPS)]
            for b in range(4):
                parts = [jnp.where(bits[b], parts[2 * m + 1], parts[2 * m]) for m in range(len(parts) // 2)]
            out.append(parts[0])
        return out

    def expand(x):
        twice = jnp.concatenate([x, x], axis=0).astype(BF16)
        return jnp.concatenate([twice] * (TILE // 16), axis=0) * emask[...]

    together = 8

    steps = tiles // together
    mid = steps // 2

    def attend(d, lo, hi):
        base = d * 3 * qw

        def step(i, carry):
            at = [i * together + m for m in range(together)]
            rs = [rows_of(a, TILE) for a in at]
            q2 = [pair(qkv[r, base : base + qw]) for r in rs]
            scores = [compact(mm_rt(qkv[r, base + qw : base + 2 * qw], x)) for r, x in zip(rs, q2, strict=True)]
            wide = []
            for m, a in enumerate(at):
                keep = mt[a] > 0.5
                for h in range(2):
                    wide.append(jnp.where(keep, scores[m][h], NEGATIVE))
            peaks = [jnp.max(x, axis=0, keepdims=True) for x in wide]
            wide = [jnp.exp(x - y) for x, y in zip(wide, peaks, strict=True)]
            totals = [jnp.sum(x, axis=0, keepdims=True) for x in wide]
            wide = [x / y for x, y in zip(wide, totals, strict=True)]
            for m, a in enumerate(at):
                for h in range(2):
                    pn[a * 8 + 2 * d + h] = wide[2 * m + h]
            turned = [
                mm_rt(eye16, jnp.concatenate([expand(wide[2 * m]), expand(wide[2 * m + 1])], axis=0)).astype(BF16)
                for m in range(together)
            ]
            v2 = [pair(qkv[r, base + 2 * qw : base + 3 * qw]) for r in rs]
            for m, r in enumerate(rs):
                ctx[r, d * qw : (d + 1) * qw] = mm(turned[m], v2[m]).astype(BF16)
            return carry

        lax.fori_loop(lo, hi, step, 0)

    gcol = mm(jnp.where(eye, gid_v[...].astype(F32), 0.0).astype(BF16), ones).astype(BF16)
    for i in range(chunks):
        gexp[i * CHUNK : (i + 1) * CHUNK, :] = mm(spread_c, gcol[i * nodes_chunk : (i + 1) * nodes_chunk])
    fetch_in[1].start_plane()
    project(0, 0, wides // 2)
    fetch_in[2].start_plane()
    project(0, wides // 2, wides)
    fetch_in[3].start_plane()
    for i in (4, 5, 6, 7):
        local[i].wait()
    fetch_ot.start_z()
    fetch_up.start_z()
    fetch_dn.start_z()
    attend(0, 0, steps)
    fetch_ot.start_plane()
    fetch_in[1].start_core()
    fetch_up.start_plane()
    fetch_in[1].end()
    fetch_in[2].start_core()
    project(1, 0, wides)
    fetch_in[3].start_core()
    attend(1, 0, steps)
    fetch_dn.start_plane()
    fetch_in[2].end()
    project(2, 0, wides)
    fetch_ot.start_core()
    attend(2, 0, steps)
    fetch_in[3].end()
    project(3, 0, wides)
    attend(3, 0, steps)
    fetch_ot.end()

    def w_out():
        return w_ot[...].reshape(4 * qw, width)

    def w_down():
        return w_dn[...].reshape(4 * w_dn.shape[1], width)

    hop3 = iota((nodes_chunk, HOPS, TILE), 1)
    lane3 = iota((nodes_chunk, HOPS, TILE), 2)
    node3 = iota((nodes_chunk, HOPS, TILE), 0)
    lane_graph = (lane3 % GRAPHS).astype(F32)

    def feed_norm(i, carry):
        r = rows_of(i, WIDE)
        x = tok[r, :].astype(F32) + mm(ctx[r, :], w_out())
        res[r, :] = x
        hat, _ = centred(x)
        n2[r, :] = (hat * gain2 + shift2).astype(BF16)
        return carry

    uw = wu_hbm.shape[1]

    def feed_up(lo, hi):
        cols = slice(lo * uw, hi * uw)

        def step(i, carry):
            r = rows_of(i, WIDE)
            value, slope = gelu_both(mm(n2[r, :], w_up[:, cols]))
            act[r, cols] = value.astype(BF16)
            gp[r, cols] = slope.astype(BF16)
            return carry

        return step

    def feed_down(i, acc):
        r = rows_of(i, WIDE)
        lay[r, :] = res[r, :] + mm(act[r, :], w_down())
        for m in range(WIDE // CHUNK):
            acc = hops(i * (WIDE // CHUNK) + m, acc)
        return acc

    def hops(i, acc):
        r = rows_of(i, CHUNK)
        out = lay[r, :]
        dr = mm(spread_c, cot[rows_of(i, nodes_chunk), :])
        logit = jnp.sum(out * hopw, axis=-1, keepdims=True)
        gcoef = jnp.sum(out * dr, axis=-1, keepdims=True)
        shape = (nodes_chunk, HOPS, TILE)
        valid = vcol[r, :].reshape(shape)
        valid = jnp.where(hop3 > 0, valid, 0.0)
        logit = jnp.where(valid > 0.5, jnp.broadcast_to(logit, (CHUNK, TILE)).reshape(shape), NEGATIVE)
        e = jnp.exp(logit - jnp.max(logit, axis=1, keepdims=True))
        e = jnp.where(hop3 > 0, e, 0.0)
        weight = e / jnp.sum(e, axis=1, keepdims=True)
        direct = valid * jnp.broadcast_to(gcoef, (CHUNK, TILE)).reshape(shape)
        wcol[r, :] = weight.reshape(CHUNK, TILE)
        dcol[r, :] = direct.reshape(CHUNK, TILE)
        mine = gexp[r, :].reshape(shape) == lane_graph
        both = jnp.where(lane3 < GRAPHS, jnp.where(hop3 == 0, 1.0, weight), -direct)
        return acc + jnp.sum(jnp.where(mine, both, 0.0), axis=0)

    lax.fori_loop(0, wides, feed_norm, 0)
    fetch_up.start_core()
    lax.fori_loop(0, wides, feed_up(0, 1), 0)
    fetch_up.end()
    lax.fori_loop(0, wides // 2, feed_up(1, 4), 0)
    fetch_dn.start_core()
    lax.fori_loop(wides // 2, wides, feed_up(1, 4), 0)
    fetch_dn.end()
    sums = lax.fori_loop(0, wides, feed_down, jnp.zeros((HOPS, TILE), F32))

    def reduce_all(value, one, by_nodes, by_tp, ssem, rsem, overlap=None):
        one[0] = value
        copies = [
            remote(one.at[0], by_nodes.at[k - 1], ssem.at[k - 1], rsem.at[k - 1], node_peer(k)) for k in range(1, 8)
        ]
        for cp in copies:
            cp.start()
        if overlap is not None:
            overlap()
        for cp in copies:
            cp.wait()
        value = one[0]
        for k in range(7):
            value = value + by_nodes[k]
        at = 7
        for b in extra:
            one[at - 6] = value
            cp = remote(one.at[at - 6], by_nodes.at[at], ssem.at[at], rsem.at[at], node_peer(1 << b))
            cp.start()
            cp.wait()
            value = value + by_nodes[at]
            at += 1
        last = one.shape[0] - 1
        one[last] = value
        copies = [
            remote(one.at[last], by_tp.at[k - 1], ssem.at[at + k - 1], rsem.at[at + k - 1], tp_peer(k))
            for k in range(1, 4)
        ]
        for cp in copies:
            cp.start()
        return copies, lambda: one[last] + by_tp[0] + by_tp[1] + by_tp[2]

    def small_products():
        drdown = mm_rt(cot[...], w_down()).astype(BF16)
        hopdown = mm_rt(hop16, w_down()).astype(BF16)
        for i in range(chunks):
            piece = drdown[i * nodes_chunk : (i + 1) * nodes_chunk]
            ab[i, 0:nodes_chunk] = piece
            ab[i, nodes_chunk : 2 * nodes_chunk] = piece
            ab[i, 2 * nodes_chunk : 2 * nodes_chunk + 16] = hopdown
            ab[i, 2 * nodes_chunk + 16 :] = jnp.zeros((TILE - 2 * nodes_chunk - 16, ab.shape[2]), BF16)
        for i in range(chunks):
            at = slice(i * CHUNK, (i + 1) * CHUNK)
            for src, dst in ((n2, n2t), (ctx, ctxt), (n1, n1t)):
                dst[:, at] = src[at, :].T

    copies, total = reduce_all(sums, ar_one, ar_nodes, ar_tp, asend, arecv, small_products)
    for cp in copies:
        cp.wait()
    sums = total()
    row = jnp.broadcast_to(sums[0:1, :], (HOPS, TILE))
    counts = jnp.where(lane8 < GRAPHS, row, pltpu.roll(row, GRAPHS, 1))
    means = (sums / (counts + 1.0))[None]

    def back_one(i, carry):
        zed_acc = carry
        r = rows_of(i, CHUNK)
        shape = (nodes_chunk, HOPS, TILE)
        picked = jnp.where(gexp[r, :].reshape(shape) == lane_graph, means, 0.0)
        mean_r = jnp.sum(jnp.where(lane3 < GRAPHS, picked, 0.0), axis=-1, keepdims=True)
        grad_mean = jnp.sum(jnp.where(lane3 < GRAPHS, 0.0, picked), axis=-1, keepdims=True)
        weight = wcol[r, :].reshape(shape)
        valid = vcol[r, :].reshape(shape)
        coef = jnp.where(hop3 > 0, valid * (weight - mean_r), 1.0)
        grad_w = dcol[r, :].reshape(shape) + grad_mean
        glog = weight * (grad_w - jnp.sum(weight * grad_w, axis=1, keepdims=True))
        coef_hi = coef.astype(BF16).astype(F32)
        glog_hi = glog.astype(BF16).astype(F32)
        zero = jnp.zeros_like(coef)
        mix = jnp.where(lane3 == node3, coef_hi, zero)
        mix = jnp.where(lane3 == node3 + nodes_chunk, coef - coef_hi, mix)
        mix = jnp.where(lane3 == 2 * nodes_chunk, glog_hi, mix)
        mix = jnp.where(lane3 == 2 * nodes_chunk + 1, glog - glog_hi, mix)
        mix = mix.reshape(CHUNK, TILE).astype(BF16)

        mixes[r, :] = mix
        gbef[r, :] = (mm(mix, ab[i]) * gp[r, :].astype(F32)).astype(BF16)

        fold = mm_lt(mix, act[r, :])
        zed[rows_of(i, nodes_chunk), :] = (fold[0:nodes_chunk] + fold[nodes_chunk : 2 * nodes_chunk]).astype(BF16)
        zed_acc = zed_acc + fold[2 * nodes_chunk : 2 * nodes_chunk + 8]

        return zed_acc

    def back_norm(i, carry):
        gain_acc, shift_acc, hop_acc = carry
        r = rows_of(i, WIDE)
        hop_acc = layer_grads(i, hop_acc)
        dy = mm_rt(gbef[r, :], w_up[...])
        hat, inv = centred(res[r, :])
        gain_acc = gain_acc + jnp.sum((dy * hat).reshape(WIDE // HOPS, HOPS, width), axis=0)
        shift_acc = shift_acc + jnp.sum(dy.reshape(WIDE // HOPS, HOPS, width), axis=0)
        g = dy * gain2
        back = inv * (
            g - jnp.mean(g, axis=-1, keepdims=True) - hat * jnp.mean(g * hat, axis=-1, keepdims=True)
        )
        grad_res = gl[r, :] + back
        gl[r, :] = grad_res
        att = grad_res.astype(BF16)
        datt[r, :] = att
        dctx[r, :] = mm_rt(att, w_out()).astype(BF16)
        return gain_acc, shift_acc, hop_acc

    def layer_grads(wide, hop_acc):
        for m in range(WIDE // CHUNK):
            i = wide * (WIDE // CHUNK) + m
            r = rows_of(i, CHUNK)
            mix = mixes[r, :]
            dr = cot[rows_of(i, nodes_chunk), :]
            rest = jnp.zeros((TILE - 2 * nodes_chunk - 16, width), BF16)
            gl[r, :] = mm(mix, jnp.concatenate([dr, dr, hop16, rest], axis=0))
            seen = mm_lt(mix, lay[r, :].astype(BF16))
            both = seen[0:nodes_chunk] + seen[nodes_chunk : 2 * nodes_chunk]
            readout_ref[rows_of(i, nodes_chunk), :] = both.astype(BF16)
            hop_acc = hop_acc + seen[2 * nodes_chunk : 2 * nodes_chunk + 8]
        return hop_acc

    zero8 = jnp.zeros((HOPS, width), F32)
    zed_sum = lax.fori_loop(0, chunks, back_one, jnp.zeros((HOPS, zed.shape[1]), F32))

    def group(at, array, wide, cols, rc, rp, rz, final, more):
        return Group(array, wide, cols, rc, rp, rz, final, more, gsend, grecv, at * (15 + len(extra)))

    dn = group(0, g_dn, False, (0, 4), rc_dn, rp_dn, rz_dn, fin_dn_ref, mo_dn)
    up = group(1, g_up, True, (0, 4), rc_up, rp_up, rz_up, fin_up_ref, mo_up)
    ot = group(2, g_out, False, (0, 4), rc_out, rp_out, rz_out, fin_out_ref, mo_out)
    qk = [
        group(3 + d, g_in, True, (d, d + 1), rc_in.at[d], rp_in.at[d], rz_in, fin_in_ref, mo_in) for d in range(4)
    ]
    every = (1, 2, 3)

    def core_copy(g):
        s, r = g.sems(0)
        return remote(g.block(g.rows(1 - c)), g.recv_core, s, r, node_peer(1))

    def go_core(g):
        core_copy(g).start()

    def add_core(g):
        core_copy(g).wait()
        mine = g.block(g.rows(c))
        mine[...] = mine[...] + g.recv_core[...]

    def plane_copies(g):
        return [
            remote(g.block(g.rows(c, plane_of(e))), g.recv_plane.at[e - 1], *g.sems(e), node_peer(2 * e))
            for e in (1, 2, 3)
        ]

    def go_plane(g):
        add_core(g)
        for cp in plane_copies(g):
            cp.start()

    def cut(g, p, e):
        if g.wide:
            w = g.piece_rows // 2
            rows = pl.ds(pl.multiple_of(c * g.half_rows + p * g.piece_rows + e * w, 16), w)
            return g.array.at[rows, g.cols[0] * g.width : g.cols[1] * g.width]
        w = g.width // 2
        return g.array.at[:, g.rows(c, p), e * w : (e + 1) * w]

    def landing(g, m, e):
        if g.wide:
            w = g.piece_rows // 2
            return g.recv_plane.at[m, e * w : (e + 1) * w]
        w = g.width // 2
        return g.recv_plane.at[m, :, :, e * w : (e + 1) * w]

    def fold_copies(g):
        out = []
        for e in range(2):
            for m, far in enumerate((plane_of(1 << e), plane_of(3))):
                sems = g.sems(11 + 2 * e + m)
                out.append(remote(cut(g, far, e), landing(g, m, e), *sems, node_peer(2 << e)))
        return out

    def go_fold(g):
        add_core(g)
        for cp in fold_copies(g):
            cp.start()

    def fold_last(g):
        return [
            remote(cut(g, plane_of(2 >> e), e), landing(g, 2, e), *g.sems(1 + e), node_peer(4 >> e)) for e in range(2)
        ]

    def go_fold_last(g):
        for cp in fold_copies(g):
            cp.wait()
        for e in range(2):
            for m, keep in enumerate((plane, plane_of(2 >> e))):
                mine = cut(g, keep, e)
                mine[...] = mine[...] + landing(g, m, e)[...]
        for cp in fold_last(g):
            cp.start()

    def go_z_fold(g, slots):
        for cp in fold_last(g):
            cp.wait()
        mine = g.block(g.rows(c, plane))
        mine[...] = mine[...] + g.recv_plane[2]
        for cp in z_copies(g, slots):
            cp.start()

    def z_copies(g, slots):
        return [
            remote(g.slot(g.rows(c, plane), d), g.recv_z.at[d - 1], *g.sems(3 + d), tp_peer(d)) for d in slots
        ]

    def go_z(g, slots):
        for cp in plane_copies(g):
            cp.wait()
        mine = g.block(g.rows(c, plane))
        total = mine[...].astype(F32)
        for e in range(3):
            total = total + g.recv_plane[e].astype(F32)
        mine[...] = total.astype(BF16)
        for cp in z_copies(g, slots):
            cp.start()

    def z_first(g):
        return [remote(g.slot(g.rows(c), d), g.recv_z.at[d - 1], *g.sems(3 + d), tp_peer(d)) for d in every]

    def go_z_first(g):
        add_core(g)
        for cp in z_first(g):
            cp.start()

    def own_pieces(g):
        return [
            remote(g.slot(g.rows(c, plane_of(e)), 0), g.recv_plane.at[e - 1], *g.sems(e), node_peer(2 * e))
            for e in (1, 2, 3)
        ]

    def go_own_plane(g):
        for cp in z_first(g):
            cp.wait()
        mine = g.slot(g.rows(c), 0)
        total = mine[...].astype(F32)
        for d in range(3):
            total = total + g.recv_z[d].astype(F32)
        mine[...] = total.astype(BF16)
        for cp in own_pieces(g):
            cp.start()

    def go_own_final(g):
        for cp in own_pieces(g):
            cp.wait()
        total = g.slot(g.rows(c, plane), 0)[...].astype(F32)
        for e in range(3):
            total = total + g.recv_plane[e].astype(F32)
        share(g, total)

    def final_copies(g):
        mine = g.final.at[g.rows(c, plane)]
        return [remote(mine, mine, *g.sems(6 + e), node_peer(2 * e)) for e in (1, 2, 3)]

    def last_copy(g):
        mine = g.final.at[g.rows(c)]
        return remote(mine, mine, *g.sems(10), node_peer(1))

    def go_final(g, waits):
        for cp in waits:
            cp.wait()
        total = g.slot(g.rows(c, plane), 0)[...].astype(F32)
        for d in range(3):
            total = total + g.recv_z[d].astype(F32)
        share(g, total)

    def share(g, total):
        for j, b in enumerate(extra):
            g.more[2 * j] = total.astype(BF16)
            cp = remote(g.more.at[2 * j], g.more.at[2 * j + 1], *g.sems(15 + j), node_peer(1 << b))
            cp.start()
            cp.wait()
            total = total + g.more[2 * j + 1].astype(F32)
        g.final.at[g.rows(c, plane)][...] = total.astype(BF16)
        for cp in final_copies(g):
            cp.start()

    def go_last(g):
        for cp in final_copies(g):
            cp.wait()
        last_copy(g).start()

    def finish(g):
        last_copy(g).wait()

    zed[rows_here // HOPS :, :] = jnp.concatenate([zed_sum, jnp.zeros_like(zed_sum)], axis=0).astype(BF16)
    drh = jnp.concatenate([cot[...], hop16], axis=0)
    g_dn[...] = mm_lt(zed[...], drh).astype(BF16).reshape(g_dn.shape)
    go_core(dn)
    g_up[...] = mm(n2t[...], gbef[...]).astype(BF16)
    go_core(up)
    norm_sums = lax.fori_loop(0, wides // 2, back_norm, (zero8, zero8, zero8))
    go_z_first(dn)
    gain_two, shift_two, hop_sum = lax.fori_loop(wides // 2, wides, back_norm, norm_sums)
    go_fold(up)
    g_out[...] = mm(ctxt[...], datt[...]).astype(BF16).reshape(g_out.shape)
    go_core(ot)

    def attend_back(d):
        base = d * 3 * qw

        def step(i, carry):
            at = [i * together + m for m in range(together)]
            rs = [rows_of(a, TILE) for a in at]
            do2 = [pair(dctx[r, d * qw : (d + 1) * qw]) for r in rs]
            grads = [
                compact(mm_rt(qkv[r, base + 2 * qw : base + 3 * qw], x)) for r, x in zip(rs, do2, strict=True)
            ]
            probs = [[pn[a * 8 + 2 * d + h] for h in range(2)] for a in at]
            probs_wide = [jnp.concatenate([expand(p) for p in ps], axis=1) for ps in probs]
            for m, r in enumerate(rs):
                dqkv[r, base + 2 * qw : base + 3 * qw] = mm(probs_wide[m], do2[m]).astype(BF16)
            inner = [[jnp.sum(p * g, axis=0, keepdims=True) for p, g in zip(*x, strict=True)] for x in zip(probs, grads, strict=True)]
            back = [
                [expand(probs[m][h] * (grads[m][h] - inner[m][h])) for h in range(2)] for m in range(together)
            ]
            q2 = [pair(qkv[r, base : base + qw]) for r in rs]
            for m, r in enumerate(rs):
                wide = jnp.concatenate(back[m], axis=1)
                dqkv[r, base + qw : base + 2 * qw] = mm(wide, q2[m]).astype(BF16)
            turned = [mm_rt(eye16, jnp.concatenate(x, axis=0)).astype(BF16) for x in back]
            k2 = [pair(qkv[r, base + qw : base + 2 * qw]) for r in rs]
            for m, r in enumerate(rs):
                dqkv[r, base : base + qw] = (mm(turned[m], k2[m]) * (HEAD**-0.5)).astype(BF16)
            return carry

        lax.fori_loop(0, tiles // together, step, 0)
        g_in[:, base : base + 3 * qw] = mm(n1t[...], dqkv[:, base : base + 3 * qw]).astype(BF16)
        go_core(qk[d])

    def back_two(i, carry):
        gain_acc, shift_acc = carry
        r = rows_of(i, WIDE)
        dy = mm_rt(dqkv[r, :], w_in[...])
        hat, inv = centred(tok[r, :].astype(F32))
        gain_acc = gain_acc + jnp.sum((dy * hat).reshape(WIDE // HOPS, HOPS, width), axis=0)
        shift_acc = shift_acc + jnp.sum(dy.reshape(WIDE // HOPS, HOPS, width), axis=0)
        g = dy * gain1
        back = inv * (
            g - jnp.mean(g, axis=-1, keepdims=True) - hat * jnp.mean(g * hat, axis=-1, keepdims=True)
        )
        gtok_ref[r, :] = (gl[r, :] + back).astype(BF16)
        return gain_acc, shift_acc

    attend_back(3)
    go_fold(ot)
    attend_back(2)
    go_fold(qk[3])
    go_fold_last(up)
    attend_back(1)
    go_fold(qk[2])
    go_fold_last(ot)
    attend_back(0)
    go_plane(qk[1])
    go_z_fold(up, every)
    go_fold_last(qk[3])
    norm_sums = lax.fori_loop(0, wides // 2, back_two, (zero8, zero8))
    go_plane(qk[0])
    go_z_fold(ot, every)
    go_fold_last(qk[2])
    go_own_plane(dn)
    go_z_fold(qk[3], (3,))
    gain_one, shift_one = lax.fori_loop(wides // 2, wides, back_two, norm_sums)
    go_z(qk[1], (1,))
    go_z_fold(qk[2], (2,))

    def fold8(x):
        return jnp.sum(x, axis=0, keepdims=True)

    small = jnp.concatenate(
        [fold8(gain_one), fold8(shift_one), fold8(gain_two), fold8(shift_two), fold8(hop_sum[0:2]), zero8[0:3]], axis=0
    )

    def rest_of():
        go_final(up, z_copies(up, every))
        go_final(ot, z_copies(ot, every))
        go_own_final(dn)
        go_z(qk[0], ())
        go_final(qk[0], [z_copies(qk[d], (d,))[0] for d in every])

    copies, total_small = reduce_all(small, sv_one, sv_nodes, sv_tp, bsend, brecv, rest_of)
    go_last(up)
    go_last(dn)
    go_last(ot)
    go_last(qk[0])
    for g, wide in ((dn, wide_dn_ref), (up, wide_up_ref), (ot, wide_out_ref)):
        finish(g)
        wide[...] = g.final[...].astype(F32)
    for cp in copies:
        cp.wait()
    small_ref[...] = total_small()
    finish(qk[0])


def results_kernel(readout, gtok, small, fin_in, fin_out, fin_up, fin_dn, *rest):
    o_read, o_tok, o_g1, o_s1, o_q, o_k, o_v, o_out, o_g2, o_s2, o_up, o_dn, o_hop = rest[:13]
    v_q, v_k, v_v, *lines, sems = rest[13:]
    moves = []

    def send(src, dst):
        moves.append(pltpu.make_async_copy(src, dst, sems.at[len(moves)]))
        moves[-1].start()

    send(gtok, o_tok)
    send(readout, o_read)
    send(fin_up, o_up)
    send(fin_dn, o_dn)
    send(fin_out, o_out)
    qw = o_q.shape[1]
    for i, (x, o) in enumerate(((v_q, o_q), (v_k, o_k), (v_v, o_v))):
        x[...] = fin_in[:, i * qw : (i + 1) * qw].astype(F32)
        send(x, o)
    width = small.shape[1]
    for i, (x, o) in enumerate(zip(lines, (o_g1, o_s1, o_g2, o_s2, o_hop), strict=True)):
        x[...] = small[i : i + 1, :].reshape(width)
        send(x, o)
    for cp in moves:
        cp.wait()


def shards(
    nn,
    tokens,
    hop_mask,
    graph_ids,
    norm1_gain,
    norm1_shift,
    w_query,
    w_key,
    w_value,
    w_out,
    norm2_gain,
    norm2_shift,
    w_up,
    w_down,
    hop_weight,
    cotangent,
):
    rows, width = tokens.shape
    nodes = rows // HOPS
    qw, uw = w_query.shape[1], w_up.shape[1]
    vm = pl.BlockSpec(memory_space=pltpu.VMEM)
    hbm = pl.BlockSpec(memory_space=pl.ANY)
    extra = len([b for b in range(3, 12) if (1 << b) < nn])

    def v(*shape, dtype=BF16):
        return pltpu.VMEM(shape, dtype)

    tiles, chunks = rows // TILE, rows // CHUNK
    half = width // 2
    more = max(2 * extra, 1)
    scratch = [
        v(qw, width),
        v(width, uw),
        v(uw, width),
        v(tiles, TILE, dtype=jnp.int32),
        v(1, nodes, dtype=jnp.int32),
        v(width),
        v(width),
        v(width),
        v(width),
        v(width),
        v(width, 12 * qw),
        v(width, 4 * uw),
        v(4, qw, width),
        v(4, uw, width),
        v(rows, width),
        v(nodes, width),
        v(rows, width),
        v(rows, 12 * qw),
        v(tiles * 8, HOPS, TILE, dtype=F32),
        v(rows, width),
        v(rows, width, dtype=F32),
        v(rows, width),
        v(rows, 4 * uw),
        v(rows, 4 * uw),
        v(rows, width, dtype=F32),
        v(TILE, TILE),
        v(2 * TILE, TILE),
        v(width, rows),
        v(width, rows),
        v(width, rows),
        v(rows, TILE, dtype=F32),
        v(tiles, HOPS, TILE, dtype=F32),
        v(rows, TILE, dtype=F32),
        v(rows, TILE, dtype=F32),
        v(rows, TILE, dtype=F32),
        v(chunks, TILE, 4 * uw),
        v(nodes + 16, 4 * uw),
        v(rows, TILE),
        v(rows, 4 * uw),
        v(rows, width, dtype=F32),
        v(rows, width),
        v(rows, width),
        v(rows, 12 * qw),
        v(width, 4 * uw),
        v(4, uw, width),
        v(4, qw, width),
        v(width, 12 * qw),
        v(half, 4 * uw),
        v(4, uw // 2, width),
        v(4, qw // 2, width),
        v(4, half, 3 * qw),
        v(3, half // 4, 4 * uw),
        v(3, uw // 8, width),
        v(3, 4, qw // 8, width),
        v(4, 3, half // 4, 3 * qw),
        v(3, half // 4, uw),
        v(3, uw // 2, width),
        v(3, qw // 8, width),
        v(3, half // 4, 3 * qw),
        v(more, half // 4, uw),
        v(more, uw // 8, width),
        v(more, qw // 8, width),
        v(more, half // 4, 3 * qw),
        v(2 + extra, HOPS, TILE, dtype=F32),
        v(7 + extra, HOPS, TILE, dtype=F32),
        v(3, HOPS, TILE, dtype=F32),
        v(2 + extra, 8, width, dtype=F32),
        v(7 + extra, 8, width, dtype=F32),
        v(3, 8, width, dtype=F32),
        pltpu.SemaphoreType.DMA((15,)),
        pltpu.SemaphoreType.DMA((48,)),
        pltpu.SemaphoreType.DMA((48,)),
        pltpu.SemaphoreType.DMA((7 * (15 + extra),)),
        pltpu.SemaphoreType.DMA((7 * (15 + extra),)),
        pltpu.SemaphoreType.DMA((10 + extra,)),
        pltpu.SemaphoreType.DMA((10 + extra,)),
        pltpu.SemaphoreType.DMA((10 + extra,)),
        pltpu.SemaphoreType.DMA((10 + extra,)),
    ]
    outs = [
        pltpu.VMEM((nodes, width), BF16),
        pltpu.VMEM((rows, width), BF16),
        pltpu.VMEM((8, width), F32),
        pltpu.VMEM((width, 3 * qw), BF16),
        pltpu.VMEM((qw, width), F32),
        pltpu.VMEM((width, uw), F32),
        pltpu.VMEM((uw, width), F32),
    ]
    readout, gtok, small, fin_in, fin_out, fin_up, fin_dn = pl.pallas_call(
        functools.partial(kernel, nn),
        out_shape=outs,
        in_specs=[hbm] * 15,
        out_specs=[vm] * 7,
        scratch_shapes=scratch,
        compiler_params=pltpu.CompilerParams(
            collective_id=0, has_side_effects=True, vmem_limit_bytes=54 * 1024 * 1024
        ),
        name="layer",
    )(
        tokens,
        hop_mask.reshape(tiles, TILE),
        graph_ids.reshape(1, nodes),
        norm1_gain,
        norm1_shift,
        w_query,
        w_key,
        w_value,
        w_out,
        norm2_gain,
        norm2_shift,
        w_up,
        w_down,
        hop_weight,
        cotangent,
    )
    line = jax.ShapeDtypeStruct((width,), F32)
    square = jax.ShapeDtypeStruct((width, qw), F32)
    return pl.pallas_call(
        results_kernel,
        out_shape=[
            jax.ShapeDtypeStruct((nodes, width), BF16),
            jax.ShapeDtypeStruct((rows, width), BF16),
            line,
            line,
            square,
            square,
            square,
            jax.ShapeDtypeStruct((qw, width), F32),
            line,
            line,
            jax.ShapeDtypeStruct((width, uw), F32),
            jax.ShapeDtypeStruct((uw, width), F32),
            line,
        ],
        in_specs=[vm] * 7,
        out_specs=[hbm] * 13,
        scratch_shapes=[v(width, qw, dtype=F32)] * 3 + [v(width, dtype=F32)] * 5 + [pltpu.SemaphoreType.DMA((13,))],
        compiler_params=pltpu.CompilerParams(vmem_limit_bytes=16 * 1024 * 1024),
        name="results",
    )(readout, gtok, small, fin_in, fin_out, fin_up, fin_dn)


def solution(mesh):
    spread = P(("nodes", "tp"), None)
    flat = P(("nodes", "tp"))
    cols, rows = P(None, "tp"), P("tp", None)
    return jax.shard_map(
        functools.partial(shards, mesh.shape["nodes"]),
        mesh=mesh,
        in_specs=(spread, flat, flat, P(), P(), cols, cols, cols, rows, P(), P(), cols, rows, P(), spread),
        out_specs=(spread, spread, P(), P(), cols, cols, cols, rows, P(), P(), cols, rows, P()),
        check_vma=False,
    )
```

```python
import functools

import jax
import jax.numpy as jnp
from jax import lax
from jax.experimental import pallas as pl
from jax.experimental.pallas import tpu as pltpu
from jax.sharding import PartitionSpec as P

HOPS = 8
HEAD = 64
GRAPHS = 64
EPSILON = 1e-05
NEGATIVE = -1000000000.0
MESH = pl.DeviceIdType.MESH
F32 = jnp.float32
BF16 = jnp.bfloat16
CHUNK = 256
WIDE = 512
TILE = 128


def mm(a, b):
    return lax.dot_general(a, b, (((1,), (0,)), ((), ())), preferred_element_type=F32)


def mm_rt(a, b):
    return lax.dot_general(a, b, (((1,), (1,)), ((), ())), preferred_element_type=F32)


def mm_lt(a, b):
    return lax.dot_general(a, b, (((0,), (0,)), ((), ())), preferred_element_type=F32)


def iota(shape, axis):
    return lax.broadcasted_iota(jnp.int32, shape, axis)


def centred(values):
    centre = values - jnp.mean(values, axis=-1, keepdims=True)
    spread = jnp.mean(centre * centre, axis=-1, keepdims=True)
    return centre * lax.rsqrt(spread + EPSILON), lax.rsqrt(spread + EPSILON)


def gelu_both(x):
    phi = 0.5 + 0.5 * lax.erf(x * 0.7071067811865476)
    bell = jnp.exp2((-0.5 * 1.4426950408889634) * (x * x))
    return x * phi, phi + x * (bell * 0.3989422804014327)


def tokens_of(ref):
    return ref[...].astype(F32).reshape(1, ref.shape[0])


class Group:
    def __init__(self, array, wide, cols, recv_core, recv_plane, recv_z, final, more, send, recv, base):
        self.array, self.wide = array, wide
        self.cols = cols
        self.recv_core, self.recv_plane, self.recv_z = recv_core, recv_plane, recv_z
        self.final = final
        self.more = more
        self.send, self.recv, self.base = send, recv, base
        rows = final.shape[0]
        self.half_rows = rows // 2
        self.piece_rows = rows // 8
        self.width = final.shape[1]

    def sems(self, k):
        return self.send.at[self.base + k], self.recv.at[self.base + k]

    def rows(self, c, p=None):
        if p is None:
            return pl.ds(pl.multiple_of(c * self.half_rows, 16), self.half_rows)
        return pl.ds(pl.multiple_of(c * self.half_rows + p * self.piece_rows, 16), self.piece_rows)

    def block(self, rows):
        if self.wide:
            return self.array.at[rows, self.cols[0] * self.width : self.cols[1] * self.width]
        return self.array.at[:, rows]

    def slot(self, rows, d):
        if self.wide:
            return self.array.at[rows, d * self.width : (d + 1) * self.width]
        return self.array.at[d, rows]


def kernel(
    nn,
    tok_hbm,
    mask_ref,
    gid_ref,
    g1_ref,
    s1_ref,
    wq_hbm,
    wk_hbm,
    wv_hbm,
    wo_hbm,
    g2_ref,
    s2_ref,
    wu_hbm,
    wd_hbm,
    hw_ref,
    cot_hbm,
    readout_ref,
    gtok_ref,
    small_ref,
    fin_in_ref,
    wide_out_ref,
    wide_up_ref,
    wide_dn_ref,
    fin_out_ref,
    fin_up_ref,
    fin_dn_ref,
    mask_v,
    gid_v,
    g1_v,
    s1_v,
    g2_v,
    s2_v,
    hw_v,
    w_in,
    w_up,
    w_ot,
    w_dn,
    tok,
    cot,
    n1,
    qkv,
    pn,
    ctx,
    res,
    n2,
    act,
    gp,
    lay,
    emask,
    pmask,
    n1t,
    n2t,
    ctxt,
    vcol,
    mt,
    gexp,
    wcol,
    dcol,
    ab,
    zed,
    mixes,
    gbef,
    gl,
    datt,
    dctx,
    dqkv,
    g_up,
    g_dn,
    g_out,
    g_in,
    rc_up,
    rc_dn,
    rc_out,
    rc_in,
    rp_up,
    rp_dn,
    rp_out,
    rp_in,
    rz_up,
    rz_dn,
    rz_out,
    rz_in,
    mo_up,
    mo_dn,
    mo_out,
    mo_in,
    ar_one,
    ar_nodes,
    ar_tp,
    sv_one,
    sv_nodes,
    sv_tp,
    lsem,
    wsend,
    wrecv,
    gsend,
    grecv,
    asend,
    arecv,
    bsend,
    brecv,
):
    n, t = lax.axis_index("nodes"), lax.axis_index("tp")
    rows_here, width = tok.shape
    chunks = rows_here // CHUNK
    wides = rows_here // WIDE
    tiles = rows_here // TILE
    c = n % 2
    plane = (n // 2) % 4
    eighth = 4 * c + plane
    extra = [b for b in range(3, 12) if (1 << b) < nn]

    def node_peer(k):
        out = n
        for b in range(12):
            if (k >> b) & 1:
                bit = (n // (1 << b)) % 2
                out = out + (1 << b) * (1 - 2 * bit)
        return (out, t)

    def tp_peer(k):
        out = t
        for b in range(2):
            if (k >> b) & 1:
                bit = (t // (1 << b)) % 2
                out = out + (1 << b) * (1 - 2 * bit)
        return (n, out)

    def remote(src, dst, ssem, rsem, peer):
        return pltpu.make_async_remote_copy(
            src_ref=src, dst_ref=dst, send_sem=ssem, recv_sem=rsem, device_id=peer, device_id_type=MESH
        )

    qw = wq_hbm.shape[1]
    local = [
        pltpu.make_async_copy(wq_hbm, w_in.at[:, 0:qw], lsem.at[0]),
        pltpu.make_async_copy(wk_hbm, w_in.at[:, qw : 2 * qw], lsem.at[1]),
        pltpu.make_async_copy(wv_hbm, w_in.at[:, 2 * qw : 3 * qw], lsem.at[2]),
        pltpu.make_async_copy(tok_hbm, tok, lsem.at[3]),
        pltpu.make_async_copy(wo_hbm, w_ot.at[0], lsem.at[4]),
        pltpu.make_async_copy(wd_hbm, w_dn.at[0], lsem.at[5]),
        pltpu.make_async_copy(wu_hbm, w_up.at[:, 0 : wu_hbm.shape[1]], lsem.at[6]),
        pltpu.make_async_copy(cot_hbm, cot, lsem.at[7]),
    ]
    tiny = ((mask_ref, mask_v), (gid_ref, gid_v), (g1_ref, g1_v), (s1_ref, s1_v), (g2_ref, g2_v), (s2_ref, s2_v))
    for i, (src, dst) in enumerate(tiny + ((hw_ref, hw_v),)):
        local.append(pltpu.make_async_copy(src, dst, lsem.at[8 + i]))
    for copy in local:
        copy.start()

    barrier = pltpu.get_barrier_semaphore()
    greet = [node_peer(k) for k in range(1, 8)] + [node_peer(1 << b) for b in extra]
    greet += [tp_peer(k) for k in range(1, 4)]
    for peer in greet:
        pl.semaphore_signal(barrier, inc=1, device_id=peer, device_id_type=MESH)
    pl.semaphore_wait(barrier, len(greet))

    def plane_of(e):
        out = plane
        for b in range(2):
            if (e >> b) & 1:
                out = out + (1 << b) * (1 - 2 * ((plane // (1 << b)) % 2))
        return out

    def weight_block(ref, off, size, d0, d1):
        rows = pl.ds(pl.multiple_of(off, 16), size)
        if len(ref.shape) == 3:
            return ref.at[d0:d1, rows]
        w = ref.shape[1] // 4
        return ref.at[rows, d0 * w : d1 * w]

    class Fetch:
        def __init__(self, ref, slots, base, relay=False):
            total = ref.shape[1] if len(ref.shape) == 3 else ref.shape[0]
            d0, d1 = slots
            sems = iter(range(base, base + 8))

            def go(src, dst, peer):
                k = next(sems)
                return remote(src, dst, wsend.at[k], wrecv.at[k], peer)

            def rows(off, size):
                return weight_block(ref, off, size, d0, d1)

            part = total // 8
            own = eighth * part
            self.z = [
                go(weight_block(ref, own, part, 0, 1), weight_block(ref, own, part, d, d + 1), tp_peer(d))
                for d in range(d0, d1)
            ]
            self.more = []
            lots = [rows(c * (total // 2), total // 2)]
            if relay:
                self.plane = [go(rows(own, part), rows(own, part), node_peer(2 << e)) for e in range(2)]
                for e in range(2):
                    got = rows((4 * c + plane_of(1 << e)) * part + e * (part // 2), part // 2)
                    self.more.append(go(got, got, node_peer(4 >> e)))
            else:
                self.plane = [go(rows(own, part), rows(own, part), node_peer(2 * e)) for e in (1, 2, 3)]
            self.core = [go(x, x, node_peer(1)) for x in lots]

        def start_z(self):
            for cp in self.z:
                cp.start()

        def start_plane(self):
            for cp in self.z:
                cp.wait()
            for cp in self.plane:
                cp.start()

        def start_relay(self):
            for cp in self.plane:
                cp.wait()
            for cp in self.more:
                cp.start()

        def start_core(self):
            for cp in self.more or self.plane:
                cp.wait()
            for cp in self.core:
                cp.start()

        def end(self):
            for cp in self.core:
                cp.wait()

    fetch_in = [None] + [Fetch(w_in, (d, d + 1), 8 * (d - 1)) for d in (1, 2, 3)]
    fetch_ot = Fetch(w_ot, (1, 4), 24)
    fetch_up = Fetch(w_up, (1, 4), 32)
    fetch_dn = Fetch(w_dn, (1, 4), 40)

    for i in (0, 1, 2):
        local[i].wait()
    for d in (1, 2, 3):
        fetch_in[d].start_z()

    for i in range(8, 15):
        local[i].wait()
    gain1 = tokens_of(g1_v)
    shift1 = tokens_of(s1_v)
    gain2 = tokens_of(g2_v)
    shift2 = tokens_of(s2_v)
    hopw = tokens_of(hw_v)
    hop16 = jnp.broadcast_to(hopw, (16, width)).astype(BF16)

    eye = iota((TILE, TILE), 0) == iota((TILE, TILE), 1)
    ones = jnp.ones((TILE, TILE), BF16)
    lane8 = iota((HOPS, TILE), 1)
    block8 = lane8 // HOPS
    eye16 = eye.astype(F32).astype(BF16)
    emask[...] = (iota((TILE, TILE), 0) // HOPS == iota((TILE, TILE), 1) // HOPS).astype(F32).astype(BF16)
    first = (iota((2 * TILE, TILE), 0) < TILE) == (iota((2 * TILE, TILE), 1) < HEAD)
    pmask[...] = first.astype(F32).astype(BF16)
    nodes_chunk = CHUNK // HOPS
    spread_c = (iota((CHUNK, nodes_chunk), 0) // HOPS == iota((CHUNK, nodes_chunk), 1)).astype(F32).astype(BF16)

    def rows_of(i, size):
        return pl.ds(pl.multiple_of(i * size, size), size)

    mask_f = mask_v[...].astype(F32)
    for i in range(tiles):
        col = mm(jnp.where(eye, mask_f[i : i + 1, :], 0.0).astype(BF16), ones)
        vcol[i * TILE : (i + 1) * TILE, :] = col
        acc = jnp.zeros((HOPS, TILE), F32)
        col3 = col.reshape(TILE // HOPS, HOPS, TILE)
        for r in range(TILE // HOPS):
            acc = jnp.where(block8 == r, col3[r], acc)
        mt[i] = acc

    local[3].wait()

    def norm_one(i, carry):
        x = tok[rows_of(i, CHUNK), :].astype(F32)
        hat, _ = centred(x)
        n1[rows_of(i, CHUNK), :] = (hat * gain1 + shift1).astype(BF16)
        return carry

    lax.fori_loop(0, chunks, norm_one, 0)

    def project(d, lo, hi):
        base = d * 3 * qw

        def step(i, carry):
            r = rows_of(i, WIDE)
            out = mm(n1[r, :], w_in[:, base : base + 3 * qw])
            qkv[r, base : base + qw] = (out[:, 0:qw] * (HEAD**-0.5)).astype(BF16)
            qkv[r, base + qw : base + 3 * qw] = out[:, qw:].astype(BF16)
            return carry

        lax.fori_loop(lo, hi, step, 0)

    def pair(x):
        return jnp.concatenate([x, x], axis=0) * pmask[...]

    bits = [((lane8 // (HOPS << b)) % 2) == 1 for b in range(4)]

    def compact(x):
        out = []
        for h in range(2):
            x3 = x[:, h * TILE : (h + 1) * TILE].reshape(TILE // HOPS, HOPS, TILE)
            parts = [x3[r] for r in range(TILE // HOPS)]
            for b in range(4):
                parts = [jnp.where(bits[b], parts[2 * m + 1], parts[2 * m]) for m in range(len(parts) // 2)]
            out.append(parts[0])
        return out

    def expand(x):
        twice = jnp.concatenate([x, x], axis=0).astype(BF16)
        return jnp.concatenate([twice] * (TILE // 16), axis=0) * emask[...]

    together = 8

    steps = tiles // together
    mid = steps // 2

    def attend(d, lo, hi):
        base = d * 3 * qw

        def step(i, carry):
            at = [i * together + m for m in range(together)]
            rs = [rows_of(a, TILE) for a in at]
            q2 = [pair(qkv[r, base : base + qw]) for r in rs]
            scores = [compact(mm_rt(qkv[r, base + qw : base + 2 * qw], x)) for r, x in zip(rs, q2, strict=True)]
            wide = []
            for m, a in enumerate(at):
                keep = mt[a] > 0.5
                for h in range(2):
                    wide.append(jnp.where(keep, scores[m][h], NEGATIVE))
            peaks = [jnp.max(x, axis=0, keepdims=True) for x in wide]
            wide = [jnp.exp(x - y) for x, y in zip(wide, peaks, strict=True)]
            totals = [jnp.sum(x, axis=0, keepdims=True) for x in wide]
            wide = [x / y for x, y in zip(wide, totals, strict=True)]
            for m, a in enumerate(at):
                for h in range(2):
                    pn[a * 8 + 2 * d + h] = wide[2 * m + h]
            turned = [
                mm_rt(eye16, jnp.concatenate([expand(wide[2 * m]), expand(wide[2 * m + 1])], axis=0)).astype(BF16)
                for m in range(together)
            ]
            v2 = [pair(qkv[r, base + 2 * qw : base + 3 * qw]) for r in rs]
            for m, r in enumerate(rs):
                ctx[r, d * qw : (d + 1) * qw] = mm(turned[m], v2[m]).astype(BF16)
            return carry

        lax.fori_loop(lo, hi, step, 0)

    gcol = mm(jnp.where(eye, gid_v[...].astype(F32), 0.0).astype(BF16), ones).astype(BF16)
    for i in range(chunks):
        gexp[i * CHUNK : (i + 1) * CHUNK, :] = mm(spread_c, gcol[i * nodes_chunk : (i + 1) * nodes_chunk])
    fetch_in[1].start_plane()
    project(0, 0, wides // 2)
    fetch_in[2].start_plane()
    project(0, wides // 2, wides)
    fetch_in[3].start_plane()
    for i in (4, 5, 6, 7):
        local[i].wait()
    fetch_ot.start_z()
    fetch_up.start_z()
    fetch_dn.start_z()
    attend(0, 0, steps)
    fetch_ot.start_plane()
    fetch_in[1].start_core()
    fetch_up.start_plane()
    fetch_in[1].end()
    fetch_in[2].start_core()
    project(1, 0, wides)
    fetch_in[3].start_core()
    attend(1, 0, steps)
    fetch_dn.start_plane()
    fetch_in[2].end()
    project(2, 0, wides)
    fetch_ot.start_core()
    attend(2, 0, steps)
    fetch_in[3].end()
    project(3, 0, wides)
    attend(3, 0, steps)
    fetch_ot.end()

    def w_out():
        return w_ot[...].reshape(4 * qw, width)

    def w_down():
        return w_dn[...].reshape(4 * w_dn.shape[1], width)

    hop3 = iota((nodes_chunk, HOPS, TILE), 1)
    lane3 = iota((nodes_chunk, HOPS, TILE), 2)
    node3 = iota((nodes_chunk, HOPS, TILE), 0)
    lane_graph = (lane3 % GRAPHS).astype(F32)

    def feed_norm(i, carry):
        r = rows_of(i, WIDE)
        x = tok[r, :].astype(F32) + mm(ctx[r, :], w_out())
        res[r, :] = x
        hat, _ = centred(x)
        n2[r, :] = (hat * gain2 + shift2).astype(BF16)
        return carry

    uw = wu_hbm.shape[1]

    def feed_up(lo, hi):
        cols = slice(lo * uw, hi * uw)

        def step(i, carry):
            r = rows_of(i, WIDE)
            value, slope = gelu_both(mm(n2[r, :], w_up[:, cols]))
            act[r, cols] = value.astype(BF16)
            gp[r, cols] = slope.astype(BF16)
            return carry

        return step

    def feed_down(i, acc):
        r = rows_of(i, WIDE)
        lay[r, :] = res[r, :] + mm(act[r, :], w_down())
        for m in range(WIDE // CHUNK):
            acc = hops(i * (WIDE // CHUNK) + m, acc)
        return acc

    def hops(i, acc):
        r = rows_of(i, CHUNK)
        out = lay[r, :]
        dr = mm(spread_c, cot[rows_of(i, nodes_chunk), :])
        logit = jnp.sum(out * hopw, axis=-1, keepdims=True)
        gcoef = jnp.sum(out * dr, axis=-1, keepdims=True)
        shape = (nodes_chunk, HOPS, TILE)
        valid = vcol[r, :].reshape(shape)
        valid = jnp.where(hop3 > 0, valid, 0.0)
        logit = jnp.where(valid > 0.5, jnp.broadcast_to(logit, (CHUNK, TILE)).reshape(shape), NEGATIVE)
        e = jnp.exp(logit - jnp.max(logit, axis=1, keepdims=True))
        e = jnp.where(hop3 > 0, e, 0.0)
        weight = e / jnp.sum(e, axis=1, keepdims=True)
        direct = valid * jnp.broadcast_to(gcoef, (CHUNK, TILE)).reshape(shape)
        wcol[r, :] = weight.reshape(CHUNK, TILE)
        dcol[r, :] = direct.reshape(CHUNK, TILE)
        mine = gexp[r, :].reshape(shape) == lane_graph
        both = jnp.where(lane3 < GRAPHS, jnp.where(hop3 == 0, 1.0, weight), -direct)
        return acc + jnp.sum(jnp.where(mine, both, 0.0), axis=0)

    lax.fori_loop(0, wides, feed_norm, 0, unroll=True)
    fetch_up.start_core()
    lax.fori_loop(0, wides, feed_up(0, 1), 0)
    fetch_up.end()
    lax.fori_loop(0, wides // 2, feed_up(1, 4), 0)
    fetch_dn.start_core()
    lax.fori_loop(wides // 2, wides, feed_up(1, 4), 0)
    fetch_dn.end()
    sums = lax.fori_loop(0, wides, feed_down, jnp.zeros((HOPS, TILE), F32), unroll=True)

    def reduce_all(value, one, by_nodes, by_tp, ssem, rsem, overlap=None):
        one[0] = value
        copies = [
            remote(one.at[0], by_nodes.at[k - 1], ssem.at[k - 1], rsem.at[k - 1], node_peer(k)) for k in range(1, 8)
        ]
        for cp in copies:
            cp.start()
        if overlap is not None:
            overlap()
        for cp in copies:
            cp.wait()
        value = one[0]
        for k in range(7):
            value = value + by_nodes[k]
        at = 7
        for b in extra:
            one[at - 6] = value
            cp = remote(one.at[at - 6], by_nodes.at[at], ssem.at[at], rsem.at[at], node_peer(1 << b))
            cp.start()
            cp.wait()
            value = value + by_nodes[at]
            at += 1
        last = one.shape[0] - 1
        one[last] = value
        copies = [
            remote(one.at[last], by_tp.at[k - 1], ssem.at[at + k - 1], rsem.at[at + k - 1], tp_peer(k))
            for k in range(1, 4)
        ]
        for cp in copies:
            cp.start()
        return copies, lambda: one[last] + by_tp[0] + by_tp[1] + by_tp[2]

    def small_products():
        drdown = mm_rt(cot[...], w_down()).astype(BF16)
        hopdown = mm_rt(hop16, w_down()).astype(BF16)
        for i in range(chunks):
            piece = drdown[i * nodes_chunk : (i + 1) * nodes_chunk]
            ab[i, 0:nodes_chunk] = piece
            ab[i, nodes_chunk : 2 * nodes_chunk] = piece
            ab[i, 2 * nodes_chunk : 2 * nodes_chunk + 16] = hopdown
            ab[i, 2 * nodes_chunk + 16 :] = jnp.zeros((TILE - 2 * nodes_chunk - 16, ab.shape[2]), BF16)
        for i in range(chunks):
            at = slice(i * CHUNK, (i + 1) * CHUNK)
            for src, dst in ((n2, n2t), (ctx, ctxt), (n1, n1t)):
                dst[:, at] = src[at, :].T

    copies, total = reduce_all(sums, ar_one, ar_nodes, ar_tp, asend, arecv, small_products)
    for cp in copies:
        cp.wait()
    sums = total()
    row = jnp.broadcast_to(sums[0:1, :], (HOPS, TILE))
    counts = jnp.where(lane8 < GRAPHS, row, pltpu.roll(row, GRAPHS, 1))
    means = (sums / (counts + 1.0))[None]

    def back_one(i, carry):
        zed_acc = carry
        r = rows_of(i, CHUNK)
        shape = (nodes_chunk, HOPS, TILE)
        picked = jnp.where(gexp[r, :].reshape(shape) == lane_graph, means, 0.0)
        mean_r = jnp.sum(jnp.where(lane3 < GRAPHS, picked, 0.0), axis=-1, keepdims=True)
        grad_mean = jnp.sum(jnp.where(lane3 < GRAPHS, 0.0, picked), axis=-1, keepdims=True)
        weight = wcol[r, :].reshape(shape)
        valid = vcol[r, :].reshape(shape)
        coef = jnp.where(hop3 > 0, valid * (weight - mean_r), 1.0)
        grad_w = dcol[r, :].reshape(shape) + grad_mean
        glog = weight * (grad_w - jnp.sum(weight * grad_w, axis=1, keepdims=True))
        coef_hi = coef.astype(BF16).astype(F32)
        glog_hi = glog.astype(BF16).astype(F32)
        zero = jnp.zeros_like(coef)
        mix = jnp.where(lane3 == node3, coef_hi, zero)
        mix = jnp.where(lane3 == node3 + nodes_chunk, coef - coef_hi, mix)
        mix = jnp.where(lane3 == 2 * nodes_chunk, glog_hi, mix)
        mix = jnp.where(lane3 == 2 * nodes_chunk + 1, glog - glog_hi, mix)
        mix = mix.reshape(CHUNK, TILE).astype(BF16)

        mixes[r, :] = mix
        gbef[r, :] = (mm(mix, ab[i]) * gp[r, :].astype(F32)).astype(BF16)

        fold = mm_lt(mix, act[r, :])
        zed[rows_of(i, nodes_chunk), :] = (fold[0:nodes_chunk] + fold[nodes_chunk : 2 * nodes_chunk]).astype(BF16)
        zed_acc = zed_acc + fold[2 * nodes_chunk : 2 * nodes_chunk + 8]

        return zed_acc

    def back_norm(i, carry):
        gain_acc, shift_acc = carry
        r = rows_of(i, WIDE)
        layer_grads(i)
        dy = mm_rt(gbef[r, :], w_up[...])
        hat, inv = centred(res[r, :])
        gain_acc = gain_acc + jnp.sum((dy * hat).reshape(WIDE // HOPS, HOPS, width), axis=0)
        shift_acc = shift_acc + jnp.sum(dy.reshape(WIDE // HOPS, HOPS, width), axis=0)
        g = dy * gain2
        back = inv * (
            g - jnp.mean(g, axis=-1, keepdims=True) - hat * jnp.mean(g * hat, axis=-1, keepdims=True)
        )
        grad_res = gl[r, :] + back
        gl[r, :] = grad_res
        att = grad_res.astype(BF16)
        datt[r, :] = att
        dctx[r, :] = mm_rt(att, w_out()).astype(BF16)
        return gain_acc, shift_acc

    def layer_grads(wide):
        for m in range(WIDE // CHUNK):
            i = wide * (WIDE // CHUNK) + m
            r = rows_of(i, CHUNK)
            mix = mixes[r, :]
            dr = cot[rows_of(i, nodes_chunk), :]
            rest = jnp.zeros((TILE - 2 * nodes_chunk - 16, width), BF16)
            gl[r, :] = mm(mix, jnp.concatenate([dr, dr, hop16, rest], axis=0))

    def readouts(i, hop_acc):
        r = rows_of(i, CHUNK)
        seen = mm_lt(mixes[r, :], lay[r, :].astype(BF16))
        both = seen[0:nodes_chunk] + seen[nodes_chunk : 2 * nodes_chunk]
        readout_ref[rows_of(i, nodes_chunk), :] = both.astype(BF16)
        return hop_acc + seen[2 * nodes_chunk : 2 * nodes_chunk + 8]

    zero8 = jnp.zeros((HOPS, width), F32)
    zed_sum = lax.fori_loop(0, chunks, back_one, jnp.zeros((HOPS, zed.shape[1]), F32), unroll=True)

    def group(at, array, wide, cols, rc, rp, rz, final, more):
        return Group(array, wide, cols, rc, rp, rz, final, more, gsend, grecv, at * (15 + len(extra)))

    dn = group(0, g_dn, False, (0, 4), rc_dn, rp_dn, rz_dn, fin_dn_ref, mo_dn)
    up = group(1, g_up, True, (0, 4), rc_up, rp_up, rz_up, fin_up_ref, mo_up)
    ot = group(2, g_out, False, (0, 4), rc_out, rp_out, rz_out, fin_out_ref, mo_out)
    qk = [
        group(3 + d, g_in, True, (d, d + 1), rc_in.at[d], rp_in.at[d], rz_in, fin_in_ref, mo_in) for d in range(4)
    ]
    every = (1, 2, 3)

    def core_copy(g):
        s, r = g.sems(0)
        return remote(g.block(g.rows(1 - c)), g.recv_core, s, r, node_peer(1))

    def go_core(g):
        core_copy(g).start()

    def add_core(g):
        core_copy(g).wait()
        mine = g.block(g.rows(c))
        mine[...] = mine[...] + g.recv_core[...]

    def plane_copies(g):
        return [
            remote(g.block(g.rows(c, plane_of(e))), g.recv_plane.at[e - 1], *g.sems(e), node_peer(2 * e))
            for e in (1, 2, 3)
        ]

    def go_plane(g):
        add_core(g)
        for cp in plane_copies(g):
            cp.start()

    def cut(g, p, e):
        if g.wide:
            w = g.piece_rows // 2
            rows = pl.ds(pl.multiple_of(c * g.half_rows + p * g.piece_rows + e * w, 16), w)
            return g.array.at[rows, g.cols[0] * g.width : g.cols[1] * g.width]
        w = g.width // 2
        return g.array.at[:, g.rows(c, p), e * w : (e + 1) * w]

    def landing(g, m, e):
        if g.wide:
            w = g.piece_rows // 2
            return g.recv_plane.at[m, e * w : (e + 1) * w]
        w = g.width // 2
        return g.recv_plane.at[m, :, :, e * w : (e + 1) * w]

    def fold_copies(g):
        out = []
        for e in range(2):
            for m, far in enumerate((plane_of(1 << e), plane_of(3))):
                sems = g.sems(11 + 2 * e + m)
                out.append(remote(cut(g, far, e), landing(g, m, e), *sems, node_peer(2 << e)))
        return out

    def go_fold(g):
        add_core(g)
        for cp in fold_copies(g):
            cp.start()

    def fold_last(g):
        return [
            remote(cut(g, plane_of(2 >> e), e), landing(g, 2, e), *g.sems(1 + e), node_peer(4 >> e)) for e in range(2)
        ]

    def go_fold_last(g):
        for cp in fold_copies(g):
            cp.wait()
        for e in range(2):
            for m, keep in enumerate((plane, plane_of(2 >> e))):
                mine = cut(g, keep, e)
                mine[...] = mine[...] + landing(g, m, e)[...]
        for cp in fold_last(g):
            cp.start()

    def go_z_fold(g, slots):
        for cp in fold_last(g):
            cp.wait()
        mine = g.block(g.rows(c, plane))
        mine[...] = mine[...] + g.recv_plane[2]
        for cp in z_copies(g, slots):
            cp.start()

    def z_copies(g, slots):
        return [
            remote(g.slot(g.rows(c, plane), d), g.recv_z.at[d - 1], *g.sems(3 + d), tp_peer(d)) for d in slots
        ]

    def go_z(g, slots):
        for cp in plane_copies(g):
            cp.wait()
        mine = g.block(g.rows(c, plane))
        total = mine[...].astype(F32)
        for e in range(3):
            total = total + g.recv_plane[e].astype(F32)
        mine[...] = total.astype(BF16)
        for cp in z_copies(g, slots):
            cp.start()

    def z_first(g):
        return [remote(g.slot(g.rows(c), d), g.recv_z.at[d - 1], *g.sems(3 + d), tp_peer(d)) for d in every]

    def go_z_first(g):
        add_core(g)
        for cp in z_first(g):
            cp.start()

    def own_pieces(g):
        return [
            remote(g.slot(g.rows(c, plane_of(e)), 0), g.recv_plane.at[e - 1], *g.sems(e), node_peer(2 * e))
            for e in (1, 2, 3)
        ]

    def go_own_plane(g):
        for cp in z_first(g):
            cp.wait()
        mine = g.slot(g.rows(c), 0)
        total = mine[...].astype(F32)
        for d in range(3):
            total = total + g.recv_z[d].astype(F32)
        mine[...] = total.astype(BF16)
        for cp in own_pieces(g):
            cp.start()

    def go_own_final(g):
        for cp in own_pieces(g):
            cp.wait()
        total = g.slot(g.rows(c, plane), 0)[...].astype(F32)
        for e in range(3):
            total = total + g.recv_plane[e].astype(F32)
        share(g, total)

    def final_copies(g):
        mine = g.final.at[g.rows(c, plane)]
        return [remote(mine, mine, *g.sems(6 + e), node_peer(2 * e)) for e in (1, 2, 3)]

    def last_copy(g):
        mine = g.final.at[g.rows(c)]
        return remote(mine, mine, *g.sems(10), node_peer(1))

    def go_final(g, waits):
        for cp in waits:
            cp.wait()
        total = g.slot(g.rows(c, plane), 0)[...].astype(F32)
        for d in range(3):
            total = total + g.recv_z[d].astype(F32)
        share(g, total)

    def share(g, total):
        for j, b in enumerate(extra):
            g.more[2 * j] = total.astype(BF16)
            cp = remote(g.more.at[2 * j], g.more.at[2 * j + 1], *g.sems(15 + j), node_peer(1 << b))
            cp.start()
            cp.wait()
            total = total + g.more[2 * j + 1].astype(F32)
        g.final.at[g.rows(c, plane)][...] = total.astype(BF16)
        for cp in final_copies(g):
            cp.start()

    def go_last(g):
        for cp in final_copies(g):
            cp.wait()
        last_copy(g).start()

    def finish(g):
        last_copy(g).wait()

    zed[rows_here // HOPS :, :] = jnp.concatenate([zed_sum, jnp.zeros_like(zed_sum)], axis=0).astype(BF16)
    drh = jnp.concatenate([cot[...], hop16], axis=0)
    g_dn[...] = mm_lt(zed[...], drh).astype(BF16).reshape(g_dn.shape)
    go_core(dn)
    g_up[...] = mm(n2t[...], gbef[...]).astype(BF16)
    go_core(up)
    norm_sums = lax.fori_loop(0, wides // 2, back_norm, (zero8, zero8))
    go_z_first(dn)
    gain_two, shift_two = lax.fori_loop(wides // 2, wides, back_norm, norm_sums)
    go_fold(up)
    g_out[...] = mm(ctxt[...], datt[...]).astype(BF16).reshape(g_out.shape)
    go_core(ot)

    def attend_back(d):
        base = d * 3 * qw

        def step(i, carry):
            at = [i * together + m for m in range(together)]
            rs = [rows_of(a, TILE) for a in at]
            do2 = [pair(dctx[r, d * qw : (d + 1) * qw]) for r in rs]
            grads = [
                compact(mm_rt(qkv[r, base + 2 * qw : base + 3 * qw], x)) for r, x in zip(rs, do2, strict=True)
            ]
            probs = [[pn[a * 8 + 2 * d + h] for h in range(2)] for a in at]
            probs_wide = [jnp.concatenate([expand(p) for p in ps], axis=1) for ps in probs]
            for m, r in enumerate(rs):
                dqkv[r, base + 2 * qw : base + 3 * qw] = mm(probs_wide[m], do2[m]).astype(BF16)
            inner = [[jnp.sum(p * g, axis=0, keepdims=True) for p, g in zip(*x, strict=True)] for x in zip(probs, grads, strict=True)]
            back = [
                [expand(probs[m][h] * (grads[m][h] - inner[m][h])) for h in range(2)] for m in range(together)
            ]
            q2 = [pair(qkv[r, base : base + qw]) for r in rs]
            for m, r in enumerate(rs):
                wide = jnp.concatenate(back[m], axis=1)
                dqkv[r, base + qw : base + 2 * qw] = mm(wide, q2[m]).astype(BF16)
            turned = [mm_rt(eye16, jnp.concatenate(x, axis=0)).astype(BF16) for x in back]
            k2 = [pair(qkv[r, base + qw : base + 2 * qw]) for r in rs]
            for m, r in enumerate(rs):
                dqkv[r, base : base + qw] = (mm(turned[m], k2[m]) * (HEAD**-0.5)).astype(BF16)
            return carry

        lax.fori_loop(0, tiles // together, step, 0)
        g_in[:, base : base + 3 * qw] = mm(n1t[...], dqkv[:, base : base + 3 * qw]).astype(BF16)
        go_core(qk[d])

    def back_two(i, carry):
        gain_acc, shift_acc = carry
        r = rows_of(i, WIDE)
        dy = mm_rt(dqkv[r, :], w_in[...])
        hat, inv = centred(tok[r, :].astype(F32))
        gain_acc = gain_acc + jnp.sum((dy * hat).reshape(WIDE // HOPS, HOPS, width), axis=0)
        shift_acc = shift_acc + jnp.sum(dy.reshape(WIDE // HOPS, HOPS, width), axis=0)
        g = dy * gain1
        back = inv * (
            g - jnp.mean(g, axis=-1, keepdims=True) - hat * jnp.mean(g * hat, axis=-1, keepdims=True)
        )
        gtok_ref[r, :] = (gl[r, :] + back).astype(BF16)
        return gain_acc, shift_acc

    attend_back(3)
    go_fold(ot)
    attend_back(2)
    go_fold(qk[3])
    go_fold_last(up)
    attend_back(1)
    go_fold(qk[2])
    go_fold_last(ot)
    attend_back(0)
    go_plane(qk[1])
    go_z_fold(up, every)
    go_fold_last(qk[3])
    hop_sum = lax.fori_loop(0, chunks, readouts, zero8)
    norm_sums = lax.fori_loop(0, wides // 2, back_two, (zero8, zero8))
    go_plane(qk[0])
    go_z_fold(ot, every)
    go_fold_last(qk[2])
    go_own_plane(dn)
    go_z_fold(qk[3], (3,))
    gain_one, shift_one = lax.fori_loop(wides // 2, wides, back_two, norm_sums)
    go_z(qk[1], (1,))
    go_z_fold(qk[2], (2,))

    def fold8(x):
        return jnp.sum(x, axis=0, keepdims=True)

    small = jnp.concatenate(
        [fold8(gain_one), fold8(shift_one), fold8(gain_two), fold8(shift_two), fold8(hop_sum[0:2]), zero8[0:3]], axis=0
    )

    def rest_of():
        go_final(up, z_copies(up, every))
        go_final(ot, z_copies(ot, every))
        go_own_final(dn)
        go_z(qk[0], ())
        go_final(qk[0], [z_copies(qk[d], (d,))[0] for d in every])

    copies, total_small = reduce_all(small, sv_one, sv_nodes, sv_tp, bsend, brecv, rest_of)
    go_last(up)
    go_last(dn)
    go_last(ot)
    go_last(qk[0])
    for g, wide in ((dn, wide_dn_ref), (up, wide_up_ref), (ot, wide_out_ref)):
        finish(g)
        wide[...] = g.final[...].astype(F32)
    for cp in copies:
        cp.wait()
    small_ref[...] = total_small()
    finish(qk[0])


def results_kernel(readout, gtok, small, fin_in, fin_out, fin_up, fin_dn, *rest):
    o_read, o_tok, o_g1, o_s1, o_q, o_k, o_v, o_out, o_g2, o_s2, o_up, o_dn, o_hop = rest[:13]
    v_q, v_k, v_v, *lines, sems = rest[13:]
    moves = []

    def send(src, dst):
        moves.append(pltpu.make_async_copy(src, dst, sems.at[len(moves)]))
        moves[-1].start()

    send(gtok, o_tok)
    send(readout, o_read)
    send(fin_up, o_up)
    send(fin_dn, o_dn)
    send(fin_out, o_out)
    qw = o_q.shape[1]
    for i, (x, o) in enumerate(((v_q, o_q), (v_k, o_k), (v_v, o_v))):
        x[...] = fin_in[:, i * qw : (i + 1) * qw].astype(F32)
        send(x, o)
    width = small.shape[1]
    for i, (x, o) in enumerate(zip(lines, (o_g1, o_s1, o_g2, o_s2, o_hop), strict=True)):
        x[...] = small[i : i + 1, :].reshape(width)
        send(x, o)
    for cp in moves:
        cp.wait()


def shards(
    nn,
    tokens,
    hop_mask,
    graph_ids,
    norm1_gain,
    norm1_shift,
    w_query,
    w_key,
    w_value,
    w_out,
    norm2_gain,
    norm2_shift,
    w_up,
    w_down,
    hop_weight,
    cotangent,
):
    rows, width = tokens.shape
    nodes = rows // HOPS
    qw, uw = w_query.shape[1], w_up.shape[1]
    vm = pl.BlockSpec(memory_space=pltpu.VMEM)
    hbm = pl.BlockSpec(memory_space=pl.ANY)
    extra = len([b for b in range(3, 12) if (1 << b) < nn])

    def v(*shape, dtype=BF16):
        return pltpu.VMEM(shape, dtype)

    tiles, chunks = rows // TILE, rows // CHUNK
    half = width // 2
    more = max(2 * extra, 1)
    scratch = [
        v(qw, width),
        v(width, uw),
        v(uw, width),
        v(tiles, TILE, dtype=jnp.int32),
        v(1, nodes, dtype=jnp.int32),
        v(width),
        v(width),
        v(width),
        v(width),
        v(width),
        v(width, 12 * qw),
        v(width, 4 * uw),
        v(4, qw, width),
        v(4, uw, width),
        v(rows, width),
        v(nodes, width),
        v(rows, width),
        v(rows, 12 * qw),
        v(tiles * 8, HOPS, TILE, dtype=F32),
        v(rows, width),
        v(rows, width, dtype=F32),
        v(rows, width),
        v(rows, 4 * uw),
        v(rows, 4 * uw),
        v(rows, width, dtype=F32),
        v(TILE, TILE),
        v(2 * TILE, TILE),
        v(width, rows),
        v(width, rows),
        v(width, rows),
        v(rows, TILE, dtype=F32),
        v(tiles, HOPS, TILE, dtype=F32),
        v(rows, TILE, dtype=F32),
        v(rows, TILE, dtype=F32),
        v(rows, TILE, dtype=F32),
        v(chunks, TILE, 4 * uw),
        v(nodes + 16, 4 * uw),
        v(rows, TILE),
        v(rows, 4 * uw),
        v(rows, width, dtype=F32),
        v(rows, width),
        v(rows, width),
        v(rows, 12 * qw),
        v(width, 4 * uw),
        v(4, uw, width),
        v(4, qw, width),
        v(width, 12 * qw),
        v(half, 4 * uw),
        v(4, uw // 2, width),
        v(4, qw // 2, width),
        v(4, half, 3 * qw),
        v(3, half // 4, 4 * uw),
        v(3, uw // 8, width),
        v(3, 4, qw // 8, width),
        v(4, 3, half // 4, 3 * qw),
        v(3, half // 4, uw),
        v(3, uw // 2, width),
        v(3, qw // 8, width),
        v(3, half // 4, 3 * qw),
        v(more, half // 4, uw),
        v(more, uw // 8, width),
        v(more, qw // 8, width),
        v(more, half // 4, 3 * qw),
        v(2 + extra, HOPS, TILE, dtype=F32),
        v(7 + extra, HOPS, TILE, dtype=F32),
        v(3, HOPS, TILE, dtype=F32),
        v(2 + extra, 8, width, dtype=F32),
        v(7 + extra, 8, width, dtype=F32),
        v(3, 8, width, dtype=F32),
        pltpu.SemaphoreType.DMA((15,)),
        pltpu.SemaphoreType.DMA((48,)),
        pltpu.SemaphoreType.DMA((48,)),
        pltpu.SemaphoreType.DMA((7 * (15 + extra),)),
        pltpu.SemaphoreType.DMA((7 * (15 + extra),)),
        pltpu.SemaphoreType.DMA((10 + extra,)),
        pltpu.SemaphoreType.DMA((10 + extra,)),
        pltpu.SemaphoreType.DMA((10 + extra,)),
        pltpu.SemaphoreType.DMA((10 + extra,)),
    ]
    outs = [
        pltpu.VMEM((nodes, width), BF16),
        pltpu.VMEM((rows, width), BF16),
        pltpu.VMEM((8, width), F32),
        pltpu.VMEM((width, 3 * qw), BF16),
        pltpu.VMEM((qw, width), F32),
        pltpu.VMEM((width, uw), F32),
        pltpu.VMEM((uw, width), F32),
    ]
    readout, gtok, small, fin_in, fin_out, fin_up, fin_dn = pl.pallas_call(
        functools.partial(kernel, nn),
        out_shape=outs,
        in_specs=[hbm] * 15,
        out_specs=[vm] * 7,
        scratch_shapes=scratch,
        compiler_params=pltpu.CompilerParams(
            collective_id=0, has_side_effects=True, vmem_limit_bytes=54 * 1024 * 1024
        ),
        name="layer",
    )(
        tokens,
        hop_mask.reshape(tiles, TILE),
        graph_ids.reshape(1, nodes),
        norm1_gain,
        norm1_shift,
        w_query,
        w_key,
        w_value,
        w_out,
        norm2_gain,
        norm2_shift,
        w_up,
        w_down,
        hop_weight,
        cotangent,
    )
    line = jax.ShapeDtypeStruct((width,), F32)
    square = jax.ShapeDtypeStruct((width, qw), F32)
    return pl.pallas_call(
        results_kernel,
        out_shape=[
            jax.ShapeDtypeStruct((nodes, width), BF16),
            jax.ShapeDtypeStruct((rows, width), BF16),
            line,
            line,
            square,
            square,
            square,
            jax.ShapeDtypeStruct((qw, width), F32),
            line,
            line,
            jax.ShapeDtypeStruct((width, uw), F32),
            jax.ShapeDtypeStruct((uw, width), F32),
            line,
        ],
        in_specs=[vm] * 7,
        out_specs=[hbm] * 13,
        scratch_shapes=[v(width, qw, dtype=F32)] * 3 + [v(width, dtype=F32)] * 5 + [pltpu.SemaphoreType.DMA((13,))],
        compiler_params=pltpu.CompilerParams(vmem_limit_bytes=16 * 1024 * 1024),
        name="results",
    )(readout, gtok, small, fin_in, fin_out, fin_up, fin_dn)


def solution(mesh):
    spread = P(("nodes", "tp"), None)
    flat = P(("nodes", "tp"))
    cols, rows = P(None, "tp"), P("tp", None)
    return jax.shard_map(
        functools.partial(shards, mesh.shape["nodes"]),
        mesh=mesh,
        in_specs=(spread, flat, flat, P(), P(), cols, cols, cols, rows, P(), P(), cols, rows, P(), spread),
        out_specs=(spread, spread, P(), P(), cols, cols, cols, rows, P(), P(), cols, rows, P()),
        check_vma=False,
    )
```

```python
import functools

import jax
import jax.numpy as jnp
from jax import lax
from jax.experimental import pallas as pl
from jax.experimental.pallas import tpu as pltpu
from jax.sharding import PartitionSpec as P

HOPS = 8
HEAD = 64
GRAPHS = 64
EPSILON = 1e-05
NEGATIVE = -1000000000.0
MESH = pl.DeviceIdType.MESH
F32 = jnp.float32
BF16 = jnp.bfloat16
CHUNK = 256
WIDE = 512
TILE = 128


def mm(a, b):
    return lax.dot_general(a, b, (((1,), (0,)), ((), ())), preferred_element_type=F32)


def mm_rt(a, b):
    return lax.dot_general(a, b, (((1,), (1,)), ((), ())), preferred_element_type=F32)


def mm_lt(a, b):
    return lax.dot_general(a, b, (((0,), (0,)), ((), ())), preferred_element_type=F32)


def iota(shape, axis):
    return lax.broadcasted_iota(jnp.int32, shape, axis)


def centred(values):
    centre = values - jnp.mean(values, axis=-1, keepdims=True)
    spread = jnp.mean(centre * centre, axis=-1, keepdims=True)
    return centre * lax.rsqrt(spread + EPSILON), lax.rsqrt(spread + EPSILON)


def gelu_both(x):
    phi = 0.5 + 0.5 * lax.erf(x * 0.7071067811865476)
    bell = jnp.exp2((-0.5 * 1.4426950408889634) * (x * x))
    return x * phi, phi + x * (bell * 0.3989422804014327)


def tokens_of(ref):
    return ref[...].astype(F32).reshape(1, ref.shape[0])


class Group:
    def __init__(self, array, wide, cols, recv_core, recv_plane, recv_z, final, more, send, recv, base):
        self.array, self.wide = array, wide
        self.cols = cols
        self.recv_core, self.recv_plane, self.recv_z = recv_core, recv_plane, recv_z
        self.final = final
        self.more = more
        self.send, self.recv, self.base = send, recv, base
        rows = final.shape[0]
        self.half_rows = rows // 2
        self.piece_rows = rows // 8
        self.width = final.shape[1]

    def sems(self, k):
        return self.send.at[self.base + k], self.recv.at[self.base + k]

    def rows(self, c, p=None):
        if p is None:
            return pl.ds(pl.multiple_of(c * self.half_rows, 16), self.half_rows)
        return pl.ds(pl.multiple_of(c * self.half_rows + p * self.piece_rows, 16), self.piece_rows)

    def block(self, rows):
        if self.wide:
            return self.array.at[rows, self.cols[0] * self.width : self.cols[1] * self.width]
        return self.array.at[:, rows]

    def slot(self, rows, d):
        if self.wide:
            return self.array.at[rows, d * self.width : (d + 1) * self.width]
        return self.array.at[d, rows]


def kernel(
    nn,
    tok_hbm,
    mask_ref,
    gid_ref,
    g1_ref,
    s1_ref,
    wq_hbm,
    wk_hbm,
    wv_hbm,
    wo_hbm,
    g2_ref,
    s2_ref,
    wu_hbm,
    wd_hbm,
    hw_ref,
    cot_hbm,
    readout_ref,
    gtok_ref,
    small_ref,
    fin_in_ref,
    wide_out_ref,
    wide_up_ref,
    wide_dn_ref,
    fin_out_ref,
    fin_up_ref,
    fin_dn_ref,
    mask_v,
    gid_v,
    g1_v,
    s1_v,
    g2_v,
    s2_v,
    hw_v,
    w_in,
    w_up,
    w_ot,
    w_dn,
    tok,
    cot,
    n1,
    qkv,
    pn,
    ctx,
    res,
    n2,
    act,
    gp,
    lay,
    emask,
    pmask,
    n1t,
    n2t,
    ctxt,
    vcol,
    mt,
    gexp,
    wcol,
    dcol,
    ab,
    zed,
    mixes,
    gbef,
    gl,
    datt,
    dctx,
    dqkv,
    g_up,
    g_dn,
    g_out,
    g_in,
    rc_up,
    rc_dn,
    rc_out,
    rc_in,
    rp_up,
    rp_dn,
    rp_out,
    rp_in,
    rz_up,
    rz_dn,
    rz_out,
    rz_in,
    mo_up,
    mo_dn,
    mo_out,
    mo_in,
    ar_one,
    ar_nodes,
    ar_tp,
    sv_one,
    sv_nodes,
    sv_tp,
    lsem,
    wsend,
    wrecv,
    gsend,
    grecv,
    asend,
    arecv,
    bsend,
    brecv,
):
    n, t = lax.axis_index("nodes"), lax.axis_index("tp")
    rows_here, width = tok.shape
    chunks = rows_here // CHUNK
    wides = rows_here // WIDE
    tiles = rows_here // TILE
    c = n % 2
    plane = (n // 2) % 4
    eighth = 4 * c + plane
    extra = [b for b in range(3, 12) if (1 << b) < nn]

    def node_peer(k):
        out = n
        for b in range(12):
            if (k >> b) & 1:
                bit = (n // (1 << b)) % 2
                out = out + (1 << b) * (1 - 2 * bit)
        return (out, t)

    def tp_peer(k):
        out = t
        for b in range(2):
            if (k >> b) & 1:
                bit = (t // (1 << b)) % 2
                out = out + (1 << b) * (1 - 2 * bit)
        return (n, out)

    def remote(src, dst, ssem, rsem, peer):
        return pltpu.make_async_remote_copy(
            src_ref=src, dst_ref=dst, send_sem=ssem, recv_sem=rsem, device_id=peer, device_id_type=MESH
        )

    qw = wq_hbm.shape[1]
    local = [
        pltpu.make_async_copy(wq_hbm, w_in.at[:, 0:qw], lsem.at[0]),
        pltpu.make_async_copy(wk_hbm, w_in.at[:, qw : 2 * qw], lsem.at[1]),
        pltpu.make_async_copy(wv_hbm, w_in.at[:, 2 * qw : 3 * qw], lsem.at[2]),
        pltpu.make_async_copy(tok_hbm, tok, lsem.at[3]),
        pltpu.make_async_copy(wo_hbm, w_ot.at[0], lsem.at[4]),
        pltpu.make_async_copy(wd_hbm, w_dn.at[0], lsem.at[5]),
        pltpu.make_async_copy(wu_hbm, w_up.at[:, 0 : wu_hbm.shape[1]], lsem.at[6]),
        pltpu.make_async_copy(cot_hbm, cot, lsem.at[7]),
    ]
    tiny = ((mask_ref, mask_v), (gid_ref, gid_v), (g1_ref, g1_v), (s1_ref, s1_v), (g2_ref, g2_v), (s2_ref, s2_v))
    for i, (src, dst) in enumerate(tiny + ((hw_ref, hw_v),)):
        local.append(pltpu.make_async_copy(src, dst, lsem.at[8 + i]))
    for copy in local:
        copy.start()

    barrier = pltpu.get_barrier_semaphore()
    greet = [node_peer(k) for k in range(1, 8)] + [node_peer(1 << b) for b in extra]
    greet += [tp_peer(k) for k in range(1, 4)]
    for peer in greet:
        pl.semaphore_signal(barrier, inc=1, device_id=peer, device_id_type=MESH)
    pl.semaphore_wait(barrier, len(greet))

    def plane_of(e):
        out = plane
        for b in range(2):
            if (e >> b) & 1:
                out = out + (1 << b) * (1 - 2 * ((plane // (1 << b)) % 2))
        return out

    def weight_block(ref, off, size, d0, d1):
        rows = pl.ds(pl.multiple_of(off, 16), size)
        if len(ref.shape) == 3:
            return ref.at[d0:d1, rows]
        w = ref.shape[1] // 4
        return ref.at[rows, d0 * w : d1 * w]

    class Fetch:
        def __init__(self, ref, slots, base, relay=False):
            total = ref.shape[1] if len(ref.shape) == 3 else ref.shape[0]
            d0, d1 = slots
            sems = iter(range(base, base + 8))

            def go(src, dst, peer):
                k = next(sems)
                return remote(src, dst, wsend.at[k], wrecv.at[k], peer)

            def rows(off, size):
                return weight_block(ref, off, size, d0, d1)

            part = total // 8
            own = eighth * part
            self.z = [
                go(weight_block(ref, own, part, 0, 1), weight_block(ref, own, part, d, d + 1), tp_peer(d))
                for d in range(d0, d1)
            ]
            self.more = []
            lots = [rows(c * (total // 2), total // 2)]
            if relay:
                self.plane = [go(rows(own, part), rows(own, part), node_peer(2 << e)) for e in range(2)]
                for e in range(2):
                    got = rows((4 * c + plane_of(1 << e)) * part + e * (part // 2), part // 2)
                    self.more.append(go(got, got, node_peer(4 >> e)))
            else:
                self.plane = [go(rows(own, part), rows(own, part), node_peer(2 * e)) for e in (1, 2, 3)]
            self.core = [go(x, x, node_peer(1)) for x in lots]

        def start_z(self):
            for cp in self.z:
                cp.start()

        def start_plane(self):
            for cp in self.z:
                cp.wait()
            for cp in self.plane:
                cp.start()

        def start_relay(self):
            for cp in self.plane:
                cp.wait()
            for cp in self.more:
                cp.start()

        def start_core(self):
            for cp in self.more or self.plane:
                cp.wait()
            for cp in self.core:
                cp.start()

        def end(self):
            for cp in self.core:
                cp.wait()

    fetch_in = [None] + [Fetch(w_in, (d, d + 1), 8 * (d - 1)) for d in (1, 2, 3)]
    fetch_ot = Fetch(w_ot, (1, 4), 24)
    fetch_up = Fetch(w_up, (1, 4), 32)
    fetch_dn = Fetch(w_dn, (1, 4), 40)

    for i in (0, 1, 2):
        local[i].wait()
    for d in (1, 2, 3):
        fetch_in[d].start_z()

    for i in range(8, 15):
        local[i].wait()
    gain1 = tokens_of(g1_v)
    shift1 = tokens_of(s1_v)
    gain2 = tokens_of(g2_v)
    shift2 = tokens_of(s2_v)
    hopw = tokens_of(hw_v)
    hop16 = jnp.broadcast_to(hopw, (16, width)).astype(BF16)

    eye = iota((TILE, TILE), 0) == iota((TILE, TILE), 1)
    ones = jnp.ones((TILE, TILE), BF16)
    lane8 = iota((HOPS, TILE), 1)
    block8 = lane8 // HOPS
    eye16 = eye.astype(F32).astype(BF16)
    emask[...] = (iota((TILE, TILE), 0) // HOPS == iota((TILE, TILE), 1) // HOPS).astype(F32).astype(BF16)
    first = (iota((2 * TILE, TILE), 0) < TILE) == (iota((2 * TILE, TILE), 1) < HEAD)
    pmask[...] = first.astype(F32).astype(BF16)
    nodes_chunk = CHUNK // HOPS
    spread_c = (iota((CHUNK, nodes_chunk), 0) // HOPS == iota((CHUNK, nodes_chunk), 1)).astype(F32).astype(BF16)

    def rows_of(i, size):
        return pl.ds(pl.multiple_of(i * size, size), size)

    mask_f = mask_v[...].astype(F32)
    for i in range(tiles):
        col = mm(jnp.where(eye, mask_f[i : i + 1, :], 0.0).astype(BF16), ones)
        vcol[i * TILE : (i + 1) * TILE, :] = col
        acc = jnp.zeros((HOPS, TILE), F32)
        col3 = col.reshape(TILE // HOPS, HOPS, TILE)
        for r in range(TILE // HOPS):
            acc = jnp.where(block8 == r, col3[r], acc)
        mt[i] = acc

    local[3].wait()

    def norm_one(i, carry):
        x = tok[rows_of(i, CHUNK), :].astype(F32)
        hat, _ = centred(x)
        n1[rows_of(i, CHUNK), :] = (hat * gain1 + shift1).astype(BF16)
        return carry

    lax.fori_loop(0, chunks, norm_one, 0)

    def project(d, lo, hi):
        base = d * 3 * qw

        def step(i, carry):
            r = rows_of(i, WIDE)
            out = mm(n1[r, :], w_in[:, base : base + 3 * qw])
            qkv[r, base : base + qw] = (out[:, 0:qw] * (HEAD**-0.5)).astype(BF16)
            qkv[r, base + qw : base + 3 * qw] = out[:, qw:].astype(BF16)
            return carry

        lax.fori_loop(lo, hi, step, 0)

    def pair(x):
        return jnp.concatenate([x, x], axis=0) * pmask[...]

    bits = [((lane8 // (HOPS << b)) % 2) == 1 for b in range(4)]

    def compact(x):
        out = []
        for h in range(2):
            x3 = x[:, h * TILE : (h + 1) * TILE].reshape(TILE // HOPS, HOPS, TILE)
            parts = [x3[r] for r in range(TILE // HOPS)]
            for b in range(4):
                parts = [jnp.where(bits[b], parts[2 * m + 1], parts[2 * m]) for m in range(len(parts) // 2)]
            out.append(parts[0])
        return out

    def expand(x):
        twice = jnp.concatenate([x, x], axis=0).astype(BF16)
        return jnp.concatenate([twice] * (TILE // 16), axis=0) * emask[...]

    together = 8

    steps = tiles // together
    mid = steps // 2

    def attend(d, lo, hi):
        base = d * 3 * qw

        def step(i, carry):
            at = [i * together + m for m in range(together)]
            rs = [rows_of(a, TILE) for a in at]
            q2 = [pair(qkv[r, base : base + qw]) for r in rs]
            scores = [compact(mm_rt(qkv[r, base + qw : base + 2 * qw], x)) for r, x in zip(rs, q2, strict=True)]
            wide = []
            for m, a in enumerate(at):
                keep = mt[a] > 0.5
                for h in range(2):
                    wide.append(jnp.where(keep, scores[m][h], NEGATIVE))
            peaks = [jnp.max(x, axis=0, keepdims=True) for x in wide]
            wide = [jnp.exp(x - y) for x, y in zip(wide, peaks, strict=True)]
            totals = [jnp.sum(x, axis=0, keepdims=True) for x in wide]
            wide = [x / y for x, y in zip(wide, totals, strict=True)]
            for m, a in enumerate(at):
                for h in range(2):
                    pn[a * 8 + 2 * d + h] = wide[2 * m + h]
            turned = [
                mm_rt(eye16, jnp.concatenate([expand(wide[2 * m]), expand(wide[2 * m + 1])], axis=0)).astype(BF16)
                for m in range(together)
            ]
            v2 = [pair(qkv[r, base + 2 * qw : base + 3 * qw]) for r in rs]
            for m, r in enumerate(rs):
                ctx[r, d * qw : (d + 1) * qw] = mm(turned[m], v2[m]).astype(BF16)
            return carry

        lax.fori_loop(lo, hi, step, 0)

    gcol = mm(jnp.where(eye, gid_v[...].astype(F32), 0.0).astype(BF16), ones).astype(BF16)
    for i in range(chunks):
        gexp[i * CHUNK : (i + 1) * CHUNK, :] = mm(spread_c, gcol[i * nodes_chunk : (i + 1) * nodes_chunk])
    fetch_in[1].start_plane()
    project(0, 0, wides // 2)
    fetch_in[2].start_plane()
    project(0, wides // 2, wides)
    fetch_in[3].start_plane()
    for i in (4, 5, 6, 7):
        local[i].wait()
    fetch_ot.start_z()
    fetch_up.start_z()
    fetch_dn.start_z()
    attend(0, 0, steps)
    fetch_ot.start_plane()
    fetch_in[1].start_core()
    fetch_up.start_plane()
    fetch_in[1].end()
    fetch_in[2].start_core()
    project(1, 0, wides)
    fetch_in[3].start_core()
    attend(1, 0, steps)
    fetch_dn.start_plane()
    fetch_in[2].end()
    project(2, 0, wides)
    fetch_ot.start_core()
    attend(2, 0, steps)
    fetch_in[3].end()
    project(3, 0, wides)
    attend(3, 0, steps)
    fetch_ot.end()

    def w_out():
        return w_ot[...].reshape(4 * qw, width)

    def w_down():
        return w_dn[...].reshape(4 * w_dn.shape[1], width)

    hop3 = iota((nodes_chunk, HOPS, TILE), 1)
    lane3 = iota((nodes_chunk, HOPS, TILE), 2)
    node3 = iota((nodes_chunk, HOPS, TILE), 0)
    lane_graph = (lane3 % GRAPHS).astype(F32)

    def feed_norm(i, carry):
        r = rows_of(i, WIDE)
        x = tok[r, :].astype(F32) + mm(ctx[r, :], w_out())
        res[r, :] = x
        hat, _ = centred(x)
        n2[r, :] = (hat * gain2 + shift2).astype(BF16)
        return carry

    uw = wu_hbm.shape[1]

    def feed_up(lo, hi):
        cols = slice(lo * uw, hi * uw)

        def step(i, carry):
            r = rows_of(i, WIDE)
            value, slope = gelu_both(mm(n2[r, :], w_up[:, cols]))
            act[r, cols] = value.astype(BF16)
            gp[r, cols] = slope.astype(BF16)
            return carry

        return step

    def feed_down(i, acc):
        r = rows_of(i, WIDE)
        lay[r, :] = res[r, :] + mm(act[r, :], w_down())
        for m in range(WIDE // CHUNK):
            acc = hops(i * (WIDE // CHUNK) + m, acc)
        return acc

    def hops(i, acc):
        r = rows_of(i, CHUNK)
        out = lay[r, :]
        dr = mm(spread_c, cot[rows_of(i, nodes_chunk), :])
        logit = jnp.sum(out * hopw, axis=-1, keepdims=True)
        gcoef = jnp.sum(out * dr, axis=-1, keepdims=True)
        shape = (nodes_chunk, HOPS, TILE)
        valid = vcol[r, :].reshape(shape)
        valid = jnp.where(hop3 > 0, valid, 0.0)
        logit = jnp.where(valid > 0.5, jnp.broadcast_to(logit, (CHUNK, TILE)).reshape(shape), NEGATIVE)
        e = jnp.exp(logit - jnp.max(logit, axis=1, keepdims=True))
        e = jnp.where(hop3 > 0, e, 0.0)
        weight = e / jnp.sum(e, axis=1, keepdims=True)
        direct = valid * jnp.broadcast_to(gcoef, (CHUNK, TILE)).reshape(shape)
        wcol[r, :] = weight.reshape(CHUNK, TILE)
        dcol[r, :] = direct.reshape(CHUNK, TILE)
        mine = gexp[r, :].reshape(shape) == lane_graph
        both = jnp.where(lane3 < GRAPHS, jnp.where(hop3 == 0, 1.0, weight), -direct)
        return acc + jnp.sum(jnp.where(mine, both, 0.0), axis=0)

    lax.fori_loop(0, wides, feed_norm, 0, unroll=True)
    fetch_up.start_core()
    lax.fori_loop(0, wides, feed_up(0, 1), 0)
    fetch_up.end()
    lax.fori_loop(0, wides // 2, feed_up(1, 4), 0)
    fetch_dn.start_core()
    lax.fori_loop(wides // 2, wides, feed_up(1, 4), 0)
    fetch_dn.end()
    sums = lax.fori_loop(0, wides, feed_down, jnp.zeros((HOPS, TILE), F32), unroll=True)

    def reduce_all(value, one, by_nodes, by_tp, ssem, rsem, overlap=None):
        one[0] = value
        copies = [
            remote(one.at[0], by_nodes.at[k - 1], ssem.at[k - 1], rsem.at[k - 1], node_peer(k)) for k in range(1, 8)
        ]
        for cp in copies:
            cp.start()
        if overlap is not None:
            overlap()
        for cp in copies:
            cp.wait()
        value = one[0]
        for k in range(7):
            value = value + by_nodes[k]
        at = 7
        for b in extra:
            one[at - 6] = value
            cp = remote(one.at[at - 6], by_nodes.at[at], ssem.at[at], rsem.at[at], node_peer(1 << b))
            cp.start()
            cp.wait()
            value = value + by_nodes[at]
            at += 1
        last = one.shape[0] - 1
        one[last] = value
        copies = [
            remote(one.at[last], by_tp.at[k - 1], ssem.at[at + k - 1], rsem.at[at + k - 1], tp_peer(k))
            for k in range(1, 4)
        ]
        for cp in copies:
            cp.start()
        return copies, lambda: one[last] + by_tp[0] + by_tp[1] + by_tp[2]

    def small_products():
        drdown = mm_rt(cot[...], w_down()).astype(BF16)
        hopdown = mm_rt(hop16, w_down()).astype(BF16)
        for i in range(chunks):
            piece = drdown[i * nodes_chunk : (i + 1) * nodes_chunk]
            ab[i, 0:nodes_chunk] = piece
            ab[i, nodes_chunk : 2 * nodes_chunk] = piece
            ab[i, 2 * nodes_chunk : 2 * nodes_chunk + 16] = hopdown
            ab[i, 2 * nodes_chunk + 16 :] = jnp.zeros((TILE - 2 * nodes_chunk - 16, ab.shape[2]), BF16)
        for i in range(chunks):
            at = slice(i * CHUNK, (i + 1) * CHUNK)
            for src, dst in ((n2, n2t), (ctx, ctxt), (n1, n1t)):
                dst[:, at] = src[at, :].T

    copies, total = reduce_all(sums, ar_one, ar_nodes, ar_tp, asend, arecv, small_products)
    for cp in copies:
        cp.wait()
    sums = total()
    row = jnp.broadcast_to(sums[0:1, :], (HOPS, TILE))
    counts = jnp.where(lane8 < GRAPHS, row, pltpu.roll(row, GRAPHS, 1))
    means = (sums / (counts + 1.0))[None]

    def back_one(i, carry):
        zed_acc = carry
        r = rows_of(i, CHUNK)
        shape = (nodes_chunk, HOPS, TILE)
        picked = jnp.where(gexp[r, :].reshape(shape) == lane_graph, means, 0.0)
        mean_r = jnp.sum(jnp.where(lane3 < GRAPHS, picked, 0.0), axis=-1, keepdims=True)
        grad_mean = jnp.sum(jnp.where(lane3 < GRAPHS, 0.0, picked), axis=-1, keepdims=True)
        weight = wcol[r, :].reshape(shape)
        valid = vcol[r, :].reshape(shape)
        coef = jnp.where(hop3 > 0, valid * (weight - mean_r), 1.0)
        grad_w = dcol[r, :].reshape(shape) + grad_mean
        glog = weight * (grad_w - jnp.sum(weight * grad_w, axis=1, keepdims=True))
        coef_hi = coef.astype(BF16).astype(F32)
        glog_hi = glog.astype(BF16).astype(F32)
        zero = jnp.zeros_like(coef)
        mix = jnp.where(lane3 == node3, coef_hi, zero)
        mix = jnp.where(lane3 == node3 + nodes_chunk, coef - coef_hi, mix)
        mix = jnp.where(lane3 == 2 * nodes_chunk, glog_hi, mix)
        mix = jnp.where(lane3 == 2 * nodes_chunk + 1, glog - glog_hi, mix)
        mix = mix.reshape(CHUNK, TILE).astype(BF16)

        mixes[r, :] = mix
        gbef[r, :] = (mm(mix, ab[i]) * gp[r, :].astype(F32)).astype(BF16)

        fold = mm_lt(mix, act[r, :])
        zed[rows_of(i, nodes_chunk), :] = (fold[0:nodes_chunk] + fold[nodes_chunk : 2 * nodes_chunk]).astype(BF16)
        zed_acc = zed_acc + fold[2 * nodes_chunk : 2 * nodes_chunk + 8]

        return zed_acc

    def back_norm(i, carry):
        gain_acc, shift_acc = carry
        r = rows_of(i, WIDE)
        layer_grads(i)
        dy = mm_rt(gbef[r, :], w_up[...])
        hat, inv = centred(res[r, :])
        gain_acc = gain_acc + jnp.sum((dy * hat).reshape(WIDE // HOPS, HOPS, width), axis=0)
        shift_acc = shift_acc + jnp.sum(dy.reshape(WIDE // HOPS, HOPS, width), axis=0)
        g = dy * gain2
        back = inv * (
            g - jnp.mean(g, axis=-1, keepdims=True) - hat * jnp.mean(g * hat, axis=-1, keepdims=True)
        )
        grad_res = gl[r, :] + back
        gl[r, :] = grad_res
        att = grad_res.astype(BF16)
        datt[r, :] = att
        dctx[r, :] = mm_rt(att, w_out()).astype(BF16)
        return gain_acc, shift_acc

    def layer_grads(wide):
        for m in range(WIDE // CHUNK):
            i = wide * (WIDE // CHUNK) + m
            r = rows_of(i, CHUNK)
            mix = mixes[r, :]
            dr = cot[rows_of(i, nodes_chunk), :]
            rest = jnp.zeros((TILE - 2 * nodes_chunk - 16, width), BF16)
            gl[r, :] = mm(mix, jnp.concatenate([dr, dr, hop16, rest], axis=0))

    def readouts(i, hop_acc):
        r = rows_of(i, CHUNK)
        seen = mm_lt(mixes[r, :], lay[r, :].astype(BF16))
        both = seen[0:nodes_chunk] + seen[nodes_chunk : 2 * nodes_chunk]
        readout_ref[rows_of(i, nodes_chunk), :] = both.astype(BF16)
        return hop_acc + seen[2 * nodes_chunk : 2 * nodes_chunk + 8]

    zero8 = jnp.zeros((HOPS, width), F32)
    zed_sum = lax.fori_loop(0, chunks, back_one, jnp.zeros((HOPS, zed.shape[1]), F32), unroll=True)

    def group(at, array, wide, cols, rc, rp, rz, final, more):
        return Group(array, wide, cols, rc, rp, rz, final, more, gsend, grecv, at * (15 + len(extra)))

    dn = group(0, g_dn, False, (0, 4), rc_dn, rp_dn, rz_dn, fin_dn_ref, mo_dn)
    up = group(1, g_up, True, (0, 4), rc_up, rp_up, rz_up, fin_up_ref, mo_up)
    ot = group(2, g_out, False, (0, 4), rc_out, rp_out, rz_out, fin_out_ref, mo_out)
    qk = [
        group(3 + d, g_in, True, (d, d + 1), rc_in.at[d], rp_in.at[d], rz_in, fin_in_ref, mo_in) for d in range(4)
    ]
    every = (1, 2, 3)

    def core_copy(g):
        s, r = g.sems(0)
        return remote(g.block(g.rows(1 - c)), g.recv_core, s, r, node_peer(1))

    def go_core(g):
        core_copy(g).start()

    def add_core(g):
        core_copy(g).wait()
        mine = g.block(g.rows(c))
        mine[...] = mine[...] + g.recv_core[...]

    def plane_copies(g):
        return [
            remote(g.block(g.rows(c, plane_of(e))), g.recv_plane.at[e - 1], *g.sems(e), node_peer(2 * e))
            for e in (1, 2, 3)
        ]

    def go_plane(g):
        add_core(g)
        for cp in plane_copies(g):
            cp.start()

    def cut(g, p, e):
        if g.wide:
            w = g.piece_rows // 2
            rows = pl.ds(pl.multiple_of(c * g.half_rows + p * g.piece_rows + e * w, 16), w)
            return g.array.at[rows, g.cols[0] * g.width : g.cols[1] * g.width]
        w = g.width // 2
        return g.array.at[:, g.rows(c, p), e * w : (e + 1) * w]

    def landing(g, m, e):
        if g.wide:
            w = g.piece_rows // 2
            return g.recv_plane.at[m, e * w : (e + 1) * w]
        w = g.width // 2
        return g.recv_plane.at[m, :, :, e * w : (e + 1) * w]

    def fold_copies(g):
        out = []
        for e in range(2):
            for m, far in enumerate((plane_of(1 << e), plane_of(3))):
                sems = g.sems(11 + 2 * e + m)
                out.append(remote(cut(g, far, e), landing(g, m, e), *sems, node_peer(2 << e)))
        return out

    def go_fold(g):
        add_core(g)
        for cp in fold_copies(g):
            cp.start()

    def fold_last(g):
        return [
            remote(cut(g, plane_of(2 >> e), e), landing(g, 2, e), *g.sems(1 + e), node_peer(4 >> e)) for e in range(2)
        ]

    def go_fold_last(g):
        for cp in fold_copies(g):
            cp.wait()
        for e in range(2):
            for m, keep in enumerate((plane, plane_of(2 >> e))):
                mine = cut(g, keep, e)
                mine[...] = mine[...] + landing(g, m, e)[...]
        for cp in fold_last(g):
            cp.start()

    def go_z_fold(g, slots):
        for cp in fold_last(g):
            cp.wait()
        mine = g.block(g.rows(c, plane))
        mine[...] = mine[...] + g.recv_plane[2]
        for cp in z_copies(g, slots):
            cp.start()

    def z_copies(g, slots):
        return [
            remote(g.slot(g.rows(c, plane), d), g.recv_z.at[d - 1], *g.sems(3 + d), tp_peer(d)) for d in slots
        ]

    def go_z(g, slots):
        for cp in plane_copies(g):
            cp.wait()
        mine = g.block(g.rows(c, plane))
        total = mine[...].astype(F32)
        for e in range(3):
            total = total + g.recv_plane[e].astype(F32)
        mine[...] = total.astype(BF16)
        for cp in z_copies(g, slots):
            cp.start()

    def z_first(g):
        return [remote(g.slot(g.rows(c), d), g.recv_z.at[d - 1], *g.sems(3 + d), tp_peer(d)) for d in every]

    def go_z_first(g):
        add_core(g)
        for cp in z_first(g):
            cp.start()

    def own_pieces(g):
        return [
            remote(g.slot(g.rows(c, plane_of(e)), 0), g.recv_plane.at[e - 1], *g.sems(e), node_peer(2 * e))
            for e in (1, 2, 3)
        ]

    def go_own_plane(g):
        for cp in z_first(g):
            cp.wait()
        mine = g.slot(g.rows(c), 0)
        total = mine[...].astype(F32)
        for d in range(3):
            total = total + g.recv_z[d].astype(F32)
        mine[...] = total.astype(BF16)
        for cp in own_pieces(g):
            cp.start()

    def go_own_final(g):
        for cp in own_pieces(g):
            cp.wait()
        total = g.slot(g.rows(c, plane), 0)[...].astype(F32)
        for e in range(3):
            total = total + g.recv_plane[e].astype(F32)
        share(g, total)

    def final_copies(g):
        mine = g.final.at[g.rows(c, plane)]
        return [remote(mine, mine, *g.sems(6 + e), node_peer(2 * e)) for e in (1, 2, 3)]

    def last_copy(g):
        mine = g.final.at[g.rows(c)]
        return remote(mine, mine, *g.sems(10), node_peer(1))

    def go_final(g, waits):
        for cp in waits:
            cp.wait()
        total = g.slot(g.rows(c, plane), 0)[...].astype(F32)
        for d in range(3):
            total = total + g.recv_z[d].astype(F32)
        share(g, total)

    def share(g, total):
        for j, b in enumerate(extra):
            g.more[2 * j] = total.astype(BF16)
            cp = remote(g.more.at[2 * j], g.more.at[2 * j + 1], *g.sems(15 + j), node_peer(1 << b))
            cp.start()
            cp.wait()
            total = total + g.more[2 * j + 1].astype(F32)
        g.final.at[g.rows(c, plane)][...] = total.astype(BF16)
        for cp in final_copies(g):
            cp.start()

    def go_last(g):
        for cp in final_copies(g):
            cp.wait()
        last_copy(g).start()

    def finish(g):
        last_copy(g).wait()

    zed[rows_here // HOPS :, :] = jnp.concatenate([zed_sum, jnp.zeros_like(zed_sum)], axis=0).astype(BF16)
    drh = jnp.concatenate([cot[...], hop16], axis=0)
    g_dn[...] = mm_lt(zed[...], drh).astype(BF16).reshape(g_dn.shape)
    go_core(dn)
    g_up[...] = mm(n2t[...], gbef[...]).astype(BF16)
    go_core(up)
    norm_sums = lax.fori_loop(0, wides // 2, back_norm, (zero8, zero8))
    go_z_first(dn)
    go_fold(up)
    gain_two, shift_two = lax.fori_loop(wides // 2, wides, back_norm, norm_sums)
    g_out[...] = mm(ctxt[...], datt[...]).astype(BF16).reshape(g_out.shape)
    go_core(ot)

    def attend_back(d):
        base = d * 3 * qw

        def step(i, carry):
            at = [i * together + m for m in range(together)]
            rs = [rows_of(a, TILE) for a in at]
            do2 = [pair(dctx[r, d * qw : (d + 1) * qw]) for r in rs]
            grads = [
                compact(mm_rt(qkv[r, base + 2 * qw : base + 3 * qw], x)) for r, x in zip(rs, do2, strict=True)
            ]
            probs = [[pn[a * 8 + 2 * d + h] for h in range(2)] for a in at]
            probs_wide = [jnp.concatenate([expand(p) for p in ps], axis=1) for ps in probs]
            for m, r in enumerate(rs):
                dqkv[r, base + 2 * qw : base + 3 * qw] = mm(probs_wide[m], do2[m]).astype(BF16)
            inner = [[jnp.sum(p * g, axis=0, keepdims=True) for p, g in zip(*x, strict=True)] for x in zip(probs, grads, strict=True)]
            back = [
                [expand(probs[m][h] * (grads[m][h] - inner[m][h])) for h in range(2)] for m in range(together)
            ]
            q2 = [pair(qkv[r, base : base + qw]) for r in rs]
            for m, r in enumerate(rs):
                wide = jnp.concatenate(back[m], axis=1)
                dqkv[r, base + qw : base + 2 * qw] = mm(wide, q2[m]).astype(BF16)
            turned = [mm_rt(eye16, jnp.concatenate(x, axis=0)).astype(BF16) for x in back]
            k2 = [pair(qkv[r, base + qw : base + 2 * qw]) for r in rs]
            for m, r in enumerate(rs):
                dqkv[r, base : base + qw] = (mm(turned[m], k2[m]) * (HEAD**-0.5)).astype(BF16)
            return carry

        lax.fori_loop(0, tiles // together, step, 0)
        g_in[:, base : base + 3 * qw] = mm(n1t[...], dqkv[:, base : base + 3 * qw]).astype(BF16)
        go_core(qk[d])

    def back_two(i, carry):
        gain_acc, shift_acc = carry
        r = rows_of(i, WIDE)
        dy = mm_rt(dqkv[r, :], w_in[...])
        hat, inv = centred(tok[r, :].astype(F32))
        gain_acc = gain_acc + jnp.sum((dy * hat).reshape(WIDE // HOPS, HOPS, width), axis=0)
        shift_acc = shift_acc + jnp.sum(dy.reshape(WIDE // HOPS, HOPS, width), axis=0)
        g = dy * gain1
        back = inv * (
            g - jnp.mean(g, axis=-1, keepdims=True) - hat * jnp.mean(g * hat, axis=-1, keepdims=True)
        )
        gtok_ref[r, :] = (gl[r, :] + back).astype(BF16)
        return gain_acc, shift_acc

    attend_back(3)
    go_fold(ot)
    attend_back(2)
    go_fold(qk[3])
    go_fold_last(up)
    attend_back(1)
    go_fold(qk[2])
    go_fold_last(ot)
    attend_back(0)
    go_plane(qk[1])
    go_z_fold(up, every)
    go_fold_last(qk[3])
    hop_sum = lax.fori_loop(0, chunks, readouts, zero8)
    norm_sums = lax.fori_loop(0, wides // 2, back_two, (zero8, zero8))
    go_plane(qk[0])
    go_z_fold(ot, every)
    go_fold_last(qk[2])
    go_own_plane(dn)
    go_z_fold(qk[3], (3,))
    gain_one, shift_one = lax.fori_loop(wides // 2, wides, back_two, norm_sums)
    go_z(qk[1], (1,))
    go_z_fold(qk[2], (2,))

    def fold8(x):
        return jnp.sum(x, axis=0, keepdims=True)

    small = jnp.concatenate(
        [fold8(gain_one), fold8(shift_one), fold8(gain_two), fold8(shift_two), fold8(hop_sum[0:2]), zero8[0:3]], axis=0
    )

    def rest_of():
        go_final(up, z_copies(up, every))
        go_final(ot, z_copies(ot, every))
        go_own_final(dn)
        go_z(qk[0], ())
        go_final(qk[0], [z_copies(qk[d], (d,))[0] for d in every])

    copies, total_small = reduce_all(small, sv_one, sv_nodes, sv_tp, bsend, brecv, rest_of)
    go_last(up)
    go_last(dn)
    go_last(ot)
    go_last(qk[0])
    for g, wide in ((dn, wide_dn_ref), (up, wide_up_ref), (ot, wide_out_ref)):
        finish(g)
        wide[...] = g.final[...].astype(F32)
    for cp in copies:
        cp.wait()
    small_ref[...] = total_small()
    finish(qk[0])


def results_kernel(readout, gtok, small, fin_in, fin_out, fin_up, fin_dn, *rest):
    o_read, o_tok, o_g1, o_s1, o_q, o_k, o_v, o_out, o_g2, o_s2, o_up, o_dn, o_hop = rest[:13]
    v_q, v_k, v_v, *lines, sems = rest[13:]
    moves = []

    def send(src, dst):
        moves.append(pltpu.make_async_copy(src, dst, sems.at[len(moves)]))
        moves[-1].start()

    send(gtok, o_tok)
    send(readout, o_read)
    send(fin_up, o_up)
    send(fin_dn, o_dn)
    send(fin_out, o_out)
    qw = o_q.shape[1]
    for i, (x, o) in enumerate(((v_q, o_q), (v_k, o_k), (v_v, o_v))):
        x[...] = fin_in[:, i * qw : (i + 1) * qw].astype(F32)
        send(x, o)
    width = small.shape[1]
    for i, (x, o) in enumerate(zip(lines, (o_g1, o_s1, o_g2, o_s2, o_hop), strict=True)):
        x[...] = small[i : i + 1, :].reshape(width)
        send(x, o)
    for cp in moves:
        cp.wait()


def shards(
    nn,
    tokens,
    hop_mask,
    graph_ids,
    norm1_gain,
    norm1_shift,
    w_query,
    w_key,
    w_value,
    w_out,
    norm2_gain,
    norm2_shift,
    w_up,
    w_down,
    hop_weight,
    cotangent,
):
    rows, width = tokens.shape
    nodes = rows // HOPS
    qw, uw = w_query.shape[1], w_up.shape[1]
    vm = pl.BlockSpec(memory_space=pltpu.VMEM)
    hbm = pl.BlockSpec(memory_space=pl.ANY)
    extra = len([b for b in range(3, 12) if (1 << b) < nn])

    def v(*shape, dtype=BF16):
        return pltpu.VMEM(shape, dtype)

    tiles, chunks = rows // TILE, rows // CHUNK
    half = width // 2
    more = max(2 * extra, 1)
    scratch = [
        v(qw, width),
        v(width, uw),
        v(uw, width),
        v(tiles, TILE, dtype=jnp.int32),
        v(1, nodes, dtype=jnp.int32),
        v(width),
        v(width),
        v(width),
        v(width),
        v(width),
        v(width, 12 * qw),
        v(width, 4 * uw),
        v(4, qw, width),
        v(4, uw, width),
        v(rows, width),
        v(nodes, width),
        v(rows, width),
        v(rows, 12 * qw),
        v(tiles * 8, HOPS, TILE, dtype=F32),
        v(rows, width),
        v(rows, width, dtype=F32),
        v(rows, width),
        v(rows, 4 * uw),
        v(rows, 4 * uw),
        v(rows, width, dtype=F32),
        v(TILE, TILE),
        v(2 * TILE, TILE),
        v(width, rows),
        v(width, rows),
        v(width, rows),
        v(rows, TILE, dtype=F32),
        v(tiles, HOPS, TILE, dtype=F32),
        v(rows, TILE, dtype=F32),
        v(rows, TILE, dtype=F32),
        v(rows, TILE, dtype=F32),
        v(chunks, TILE, 4 * uw),
        v(nodes + 16, 4 * uw),
        v(rows, TILE),
        v(rows, 4 * uw),
        v(rows, width, dtype=F32),
        v(rows, width),
        v(rows, width),
        v(rows, 12 * qw),
        v(width, 4 * uw),
        v(4, uw, width),
        v(4, qw, width),
        v(width, 12 * qw),
        v(half, 4 * uw),
        v(4, uw // 2, width),
        v(4, qw // 2, width),
        v(4, half, 3 * qw),
        v(3, half // 4, 4 * uw),
        v(3, uw // 8, width),
        v(3, 4, qw // 8, width),
        v(4, 3, half // 4, 3 * qw),
        v(3, half // 4, uw),
        v(3, uw // 2, width),
        v(3, qw // 8, width),
        v(3, half // 4, 3 * qw),
        v(more, half // 4, uw),
        v(more, uw // 8, width),
        v(more, qw // 8, width),
        v(more, half // 4, 3 * qw),
        v(2 + extra, HOPS, TILE, dtype=F32),
        v(7 + extra, HOPS, TILE, dtype=F32),
        v(3, HOPS, TILE, dtype=F32),
        v(2 + extra, 8, width, dtype=F32),
        v(7 + extra, 8, width, dtype=F32),
        v(3, 8, width, dtype=F32),
        pltpu.SemaphoreType.DMA((15,)),
        pltpu.SemaphoreType.DMA((48,)),
        pltpu.SemaphoreType.DMA((48,)),
        pltpu.SemaphoreType.DMA((7 * (15 + extra),)),
        pltpu.SemaphoreType.DMA((7 * (15 + extra),)),
        pltpu.SemaphoreType.DMA((10 + extra,)),
        pltpu.SemaphoreType.DMA((10 + extra,)),
        pltpu.SemaphoreType.DMA((10 + extra,)),
        pltpu.SemaphoreType.DMA((10 + extra,)),
    ]
    outs = [
        pltpu.VMEM((nodes, width), BF16),
        pltpu.VMEM((rows, width), BF16),
        pltpu.VMEM((8, width), F32),
        pltpu.VMEM((width, 3 * qw), BF16),
        pltpu.VMEM((qw, width), F32),
        pltpu.VMEM((width, uw), F32),
        pltpu.VMEM((uw, width), F32),
    ]
    readout, gtok, small, fin_in, fin_out, fin_up, fin_dn = pl.pallas_call(
        functools.partial(kernel, nn),
        out_shape=outs,
        in_specs=[hbm] * 15,
        out_specs=[vm] * 7,
        scratch_shapes=scratch,
        compiler_params=pltpu.CompilerParams(
            collective_id=0, has_side_effects=True, vmem_limit_bytes=54 * 1024 * 1024
        ),
        name="layer",
    )(
        tokens,
        hop_mask.reshape(tiles, TILE),
        graph_ids.reshape(1, nodes),
        norm1_gain,
        norm1_shift,
        w_query,
        w_key,
        w_value,
        w_out,
        norm2_gain,
        norm2_shift,
        w_up,
        w_down,
        hop_weight,
        cotangent,
    )
    line = jax.ShapeDtypeStruct((width,), F32)
    square = jax.ShapeDtypeStruct((width, qw), F32)
    return pl.pallas_call(
        results_kernel,
        out_shape=[
            jax.ShapeDtypeStruct((nodes, width), BF16),
            jax.ShapeDtypeStruct((rows, width), BF16),
            line,
            line,
            square,
            square,
            square,
            jax.ShapeDtypeStruct((qw, width), F32),
            line,
            line,
            jax.ShapeDtypeStruct((width, uw), F32),
            jax.ShapeDtypeStruct((uw, width), F32),
            line,
        ],
        in_specs=[vm] * 7,
        out_specs=[hbm] * 13,
        scratch_shapes=[v(width, qw, dtype=F32)] * 3 + [v(width, dtype=F32)] * 5 + [pltpu.SemaphoreType.DMA((13,))],
        compiler_params=pltpu.CompilerParams(vmem_limit_bytes=16 * 1024 * 1024),
        name="results",
    )(readout, gtok, small, fin_in, fin_out, fin_up, fin_dn)


def solution(mesh):
    spread = P(("nodes", "tp"), None)
    flat = P(("nodes", "tp"))
    cols, rows = P(None, "tp"), P("tp", None)
    return jax.shard_map(
        functools.partial(shards, mesh.shape["nodes"]),
        mesh=mesh,
        in_specs=(spread, flat, flat, P(), P(), cols, cols, cols, rows, P(), P(), cols, rows, P(), spread),
        out_specs=(spread, spread, P(), P(), cols, cols, cols, rows, P(), P(), cols, rows, P()),
        check_vma=False,
    )
```
